256 devices in a mesh: gx: 32 (over z_hi, x, y), gy: 8 (over z_lo, core).
Axes of the slice: x: 4, y: 4, z: 8 (z_hi: 2, z_lo: 4; z = z_hi * 4 + z_lo), core: 2. Of those that a mesh axis runs over, the one named last changes fastest.
Arguments:
- offsets: float32 [32, 8, 3, 8192], P('gx', 'gy'), may hold values from -0.5 to 0.5
- line: float32 [32, 8, 3, 8192], P('gx', 'gy'), may hold values from -6 to 6
- burgers_kind: int32 [32, 8, 8192], P('gx', 'gy'), may hold values from 0 to 7
- seg_cell: int32 [32, 8, 8192], P('gx', 'gy'), may hold values from 0 to 63
- end_node: int32 [32, 8, 2, 8192], P('gx', 'gy'), may hold values from 0 to 8191
- end_owner: int32 [32, 8, 2, 8192], P('gx', 'gy'), may hold values from 0 to 4
- drag: float32 [32, 8, 8192], P('gx', 'gy'), may hold values from 0.5 to 4
- applied: float32 [6], replicated, may hold values from -4 to 4
- pair_list: int32 [32, 8, 2, 1024], P('gx', 'gy'), may hold values from 0 to 191, as said below
- ghost_x_list: int32 [32, 8, 2, 32], P('gx', 'gy'), may hold values from 0 to 63
- ghost_y_list: int32 [32, 8, 2, 32], P('gx', 'gy'), may hold values from 0 to 127
Outputs:
- velocity: float32 [32, 8, 3, 8192], P('gx', 'gy')
The draws below stay inside these ranges and needn't reach their ends.
Inputs may be any that keep to these rules, and one draw needn't show every extreme that they name: `pair_list`: per domain the real pairs (target below 64) come first and the remaining slots are padding with target 64 and source 0; the number of real pairs is a multiple of 256, at least 512, and at least one domain has 1024.
All inputs are finite; a program needn't handle non-finite values.
Results may differ from the reference program's by a relative error of at most 0.0003.
Values sent between devices are 32-bit elements; how exact they have to be, the bound alone decides.
A program may use at most 128 MiB of HBM per device.

```python
import math
import jax
import jax.numpy as jnp
from jax import lax

SEG = 128
NB_DEV = 64
CCX = 1
CCY = 4
NCZ = 16
GX = 32
GY = 32
GHOSTS = 192
PAIRS = 1024
SEGS = 8192
NODES = 8192
CELLS = 64
N_GX = 32
N_GY = 8


def draw_pair_list(key, part):
    key = jax.random.fold_in(key, 11)
    keys = jax.random.split(key, 4)
    domains = N_GX * N_GY
    level = jax.random.randint(keys[0], (domains,), 0, 10)
    factor = jnp.where(level < 7, 2, jnp.where(level < 9, 3, 4))
    chosen = jax.random.randint(keys[1], (), 0, domains)
    factor = jnp.where(jnp.arange(domains) == chosen, 4, factor)
    real = (factor * (PAIRS // 4)).reshape(N_GX, N_GY, 1)
    targets = jax.random.randint(keys[2], (N_GX, N_GY, PAIRS), 0, NB_DEV)
    sources = jax.random.randint(keys[3], (N_GX, N_GY, PAIRS), 0, GHOSTS)
    slot = jnp.arange(PAIRS).reshape(1, 1, PAIRS)
    used = slot < real
    targets = jnp.where(used, targets, NB_DEV)
    sources = jnp.where(used, sources, 0)
    return jnp.stack([targets, sources], axis=2).astype(jnp.int32)


def set_ends(drawn, key, least, top_value):
    dims = drawn.shape
    index_at = [jax.random.randint(jax.random.fold_in(key, axis), (), 0, dims[axis]) for axis in range(len(dims))]
    drawn = drawn.at[tuple(index_at)].set(least)
    longest = dims.index(max(dims))
    index_at[longest] = (index_at[longest] + 1) % dims[longest]
    return drawn.at[tuple(index_at)].set(top_value)


def level_of(key, shape, cuts, smallest, largest):
    level, own = 1.0, jax.random.fold_in(key, 6)
    for dim, shards_of in cuts:
        draws = jnp.exp(jax.random.uniform(jax.random.fold_in(own, dim), (shards_of,), jnp.float32, smallest / len(cuts), largest / len(cuts)))
        level = level * jnp.repeat(draws, shape[dim] // shards_of).reshape([-1 if axis == dim else 1 for axis in range(len(shape))])
    return level


def centred(key, shape, width, reach, cuts=(), held_as=jnp.bfloat16):
    gain = level_of(key, shape, cuts, -0.22, 0.18) if cuts else 1.0
    entries = jax.random.normal(key, shape, jnp.float32) * width * gain
    return jnp.minimum(jnp.maximum(entries, -reach), reach).astype(held_as)


def setup_inputs(seed: int = 0) -> dict:
    key_of = jax.random.split(jax.random.key(seed), 12)
    return {
        "offsets": jnp.clip(jax.random.uniform(key_of[0], (N_GX, N_GY, 3, SEGS), jnp.float32, -0.5, 0.5) * level_of(key_of[0], (N_GX, N_GY, 3, SEGS), ((0, 32), (1, 8)), -0.4, 0.0), -0.5, 0.5),
        "line": centred(key_of[1], (N_GX, N_GY, 3, SEGS), 1.0, 6.0, ((0, 32), (1, 8)), jnp.float32),
        "burgers_kind": set_ends(jax.random.randint(key_of[2], (N_GX, N_GY, SEGS), 0, 8), jax.random.fold_in(key_of[2], 1), 0, 7).astype(jnp.int32),
        "seg_cell": set_ends(jax.random.randint(key_of[3], (N_GX, N_GY, SEGS), 0, CELLS), jax.random.fold_in(key_of[3], 1), 0, CELLS - 1).astype(jnp.int32),
        "end_node": set_ends(jax.random.randint(key_of[4], (N_GX, N_GY, 2, SEGS), 0, NODES), jax.random.fold_in(key_of[4], 1), 0, NODES - 1).astype(jnp.int32),
        "end_owner": set_ends(jax.random.randint(key_of[5], (N_GX, N_GY, 2, SEGS), 0, 5), jax.random.fold_in(key_of[5], 1), 0, 4).astype(jnp.int32),
        "drag": jnp.clip(jnp.exp(math.log(4.0) - 2.0794415 * jax.random.uniform(key_of[6], (N_GX, N_GY, NODES), jnp.float32) ** level_of(key_of[6], (N_GX, N_GY, NODES), ((0, 32), (1, 8)), -0.2, 0.2)), 0.5, 4.0),
        "applied": centred(key_of[7], (6,), 1.0, 4.0, (), jnp.float32),
        "pair_list": draw_pair_list(jax.random.fold_in(key_of[11], 71), 0),
        "ghost_x_list": set_ends(jax.random.randint(key_of[9], (N_GX, N_GY, 2, GX), 0, NB_DEV), jax.random.fold_in(key_of[9], 1), 0, NB_DEV - 1).astype(jnp.int32),
        "ghost_y_list": set_ends(jax.random.randint(key_of[10], (N_GX, N_GY, 2, GY), 0, NB_DEV + 2 * GX), jax.random.fold_in(key_of[10], 1), 0, (NB_DEV + 2 * GX) - 1).astype(jnp.int32),
    }


CORE_SQUARE = 0.25
SHEAR_TERM = 1.0 / (8.0 * math.pi)
BULK_TERM = 1.0 / (4.0 * math.pi * 0.7)
CORE_LENGTH = 1.0
COMPONENTS = ((0, 0), (1, 1), (2, 2), (0, 1), (0, 2), (1, 2))
pair_group = 8
far_group = 16

def point_stress(rx, ry, rz, moment):
    ra_square = rx * rx + ry * ry + rz * rz + CORE_SQUARE
    inv_one = 1.0 / jnp.sqrt(ra_square)
    inv_three = inv_one * inv_one * inv_one
    inv_five = inv_three * inv_one * inv_one
    slope = -(2.0 * inv_three + 3.0 * CORE_SQUARE * inv_five)
    dist = (rx, ry, rz)
    grad = (slope * rx, slope * ry, slope * rz)
    amat = [[moment[3 * first + second] for second in range(3)] for first in range(3)]
    curl = (amat[1][2] - amat[2][1], amat[2][0] - amat[0][2], amat[0][1] - amat[1][0])
    crossed = [[grad[(row + 1) % 3] * amat[(row + 2) % 3][col] - grad[(row + 2) % 3] * amat[(row + 1) % 3][col] for col in range(3)] for row in range(3)]
    curl_dist = curl[0] * rx + curl[1] * ry + curl[2] * rz
    curl_grad = curl[0] * grad[0] + curl[1] * grad[1] + curl[2] * grad[2]
    result = []
    for row, col in COMPONENTS:
        first_term = crossed[row][col] + crossed[col][row]
        second_term = -(curl[row] * dist[col] + curl[col] * dist[row]) * inv_three + 3.0 * curl_dist * dist[row] * dist[col] * inv_five
        if row == col:
            second_term = second_term - curl_dist * inv_three - curl_grad
        result.append(-SHEAR_TERM * first_term - BULK_TERM * second_term)
    return result

def local_rows(cell):
    return (cell // (CCY * NCZ), cell // NCZ % CCY, cell % NCZ)

def segment_data(offsets, line, kind, cell):
    position = jnp.stack(local_rows(cell), 0).astype(jnp.float32) + 0.5 + offsets
    burgers = jnp.stack([1.0 - 2.0 * (kind // 2 ** bit % 2).astype(jnp.float32) for bit in range(3)], 0)
    data = jnp.concatenate([position, line, burgers], 0)
    return data.reshape(9, -1, SEG)

def pick_blocks(buffer, lists):
    return jnp.moveaxis(buffer[:, lists], 1, 0)

def group_stress(owned, ghosts, targets, sources):
    blocks = owned.shape[1]
    target_data = owned[:, jnp.clip(targets, 0, blocks - 1)]
    source_data = ghosts[:, sources]
    rx = target_data[0][:, :, None] - source_data[0][:, None, :]
    ry = target_data[1][:, :, None] - source_data[1][:, None, :]
    rz = target_data[2][:, :, None] - source_data[2][:, None, :]
    moment = [source_data[6 + first][:, None, :] * source_data[3 + second][:, None, :] for first in range(3) for second in range(3)]
    parts = point_stress(rx, ry, rz, moment)
    return jnp.stack([lax.optimization_barrier(jnp.sum(piece, axis=-1)) for piece in parts], 0)

def near_stress(owned, ghosts, pairs):
    groups = pairs.reshape(2, -1, pair_group)

    def step(total, index):
        targets = groups[0, index]
        piece = group_stress(owned, ghosts, targets, groups[1, index])
        return (total.at[:, targets].add(piece, mode='drop'), None)
    start = jnp.zeros((6, owned.shape[1], owned.shape[2]), jnp.float32)
    return lax.scan(step, start, jnp.arange(groups.shape[1], dtype=jnp.int32))[0]

def cell_coords(device_x, device_y, cell):
    lower_x, lower_y, lower_z = local_rows(cell)
    coord_x = (device_x * CCX + lower_x).astype(jnp.float32)
    coord_y = (device_y * CCY + lower_y).astype(jnp.float32)
    coord_z = lower_z.astype(jnp.float32)
    return tuple(jnp.broadcast_arrays(coord_x, coord_y, coord_z))

def wrapped(diff, extent):
    half = extent / 2.0
    return jnp.where(diff > half, diff - extent, jnp.where(diff < -half, diff + extent, diff))

def far_stress(moments, device_x, device_y, grid_x, grid_y):
    count = moments.shape[2]
    cells = jnp.arange(count, dtype=jnp.int32)
    target_x, target_y, target_z = cell_coords(device_x, device_y, cells)
    extent_x = float(CCX * grid_x)
    extent_y = float(CCY * grid_y)
    extent_z = float(NCZ)

    def step(total, index):
        first = index * far_group
        block = lax.dynamic_slice_in_dim(moments, first, far_group, 0)
        devices = first + jnp.arange(far_group, dtype=jnp.int32)
        source_x, source_y, source_z = cell_coords(devices[:, None] // grid_y, devices[:, None] % grid_y, cells[None, :])
        delta_x = wrapped(target_x[:, None] - source_x.reshape(1, -1), extent_x)
        delta_y = wrapped(target_y[:, None] - source_y.reshape(1, -1), extent_y)
        delta_z = wrapped(target_z[:, None] - source_z.reshape(1, -1), extent_z)
        nearby = (jnp.abs(delta_x) <= 1.0) & (jnp.abs(delta_y) <= 1.0) & (jnp.abs(delta_z) <= 1.0)
        weight = 1.0 - nearby.astype(jnp.float32)
        moment = [block[:, entry, :].reshape(1, -1) for entry in range(9)]
        parts = point_stress(delta_x, delta_y, delta_z, moment)
        return (total + jnp.stack([lax.optimization_barrier(jnp.sum(piece * weight, axis=-1)) for piece in parts], 0), None)
    start = jnp.zeros((6, count), jnp.float32)
    turns = grid_x * grid_y // far_group
    return lax.scan(step, start, jnp.arange(turns, dtype=jnp.int32))[0]

def cell_moments(data, cell, count):
    flat = data.reshape(9, -1)
    products = jnp.stack([flat[6 + first] * flat[3 + second] for first in range(3) for second in range(3)], 0)
    onehot = (cell[:, None] == jnp.arange(count, dtype=jnp.int32)[None, :]).astype(jnp.float32)
    return (jnp.dot(products, onehot, precision=lax.Precision.HIGHEST), onehot)

def nodal_terms(sigma, data, node, owner, nodes):
    flat = data.reshape(9, -1)
    full = [[sigma[0], sigma[3], sigma[4]], [sigma[3], sigma[1], sigma[5]], [sigma[4], sigma[5], sigma[2]]]
    burgers = flat[6:9]
    dline = flat[3:6]
    push = [full[row][0] * burgers[0] + full[row][1] * burgers[1] + full[row][2] * burgers[2] for row in range(3)]
    force_x = push[1] * dline[2] - push[2] * dline[1]
    force_y = push[2] * dline[0] - push[0] * dline[2]
    force_z = push[0] * dline[1] - push[1] * dline[0]
    length = jnp.sqrt(dline[0] * dline[0] + dline[1] * dline[1] + dline[2] * dline[2])
    half = 0.5 * jnp.stack([force_x, force_y, force_z, length], 0)
    slot_start = owner[0] * nodes + node[0]
    slot_end = owner[1] * nodes + node[1]
    buffer = jnp.zeros((4, 5 * nodes), jnp.float32).at[:, slot_start].add(half).at[:, slot_end].add(half)
    return buffer.reshape(4, 5, nodes)

def reference(offsets, line, burgers_kind, seg_cell, end_node, end_owner, drag, applied, pair_list, ghost_x_list, ghost_y_list):
    grid_x = N_GX
    grid_y = N_GY
    devices = grid_x * grid_y
    nodes = drag.shape[-1]
    count = CCX * CCY * NCZ
    data = jax.vmap(jax.vmap(segment_data))(offsets, line, burgers_kind, seg_cell)
    picker = jax.vmap(jax.vmap(pick_blocks))
    packet = picker(data, ghost_x_list)
    from_lower = jnp.roll(packet[:, :, 1], 1, axis=0).at[:, :, 0].add(-float(CCX))
    from_upper = jnp.roll(packet[:, :, 0], -1, axis=0).at[:, :, 0].add(float(CCX))
    section = jnp.concatenate([data, from_lower, from_upper], axis=3)
    packet_y = picker(section, ghost_y_list)
    lower_y = jnp.roll(packet_y[:, :, 1], 1, axis=1).at[:, :, 1].add(-float(CCY))
    upper_y = jnp.roll(packet_y[:, :, 0], -1, axis=1).at[:, :, 1].add(float(CCY))
    ghosts = jnp.concatenate([section, lower_y, upper_y], axis=3)
    flat_data = data.reshape((devices,) + data.shape[2:])
    flat_ghosts = ghosts.reshape((devices,) + ghosts.shape[2:])
    flat_pairs = pair_list.reshape((devices,) + pair_list.shape[2:])
    near = lax.map(lambda item: near_stress(item[0], item[1], item[2]), (flat_data, flat_ghosts, flat_pairs))
    flat_cells = seg_cell.reshape(devices, -1)
    moments, onehots = jax.vmap(lambda dat, cel: cell_moments(dat, cel, count))(flat_data, flat_cells)
    far = lax.map(lambda index: far_stress(moments, index // grid_y, index % grid_y, grid_x, grid_y), jnp.arange(devices, dtype=jnp.int32))

    def one_domain(item):
        near_one, far_one, onehot, dat, node, owner = item
        sigma = near_one.reshape(6, -1) + jnp.dot(far_one, onehot.T, precision=lax.Precision.HIGHEST) + applied[:, None]
        return nodal_terms(sigma, dat, node, owner, nodes)
    buffers = lax.map(one_domain, (near, far, onehots, flat_data, end_node.reshape((devices,) + end_node.shape[2:]), end_owner.reshape((devices,) + end_owner.shape[2:])))
    buffers = buffers.reshape((grid_x, grid_y) + buffers.shape[1:])
    total = buffers[:, :, :, 0]
    total = total + jnp.roll(buffers[:, :, :, 2], 1, axis=0) + jnp.roll(buffers[:, :, :, 1], -1, axis=0)
    total = total + jnp.roll(buffers[:, :, :, 4], 1, axis=1) + jnp.roll(buffers[:, :, :, 3], -1, axis=1)
    return total[:, :, 0:3] / (drag[:, :, None, :] * (total[:, :, 3:4] + CORE_LENGTH))
```

```python
import functools
import math

import jax
import jax.numpy as jnp
from jax import lax
from jax.experimental import pallas as pl
from jax.experimental.pallas import tpu as pltpu
from jax.sharding import PartitionSpec as P

SEG = 128
CCX = 1
CCY = 4
NCZ = 16
CORE_SQUARE = 0.25
SHEAR_TERM = 1.0 / (8.0 * math.pi)
BULK_TERM = 1.0 / (4.0 * math.pi * 0.7)
CORE_LENGTH = 1.0
COMPONENTS = ((0, 0), (1, 1), (2, 2), (0, 1), (0, 2), (1, 2))
CUBICS = (
    ((1.0, 0, (0, 0, 0)), (1.0, 1, (1, 0, 0)), (1.0, 2, (2, 0, 0))),
    ((1.0, 0, (0, 1, 1)), (1.0, 1, (1, 1, 1)), (1.0, 2, (2, 1, 1))),
    (
        (-1.0, 0, (0, 0, 0)),
        (-1.0, 1, (1, 0, 0)),
        (-1.0, 2, (2, 0, 0)),
        (-1.0, 0, (0, 1, 1)),
        (-1.0, 1, (1, 1, 1)),
        (-1.0, 2, (2, 1, 1)),
    ),
    ((1.0, 0, (0, 0, 1)), (1.0, 1, (1, 0, 1)), (1.0, 2, (2, 0, 1))),
    ((1.0, 0, (0, 0, 2)), (1.0, 1, (0, 1, 2)), (-1.0, 2, (0, 0, 0)), (-1.0, 2, (0, 1, 1))),
    ((1.0, 0, (0, 1, 2)), (1.0, 1, (1, 1, 2)), (-1.0, 2, (0, 0, 1)), (-1.0, 2, (1, 1, 1))),
)
CENTER = (CCX / 2.0, CCY / 2.0, NCZ / 2.0)
UNROLL = 4
TRANSPOSED = (((1,), (1,)), ((), ()))
f32 = jnp.float32
bf16 = jnp.bfloat16


def burgers_of(kind):
    code = kind.astype(jnp.int32)
    return [1.0 - 2.0 * ((code >> bit) & 1).astype(f32) for bit in range(3)]


def source_columns(place, dline, kind):
    burgers = burgers_of(kind)
    amat = [[burgers[i] * dline[j] for j in range(3)] for i in range(3)]
    curl = [
        amat[1][2] - amat[2][1],
        amat[2][0] - amat[0][2],
        amat[0][1] - amat[1][0],
    ]
    turned = {
        (0, 0): (None, 2.0 * amat[2][0], -2.0 * amat[1][0]),
        (1, 1): (-2.0 * amat[2][1], None, 2.0 * amat[0][1]),
        (2, 2): (2.0 * amat[1][2], -2.0 * amat[0][2], None),
        (0, 1): (-amat[2][0], amat[2][1], amat[0][0] - amat[1][1]),
        (0, 2): (amat[1][0], amat[2][2] - amat[0][0], -amat[1][2]),
        (1, 2): (amat[1][1] - amat[2][2], -amat[0][1], amat[0][2]),
    }
    bulk3 = 3.0 * BULK_TERM
    curl_k = [BULK_TERM * item for item in curl]
    curl_3k = [bulk3 * item for item in curl]
    pairs = {(a, b): place[a] * place[b] for a in range(3) for b in range(a, 3)}
    single = [[curl_3k[i] * place[a] for a in range(3)] for i in range(3)]
    double = {}

    def doubled(i, a, b):
        key = (i, min(a, b), max(a, b))
        if key not in double:
            double[key] = curl_3k[i] * pairs[key[1:]]
        return double[key]

    columns = []
    for comp, (a, b) in enumerate(COMPONENTS):
        linear5 = [0.0, 0.0, 0.0]
        linear3 = [0.0, 0.0, 0.0]
        const5 = 0.0
        for sign, i, axes in CUBICS[comp]:
            for spot in range(3):
                rest = axes[:spot] + axes[spot + 1 :]
                linear5[axes[spot]] = linear5[axes[spot]] - sign * doubled(i, *rest)
            const5 = const5 + sign * (doubled(i, axes[0], axes[1]) * place[axes[2]])
        for axis in range(3):
            alpha3 = 0.0
            alpha5 = 0.0
            if turned[(a, b)][axis] is not None:
                alpha3 = (2.0 * SHEAR_TERM) * turned[(a, b)][axis]
                alpha5 = (3.0 * CORE_SQUARE * SHEAR_TERM) * turned[(a, b)][axis]
            if axis == b:
                alpha3 = alpha3 + curl_k[a]
            if axis == a:
                alpha3 = alpha3 + curl_k[b]
            if a == b:
                alpha3 = alpha3 - curl_k[axis]
                alpha5 = alpha5 - (3.0 * CORE_SQUARE) * curl_k[axis]
            if (a, b) == (2, 2):
                alpha3 = alpha3 - curl_3k[axis]
                alpha5 = alpha5 + CORE_SQUARE * curl_3k[axis]
            if b == 2 and a == axis and a < 2:
                alpha3 = alpha3 - curl_3k[2]
                alpha5 = alpha5 + CORE_SQUARE * curl_3k[2]
            linear3[axis] = alpha3
            linear5[axis] = linear5[axis] + alpha5
            const5 = const5 - alpha5 * place[axis]
        const3 = -(linear3[0] * place[0] + linear3[1] * place[1] + linear3[2] * place[2])
        columns.append((comp, const3, const5))
        for axis in range(3):
            columns.append((8 * (axis + 1) + comp, linear3[axis], linear5[axis]))
    spots = (32, 33, 34, 35, 36, 37, 38, 39, 6)
    for i in range(3):
        for a in range(3):
            columns.append((spots[3 * i + a], None, single[i][a]))
        columns.append((8 * (i + 1) + 6, None, curl_3k[i]))
    return columns


def parts_of(value):
    head = value.astype(bf16).astype(f32)
    rest = value - head
    middle = rest.astype(bf16).astype(f32)
    return head, middle, rest - middle


def near_kernel(
    blocks, ghosts, count_ref, pairs_ref, gh_ref, base_ref, out_ref, xb, qt, acc, scr3, scr5
):
    zero = jnp.zeros((SEG, SEG), f32)
    for part in range(8):
        scr3[pl.ds(part * SEG, SEG), :] = zero
        scr5[pl.ds(part * SEG, SEG), :] = zero

    def source_step(group, carry):
        first = pl.multiple_of(group * 64, 64)
        rows = [gh_ref[pl.ds(first + row, 8, stride=8), :] for row in range(7)]
        for spot, term3, term5 in source_columns(rows[0:3], rows[3:6], rows[6]):
            for shift, piece in zip((0, 40, 80), parts_of(term5)):
                scr5[pl.ds(spot + shift, 8, stride=SEG), :] = piece
            if term3 is not None:
                for shift, piece in zip((0, 40, 80), parts_of(term3)):
                    scr3[pl.ds(spot + shift, 8, stride=SEG), :] = piece
        for part in range(8):
            qt[group * 8 + part, :, 0:SEG] = scr3[pl.ds(part * SEG, SEG), :].astype(bf16)
            qt[group * 8 + part, :, SEG : 2 * SEG] = scr5[pl.ds(part * SEG, SEG), :].astype(bf16)
        return carry

    lax.fori_loop(0, ghosts // 8, source_step, 0)

    def target_step(block, carry):
        tile = gh_ref[pl.ds(pl.multiple_of(block * 8, 8), 8), :]
        columns = jnp.transpose(tile)
        for axis in range(3):
            xb[3 * block + axis] = jnp.broadcast_to(columns[:, axis : axis + 1], (SEG, SEG))
        acc[block] = zero
        return carry

    lax.fori_loop(0, blocks, target_step, 0)

    def pair_step(turn, carry):
        for part in range(UNROLL):
            target = pairs_ref[0, turn * UNROLL + part]
            source = pairs_ref[1, turn * UNROLL + part]
            tile = gh_ref[pl.ds(pl.multiple_of(source * 8, 8), 8), :]
            heads = []
            tails = []
            for first in range(0, SEG, 32):
                dx = xb[3 * target, first : first + 32, :] - tile[0:1]
                dy = xb[3 * target + 1, first : first + 32, :] - tile[1:2]
                dz = xb[3 * target + 2, first : first + 32, :] - tile[2:3]
                inv_one = lax.rsqrt((dx * dx + CORE_SQUARE) + dy * dy + dz * dz)
                inv_two = inv_one * inv_one
                inv_three = inv_two * inv_one
                inv_five = inv_three * inv_two
                head3 = inv_three.astype(bf16)
                head5 = inv_five.astype(bf16)
                heads.append(jnp.concatenate([head3, head5], axis=1))
                tails.append(
                    jnp.concatenate(
                        [
                            (inv_three - head3.astype(f32)).astype(bf16),
                            (inv_five - head5.astype(f32)).astype(bf16),
                        ],
                        axis=1,
                    )
                )
            weight = qt[source]
            piece = lax.dot_general(
                jnp.concatenate(heads, axis=0), weight, TRANSPOSED, preferred_element_type=f32
            ) + lax.dot_general(
                jnp.concatenate(tails, axis=0), weight, TRANSPOSED, preferred_element_type=f32
            )
            acc[target] = acc[target] + piece
        return carry

    lax.fori_loop(0, count_ref[0] // UNROLL, pair_step, 0)

    def force_step(block, carry):
        first = pl.multiple_of(block * 8, 8)
        tile = gh_ref[pl.ds(first, 8), :]
        sums = jnp.transpose(acc[block])
        sums = sums[0:40] + sums[40:80] + sums[80:120]
        place = [tile[axis : axis + 1] for axis in range(3)]
        dline = [tile[3 + axis : 4 + axis] for axis in range(3)]
        burgers = burgers_of(tile[6:7])
        linear = base_ref[:, pl.ds(pl.multiple_of(block * SEG, SEG), SEG)] + (
            sums[0:8] + place[0] * sums[8:16] + place[1] * sums[16:24] + place[2] * sums[24:32]
        )
        outer = [sums[32 + item : 33 + item] for item in range(8)] + [sums[6:7]]
        lone = [sums[14:15], sums[22:23], sums[30:31]]
        twice = {(a, b): place[a] * place[b] for a in range(3) for b in range(a, 3)}
        sigma = []
        for comp in range(6):
            total = linear[comp : comp + 1]
            if comp != 2:
                curved = 0.0
                for sign, i, axes in CUBICS[comp]:
                    value = lone[i] * place[axes[2]] - outer[3 * i + axes[2]]
                    value = value * twice[tuple(sorted(axes[:2]))]
                    value = value - place[axes[2]] * (
                        outer[3 * i + axes[0]] * place[axes[1]]
                        + outer[3 * i + axes[1]] * place[axes[0]]
                    )
                    curved = curved + sign * value
                sigma.append((total, curved))
            else:
                sigma.append((total, -(sigma[0][1] + sigma[1][1])))
        sigma = [total - curved for total, curved in sigma]
        full = [
            [sigma[0], sigma[3], sigma[4]],
            [sigma[3], sigma[1], sigma[5]],
            [sigma[4], sigma[5], sigma[2]],
        ]
        push = [
            full[row][0] * burgers[0] + full[row][1] * burgers[1] + full[row][2] * burgers[2]
            for row in range(3)
        ]
        force = [
            push[1] * dline[2] - push[2] * dline[1],
            push[2] * dline[0] - push[0] * dline[2],
            push[0] * dline[1] - push[1] * dline[0],
        ]
        length = jnp.sqrt(dline[0] * dline[0] + dline[1] * dline[1] + dline[2] * dline[2])
        out_ref[pl.ds(first, 8), :] = 0.5 * jnp.concatenate(
            force + [length] + sigma[0:4], axis=0
        )
        return carry

    lax.fori_loop(0, blocks, force_step, 0)


def near_call(count, pairs, ghosts, base):
    blocks = base.shape[1] // SEG
    number = ghosts.shape[0] // 8
    return pl.pallas_call(
        functools.partial(near_kernel, blocks, number),
        out_shape=jax.ShapeDtypeStruct((blocks * 8, SEG), f32),
        in_specs=[
            pl.BlockSpec(memory_space=pltpu.SMEM),
            pl.BlockSpec(memory_space=pltpu.SMEM),
            pl.BlockSpec(memory_space=pltpu.VMEM),
            pl.BlockSpec(memory_space=pltpu.VMEM),
        ],
        out_specs=pl.BlockSpec(memory_space=pltpu.VMEM),
        scratch_shapes=[
            pltpu.VMEM((3 * blocks, SEG, SEG), f32),
            pltpu.VMEM((number, SEG, 2 * SEG), bf16),
            pltpu.VMEM((blocks, SEG, SEG), f32),
            pltpu.VMEM((8 * SEG, SEG), f32),
            pltpu.VMEM((8 * SEG, SEG), f32),
        ],
        compiler_params=pltpu.CompilerParams(vmem_limit_bytes=48 * 1024 * 1024),
    )(count, pairs, ghosts, base)


def wrapped(diff, extent):
    half = extent / 2.0
    return jnp.where(diff > half, diff - extent, jnp.where(diff < -half, diff + extent, diff))


def far_rows(plus, minus, step):
    both = [[plus[3 * i + j] + minus[3 * i + j] for j in range(3)] for i in range(3)]
    odd = [[plus[3 * i + j] - minus[3 * i + j] for j in range(3)] for i in range(3)]

    def curl_of(amat):
        return (amat[1][2] - amat[2][1], amat[2][0] - amat[0][2], amat[0][1] - amat[1][0])

    curl_both = curl_of(both)
    curl_odd = curl_of(odd)
    shear = SHEAR_TERM
    turned = [
        (None, 2.0 * both[2][0], -2.0 * both[1][0]),
        (step * (-2.0 * odd[2][1]), None, 2.0 * both[0][1]),
        (step * (2.0 * odd[1][2]), -2.0 * both[0][2], None),
        (step * -odd[2][0], both[2][1], both[0][0] - both[1][1]),
        (step * odd[1][0], both[2][2] - both[0][0], -both[1][2]),
        (step * (odd[1][1] - odd[2][2]), -both[0][1], both[0][2]),
    ]
    turned = [[None if item is None else shear * item for item in line] for line in turned]
    curls = {
        "ox": BULK_TERM * step * curl_odd[0],
        "oy": BULK_TERM * step * curl_odd[1],
        "oz": BULK_TERM * step * curl_odd[2],
        "bx": BULK_TERM * curl_both[0],
        "by": BULK_TERM * curl_both[1],
        "bz": BULK_TERM * curl_both[2],
        "sx": BULK_TERM * step * step * curl_both[0],
    }
    return turned, curls


def exchange_kernel(
    nx,
    ny,
    off_ref,
    line_ref,
    kind_ref,
    cell_ref,
    applied_ref,
    listx_ref,
    listy_ref,
    gh_ref,
    base_ref,
    products,
    hot,
    pack_x,
    land_x,
    pack_y,
    land_y,
    mine,
    row_land,
    row_block,
    all_land,
    far_acc,
    sem_x,
    sem_y,
    row_send,
    row_recv,
    all_send,
    all_recv,
):
    segs = off_ref.shape[1]
    blocks = segs // SEG
    packet = listx_ref.shape[1]
    cells = hot.shape[0]
    me_x = lax.axis_index("gx")
    me_y = lax.axis_index("gy")
    mesh_ids = pl.DeviceIdType.MESH
    barrier = pltpu.get_barrier_semaphore()

    def greet_x(step, carry):
        pl.semaphore_signal(
            barrier, inc=1, device_id=(lax.rem(me_x + step, nx), me_y), device_id_type=mesh_ids
        )
        return carry

    def greet_y(step, carry):
        pl.semaphore_signal(
            barrier, inc=1, device_id=(me_x, lax.rem(me_y + step, ny)), device_id_type=mesh_ids
        )
        return carry

    lax.fori_loop(1, nx, greet_x, 0)
    lax.fori_loop(1, ny, greet_y, 0)

    cell_iota = lax.broadcasted_iota(jnp.int32, (cells, SEG), 0)
    origin = [0.5 - CENTER[axis] for axis in range(3)]

    def block_step(block, carry):
        lanes = pl.ds(pl.multiple_of(block * SEG, SEG), SEG)
        cell = cell_ref[:, lanes]
        kind = kind_ref[:, lanes]
        dline = line_ref[:, lanes]
        shift = off_ref[:, lanes]
        corner = (cell // (CCY * NCZ), cell // NCZ % CCY, cell % NCZ)
        place = [
            (corner[axis].astype(f32) + origin[axis]) + shift[axis : axis + 1] for axis in range(3)
        ]
        code = kind.astype(f32)
        gh_ref[block] = jnp.concatenate(
            place + [dline, code, jnp.zeros((1, SEG), f32)], axis=0
        )
        burgers = burgers_of(code)
        outer = jnp.concatenate(
            [burgers[0] * dline, burgers[1] * dline, burgers[2] * dline, jnp.zeros((7, SEG), f32)],
            axis=0,
        )
        for part, piece in enumerate(parts_of(outer)):
            products[part * 16 : part * 16 + 16, lanes] = piece.astype(bf16)
        hot[:, lanes] = (cell_iota == cell).astype(f32).astype(bf16)
        return carry

    lax.fori_loop(0, blocks, block_step, 0)

    def pick_x(item, carry):
        for side in range(2):
            source = listx_ref[side, item]
            pack_x[side, item] = gh_ref[source]
        return carry

    lax.fori_loop(0, packet, pick_x, 0)
    pl.semaphore_wait(barrier, nx - 1 + ny - 1)

    copies_x = []
    for side in range(2):
        target = lax.rem(me_x + (nx - 1 if side == 0 else 1), nx)
        copies_x.append(
            pltpu.make_async_remote_copy(
                src_ref=pack_x.at[side],
                dst_ref=land_x.at[1 - side],
                send_sem=sem_x.at[side],
                recv_sem=sem_x.at[2 + side],
                device_id=(target, me_y),
                device_id_type=mesh_ids,
            )
        )
    for copy in copies_x:
        copy.start()

    moments = lax.dot_general(products[...], hot[...], TRANSPOSED, preferred_element_type=f32)
    moments = moments[0:16] + moments[16:32] + moments[32:48]
    mine[...] = jnp.concatenate([moments, jnp.zeros((16, SEG - cells), f32)], axis=1)
    row_land[me_y] = mine[...]

    def row_copy(step):
        return pltpu.make_async_remote_copy(
            src_ref=mine,
            dst_ref=row_land.at[me_y],
            send_sem=row_send.at[step],
            recv_sem=row_recv.at[step],
            device_id=(me_x, lax.rem(me_y + step, ny)),
            device_id_type=mesh_ids,
        )

    def row_start(step, carry):
        row_copy(step).start()
        return carry

    def row_wait(step, carry):
        row_copy(step).wait()
        return carry

    lax.fori_loop(1, ny, row_start, 0)

    row_iota = lax.broadcasted_iota(jnp.int32, (8, SEG), 0)
    for copy in copies_x:
        copy.wait()
    for slot in range(2):
        moved = jnp.where(row_iota == 0, -float(CCX) if slot == 0 else float(CCX), 0.0)

        def take_x(item, carry, slot=slot, moved=moved):
            gh_ref[blocks + slot * packet + item] = land_x[slot, item] + moved
            return carry

        lax.fori_loop(0, packet, take_x, 0)

    def pick_y(item, carry):
        for side in range(2):
            source = listy_ref[side, item]
            pack_y[side, item] = gh_ref[source]
        return carry

    lax.fori_loop(0, packet, pick_y, 0)
    copies_y = []
    for side in range(2):
        target = lax.rem(me_y + (ny - 1 if side == 0 else 1), ny)
        copies_y.append(
            pltpu.make_async_remote_copy(
                src_ref=pack_y.at[side],
                dst_ref=land_y.at[1 - side],
                send_sem=sem_y.at[side],
                recv_sem=sem_y.at[2 + side],
                device_id=(me_x, target),
                device_id_type=mesh_ids,
            )
        )
    for copy in copies_y:
        copy.start()

    lax.fori_loop(1, ny, row_wait, 0)
    lane_iota = lax.broadcasted_iota(jnp.int32, (16, SEG), 1)
    lasts = []
    for tile in range(4):
        first = row_land[2 * tile]
        second = row_land[2 * tile + 1]
        merged = jnp.where(lane_iota < cells, first, pltpu.roll(second, cells, 1))
        row_block[8 * tile : 8 * tile + 8, :] = merged[0:8]
        lasts.append(merged[8:9])
    row_block[32:40, :] = jnp.concatenate(lasts + [jnp.zeros((4, SEG), f32)], axis=0)
    all_land[me_x] = row_block[...]

    def all_copy(step):
        return pltpu.make_async_remote_copy(
            src_ref=row_block,
            dst_ref=all_land.at[me_x],
            send_sem=all_send.at[step],
            recv_sem=all_recv.at[step],
            device_id=(lax.rem(me_x + step, nx), me_y),
            device_id_type=mesh_ids,
        )

    def all_start(step, carry):
        all_copy(step).start()
        return carry

    def all_wait(step, carry):
        all_copy(step).wait()
        return carry

    lax.fori_loop(1, nx, all_start, 0)

    for copy in copies_y:
        copy.wait()
    for slot in range(2):
        moved = jnp.where(row_iota == 1, -float(CCY) if slot == 0 else float(CCY), 0.0)

        def take_y(item, carry, slot=slot, moved=moved):
            gh_ref[blocks + (2 + slot) * packet + item] = land_y[slot, item] + moved
            return carry

        lax.fori_loop(0, packet, take_y, 0)

    far_acc[...] = jnp.zeros_like(far_acc)
    lax.fori_loop(1, nx, all_wait, 0)

    lane = lax.broadcasted_iota(jnp.int32, (8, SEG), 1)
    source_z = (lane % NCZ).astype(f32)
    depth = [
        wrapped((row_iota + 8 * half).astype(f32) - source_z, float(NCZ)) for half in range(2)
    ]
    extent_y = float(CCY * ny)

    def far_step(turn, carry):
        apart = turn // 4
        tile = turn % 4
        step = apart.astype(f32)
        middle = apart == nx // 2
        upper = me_x >= nx // 2
        weight_plus = jnp.where(middle & jnp.logical_not(upper), 0.0, 1.0)
        weight_minus = jnp.where((apart == 0) | (middle & upper), 0.0, 1.0)
        place_plus = lax.rem(me_x - apart + nx, nx)
        place_minus = lax.rem(me_x + apart, nx)
        rows = pl.ds(pl.multiple_of(tile * 8, 8), 8)
        head_plus = all_land[place_plus, rows, :] * weight_plus
        head_minus = all_land[place_minus, rows, :] * weight_minus
        plus = [head_plus[item : item + 1] for item in range(8)]
        minus = [head_minus[item : item + 1] for item in range(8)]
        plus.append(all_land[place_plus, pl.ds(32 + tile, 1), :] * weight_plus)
        minus.append(all_land[place_minus, pl.ds(32 + tile, 1), :] * weight_minus)
        turned, curls = far_rows(plus, minus, step)
        source_y = (lane // NCZ + tile * 8).astype(f32)
        close = apart <= 1
        for quarter in range(CCY):
            ry = wrapped((me_y * CCY + quarter).astype(f32) - source_y, extent_y)
            plane = (ry * ry + CORE_SQUARE) + step * step
            beside = jnp.logical_and(jnp.abs(ry) <= 1.0, close)
            for half in range(2):
                rz = depth[half]
                inv_one = lax.rsqrt(plane + rz * rz)
                keep = jnp.logical_and(beside, jnp.abs(rz) <= 1.0)
                inv_two = inv_one * inv_one
                inv_three = jnp.where(keep, 0.0, inv_two * inv_one)
                inv_five = inv_three * inv_two
                gain = 2.0 * inv_three + (3.0 * CORE_SQUARE) * inv_five
                dot_both = curls["ox"] + ry * curls["by"] + rz * curls["bz"]
                dot_odd = curls["sx"] + ry * curls["oy"] + rz * curls["oz"]
                trace = (inv_three + (3.0 * CORE_SQUARE) * inv_five) * dot_both
                thrice = 3.0 * inv_five
                wave = thrice * dot_both
                wave_odd = thrice * dot_odd
                wave_y = wave * ry
                bends = (
                    2.0 * curls["ox"],
                    2.0 * (ry * curls["by"]),
                    2.0 * (rz * curls["bz"]),
                    ry * curls["bx"] + curls["oy"],
                    rz * curls["bx"] + curls["oz"],
                    rz * curls["by"] + ry * curls["bz"],
                )
                curved = (
                    wave * (step * step),
                    wave_y * ry,
                    (wave * rz) * rz,
                    wave_odd * ry,
                    wave_odd * rz,
                    wave_y * rz,
                )
                spot = 8 * (2 * quarter + half)
                for comp in range(6):
                    swirl = None
                    for factor, item in zip((None, ry, rz), turned[comp]):
                        if item is not None:
                            item = item if factor is None else factor * item
                            swirl = item if swirl is None else swirl + item
                    value = gain * swirl + inv_three * bends[comp] - curved[comp]
                    if comp < 3:
                        value = value - trace
                    far_acc[comp, spot : spot + 8, :] = far_acc[comp, spot : spot + 8, :] + value
        return carry

    lax.fori_loop(0, 4 * (nx // 2 + 1), far_step, 0)

    pick = (
        lax.broadcasted_iota(jnp.int32, (8, 6 * SEG), 1) // SEG
        == lax.broadcasted_iota(jnp.int32, (8, 6 * SEG), 0)
    ).astype(f32)
    far = lax.dot_general(
        pick,
        jnp.concatenate([far_acc[comp] for comp in range(6)], axis=1),
        TRANSPOSED,
        precision=lax.Precision.HIGHEST,
        preferred_element_type=f32,
    )
    far = jnp.concatenate(list(parts_of(far)) + [jnp.zeros((8, cells), f32)], axis=0).astype(bf16)
    outside = jnp.zeros((8, 1), f32)
    comp_iota = lax.broadcasted_iota(jnp.int32, (8, 1), 0)
    for comp in range(6):
        outside = jnp.where(comp_iota == comp, applied_ref[comp], outside)
    width = 8 * SEG

    def base_step(part, carry):
        lanes = pl.ds(pl.multiple_of(part * width, width), width)
        value = jnp.dot(far, hot[:, lanes], preferred_element_type=f32)
        base_ref[:, lanes] = (value[0:8] + value[8:16] + value[16:24]) + outside
        return carry

    lax.fori_loop(0, segs // width, base_step, 0)


def exchange_call(nx, ny, offsets, dline, kind, cell, applied, list_x, list_y):
    segs = offsets.shape[1]
    blocks = segs // SEG
    packet = list_x.shape[1]
    number = blocks + 4 * packet
    cells = CCX * CCY * NCZ
    vmem = pl.BlockSpec(memory_space=pltpu.VMEM)
    smem = pl.BlockSpec(memory_space=pltpu.SMEM)
    return pl.pallas_call(
        functools.partial(exchange_kernel, nx, ny),
        out_shape=(
            jax.ShapeDtypeStruct((number, 8, SEG), f32),
            jax.ShapeDtypeStruct((8, segs), f32),
        ),
        in_specs=[vmem] * 4 + [smem] * 3,
        out_specs=(vmem, vmem),
        scratch_shapes=[
            pltpu.VMEM((48, segs), bf16),
            pltpu.VMEM((cells, segs), bf16),
            pltpu.VMEM((2, packet, 8, SEG), f32),
            pltpu.VMEM((2, packet, 8, SEG), f32),
            pltpu.VMEM((2, packet, 8, SEG), f32),
            pltpu.VMEM((2, packet, 8, SEG), f32),
            pltpu.VMEM((16, SEG), f32),
            pltpu.VMEM((ny, 16, SEG), f32),
            pltpu.VMEM((40, SEG), f32),
            pltpu.VMEM((nx, 40, SEG), f32),
            pltpu.VMEM((6, cells, SEG), f32),
            pltpu.SemaphoreType.DMA((4,)),
            pltpu.SemaphoreType.DMA((4,)),
            pltpu.SemaphoreType.DMA((ny,)),
            pltpu.SemaphoreType.DMA((ny,)),
            pltpu.SemaphoreType.DMA((nx,)),
            pltpu.SemaphoreType.DMA((nx,)),
        ],
        compiler_params=pltpu.CompilerParams(
            collective_id=0, has_side_effects=True, vmem_limit_bytes=32 * 1024 * 1024
        ),
    )(offsets, dline, kind, cell, applied, list_x, list_y)


NODE_COLS = 256
CHUNK = 2048


def nodal_kernel(
    nx,
    ny,
    half_ref,
    node_ref,
    owner_ref,
    drag_ref,
    out_ref,
    column_hot,
    row_hot,
    totals,
    outgoing,
    landing,
    send_sem,
    recv_sem,
):
    segs = node_ref.shape[1]
    rows = drag_ref.shape[0]
    me_x = lax.axis_index("gx")
    me_y = lax.axis_index("gy")
    mesh_ids = pl.DeviceIdType.MESH
    beside = (
        (lax.rem(me_x + nx - 1, nx), me_y),
        (lax.rem(me_x + 1, nx), me_y),
        (me_x, lax.rem(me_y + ny - 1, ny)),
        (me_x, lax.rem(me_y + 1, ny)),
    )
    barrier = pltpu.get_barrier_semaphore()
    for device in beside:
        pl.semaphore_signal(barrier, inc=1, device_id=device, device_id_type=mesh_ids)

    column_iota = lax.broadcasted_iota(jnp.int32, (NODE_COLS, SEG), 0)

    def column_step(block, carry):
        lanes = pl.ds(pl.multiple_of(block * SEG, SEG), SEG)
        for end in range(2):
            column = node_ref[end : end + 1, lanes] % NODE_COLS
            where = pl.ds(pl.multiple_of(end * segs + block * SEG, SEG), SEG)
            column_hot[:, where] = (column_iota == column).astype(f32).astype(bf16)
        return carry

    lax.fori_loop(0, segs // SEG, column_step, 0)

    def add_up(first_row, count):
        row_iota = lax.broadcasted_iota(jnp.int32, (count, SEG), 0) + first_row

        def chunk_step(chunk, carry):
            for end in range(2):

                def tile_step(tile, inner):
                    block = chunk * (CHUNK // SEG) + tile
                    lanes = pl.ds(pl.multiple_of(block * SEG, SEG), SEG)
                    slot = (
                        owner_ref[end : end + 1, lanes] * rows
                        + node_ref[end : end + 1, lanes] // NODE_COLS
                    )
                    mask = row_iota == slot
                    values = half_ref[pl.ds(pl.multiple_of(block * 8, 8), 8), :]
                    heads = values.astype(bf16).astype(f32)
                    tails = values - heads
                    where = pl.ds(pl.multiple_of(tile * SEG, SEG), SEG)
                    for item in range(4):
                        for part, piece in enumerate((heads, tails)):
                            spot = (2 * item + part) * count
                            row_hot[spot : spot + count, where] = jnp.where(
                                mask, piece[item : item + 1], 0.0
                            ).astype(bf16)
                    return inner

                lax.fori_loop(0, CHUNK // SEG, tile_step, 0)
                where = pl.ds(pl.multiple_of(end * segs + chunk * CHUNK, CHUNK), CHUNK)
                totals[0 : 8 * count, :] = totals[0 : 8 * count, :] + lax.dot_general(
                    row_hot[0 : 8 * count, :],
                    column_hot[:, where],
                    TRANSPOSED,
                    preferred_element_type=f32,
                )
            return carry

        totals[0 : 8 * count, :] = jnp.zeros((8 * count, NODE_COLS), f32)
        lax.fori_loop(0, segs // CHUNK, chunk_step, 0)

    add_up(rows, 4 * rows)
    for side in range(4):
        for item in range(4):
            spot = 2 * item * 4 * rows + side * rows
            outgoing[side, item * rows : (item + 1) * rows, :] = (
                totals[spot : spot + rows, :] + totals[spot + 4 * rows : spot + 5 * rows, :]
            )
    pl.semaphore_wait(barrier, 4)
    copies = []
    for side in range(4):
        copies.append(
            pltpu.make_async_remote_copy(
                src_ref=outgoing.at[side],
                dst_ref=landing.at[side],
                send_sem=send_sem.at[side],
                recv_sem=recv_sem.at[side],
                device_id=beside[side],
                device_id_type=mesh_ids,
            )
        )
    for copy in copies:
        copy.start()
    add_up(0, rows)
    for copy in copies:
        copy.wait()
    sums = []
    for item in range(4):
        spot = 2 * item * rows
        value = totals[spot : spot + rows, :] + totals[spot + rows : spot + 2 * rows, :]
        for side in range(4):
            value = value + landing[side, item * rows : (item + 1) * rows, :]
        sums.append(value)
    scale = drag_ref[...] * (sums[3] + CORE_LENGTH)
    for item in range(3):
        out_ref[item] = sums[item] / scale


def nodal_call(nx, ny, half, node, owner, drag):
    segs = node.shape[1]
    rows = drag.shape[0]
    vmem = pl.BlockSpec(memory_space=pltpu.VMEM)
    return pl.pallas_call(
        functools.partial(nodal_kernel, nx, ny),
        out_shape=jax.ShapeDtypeStruct((3, rows, NODE_COLS), f32),
        in_specs=[vmem] * 4,
        out_specs=vmem,
        scratch_shapes=[
            pltpu.VMEM((NODE_COLS, 2 * segs), bf16),
            pltpu.VMEM((32 * rows, CHUNK), bf16),
            pltpu.VMEM((32 * rows, NODE_COLS), f32),
            pltpu.VMEM((4, 4 * rows, NODE_COLS), f32),
            pltpu.VMEM((4, 4 * rows, NODE_COLS), f32),
            pltpu.SemaphoreType.DMA((4,)),
            pltpu.SemaphoreType.DMA((4,)),
        ],
        compiler_params=pltpu.CompilerParams(
            collective_id=1, has_side_effects=True, vmem_limit_bytes=48 * 1024 * 1024
        ),
    )(half, node, owner, drag)


def on_device(
    offsets,
    line,
    burgers_kind,
    seg_cell,
    end_node,
    end_owner,
    drag,
    applied,
    pair_list,
    ghost_x_list,
    ghost_y_list,
):
    nx = lax.axis_size("gx")
    ny = lax.axis_size("gy")
    pairs = pair_list[0, 0]
    blocks = offsets.shape[-1] // SEG
    ghosts, base = exchange_call(
        nx,
        ny,
        offsets[0, 0],
        line[0, 0],
        burgers_kind[0],
        seg_cell[0],
        applied,
        ghost_x_list[0, 0],
        ghost_y_list[0, 0],
    )
    count = jnp.sum((pairs[0] < blocks).astype(jnp.int32)).reshape(1)
    half = near_call(count, pairs, ghosts.reshape(-1, SEG), base)
    drag_rows = drag[0, 0].reshape(-1, NODE_COLS)
    velocity = nodal_call(nx, ny, half, end_node[0, 0], end_owner[0, 0], drag_rows)
    return velocity.reshape(1, 1, 3, -1)


def solution(mesh):
    return jax.shard_map(
        on_device,
        mesh=mesh,
        in_specs=(
            P("gx", "gy", None, None),
            P("gx", "gy", None, None),
            P("gx", "gy", None),
            P("gx", "gy", None),
            P("gx", "gy", None, None),
            P("gx", "gy", None, None),
            P("gx", "gy", None),
            P(),
            P("gx", "gy", None, None),
            P("gx", "gy", None, None),
            P("gx", "gy", None, None),
        ),
        out_specs=P("gx", "gy", None, None),
        check_vma=False,
    )
```

```python
import functools
import math

import jax
import jax.numpy as jnp
from jax import lax
from jax.experimental import pallas as pl
from jax.experimental.pallas import tpu as pltpu
from jax.sharding import PartitionSpec as P

SEG = 128
CCX = 1
CCY = 4
NCZ = 16
CORE_SQUARE = 0.25
SHEAR_TERM = 1.0 / (8.0 * math.pi)
BULK_TERM = 1.0 / (4.0 * math.pi * 0.7)
CORE_LENGTH = 1.0
COMPONENTS = ((0, 0), (1, 1), (2, 2), (0, 1), (0, 2), (1, 2))
CUBICS = (
    ((1.0, 0, (0, 0, 0)), (1.0, 1, (1, 0, 0)), (1.0, 2, (2, 0, 0))),
    ((1.0, 0, (0, 1, 1)), (1.0, 1, (1, 1, 1)), (1.0, 2, (2, 1, 1))),
    (
        (-1.0, 0, (0, 0, 0)),
        (-1.0, 1, (1, 0, 0)),
        (-1.0, 2, (2, 0, 0)),
        (-1.0, 0, (0, 1, 1)),
        (-1.0, 1, (1, 1, 1)),
        (-1.0, 2, (2, 1, 1)),
    ),
    ((1.0, 0, (0, 0, 1)), (1.0, 1, (1, 0, 1)), (1.0, 2, (2, 0, 1))),
    ((1.0, 0, (0, 0, 2)), (1.0, 1, (0, 1, 2)), (-1.0, 2, (0, 0, 0)), (-1.0, 2, (0, 1, 1))),
    ((1.0, 0, (0, 1, 2)), (1.0, 1, (1, 1, 2)), (-1.0, 2, (0, 0, 1)), (-1.0, 2, (1, 1, 1))),
)
CENTER = (CCX / 2.0, CCY / 2.0, NCZ / 2.0)
UNROLL = 32
TRANSPOSED = (((1,), (1,)), ((), ()))
f32 = jnp.float32
bf16 = jnp.bfloat16


def burgers_of(kind):
    code = kind.astype(jnp.int32)
    return [1.0 - 2.0 * ((code >> bit) & 1).astype(f32) for bit in range(3)]


def source_columns(place, dline, kind):
    burgers = burgers_of(kind)
    amat = [[burgers[i] * dline[j] for j in range(3)] for i in range(3)]
    curl = [
        amat[1][2] - amat[2][1],
        amat[2][0] - amat[0][2],
        amat[0][1] - amat[1][0],
    ]
    turned = {
        (0, 0): (None, 2.0 * amat[2][0], -2.0 * amat[1][0]),
        (1, 1): (-2.0 * amat[2][1], None, 2.0 * amat[0][1]),
        (2, 2): (2.0 * amat[1][2], -2.0 * amat[0][2], None),
        (0, 1): (-amat[2][0], amat[2][1], amat[0][0] - amat[1][1]),
        (0, 2): (amat[1][0], amat[2][2] - amat[0][0], -amat[1][2]),
        (1, 2): (amat[1][1] - amat[2][2], -amat[0][1], amat[0][2]),
    }
    bulk3 = 3.0 * BULK_TERM
    curl_k = [BULK_TERM * item for item in curl]
    curl_3k = [bulk3 * item for item in curl]
    pairs = {(a, b): place[a] * place[b] for a in range(3) for b in range(a, 3)}
    single = [[curl_3k[i] * place[a] for a in range(3)] for i in range(3)]
    double = {}

    def doubled(i, a, b):
        key = (i, min(a, b), max(a, b))
        if key not in double:
            double[key] = curl_3k[i] * pairs[key[1:]]
        return double[key]

    columns = []
    for comp, (a, b) in enumerate(COMPONENTS):
        linear5 = [0.0, 0.0, 0.0]
        linear3 = [0.0, 0.0, 0.0]
        const5 = 0.0
        for sign, i, axes in CUBICS[comp]:
            for spot in range(3):
                rest = axes[:spot] + axes[spot + 1 :]
                linear5[axes[spot]] = linear5[axes[spot]] - sign * doubled(i, *rest)
            const5 = const5 + sign * (doubled(i, axes[0], axes[1]) * place[axes[2]])
        for axis in range(3):
            alpha3 = 0.0
            alpha5 = 0.0
            if turned[(a, b)][axis] is not None:
                alpha3 = (2.0 * SHEAR_TERM) * turned[(a, b)][axis]
                alpha5 = (3.0 * CORE_SQUARE * SHEAR_TERM) * turned[(a, b)][axis]
            if axis == b:
                alpha3 = alpha3 + curl_k[a]
            if axis == a:
                alpha3 = alpha3 + curl_k[b]
            if a == b:
                alpha3 = alpha3 - curl_k[axis]
                alpha5 = alpha5 - (3.0 * CORE_SQUARE) * curl_k[axis]
            if (a, b) == (2, 2):
                alpha3 = alpha3 - curl_3k[axis]
                alpha5 = alpha5 + CORE_SQUARE * curl_3k[axis]
            if b == 2 and a == axis and a < 2:
                alpha3 = alpha3 - curl_3k[2]
                alpha5 = alpha5 + CORE_SQUARE * curl_3k[2]
            linear3[axis] = alpha3
            linear5[axis] = linear5[axis] + alpha5
            const5 = const5 - alpha5 * place[axis]
        const3 = -(linear3[0] * place[0] + linear3[1] * place[1] + linear3[2] * place[2])
        columns.append((comp, const3, const5))
        for axis in range(3):
            columns.append((8 * (axis + 1) + comp, linear3[axis], linear5[axis]))
    spots = (32, 33, 34, 35, 36, 37, 38, 39, 6)
    for i in range(3):
        for a in range(3):
            columns.append((spots[3 * i + a], None, single[i][a]))
        columns.append((8 * (i + 1) + 6, None, curl_3k[i]))
    return columns


def parts_of(value):
    head = value.astype(bf16).astype(f32)
    rest = value - head
    middle = rest.astype(bf16).astype(f32)
    return head, middle, rest - middle


def near_kernel(
    blocks, ghosts, count_ref, pairs_ref, gh_ref, base_ref, out_ref, xb, qt, acc
):
    zero = jnp.zeros((SEG, SEG), f32)
    blank = jnp.zeros((8, SEG), f32)

    def source_step(group, carry):
        first = pl.multiple_of(group * 64, 64)
        rows = [gh_ref[pl.ds(first + row, 8, stride=8), :] for row in range(7)]
        spots3 = [blank] * 40
        spots5 = [blank] * 40
        for spot, term3, term5 in source_columns(rows[0:3], rows[3:6], rows[6]):
            spots5[spot] = term5
            if term3 is not None:
                spots3[spot] = term3
        for half, spots, size in ((0, spots3, 32), (1, spots5, 40)):
            swapped = jnp.transpose(jnp.stack(spots[:size], axis=0), (1, 0, 2))
            for part in range(8):
                pieces = []
                for piece in parts_of(swapped[part]):
                    pieces.append(piece)
                    if size < 40:
                        pieces.append(blank)
                pieces.append(blank)
                qt[group * 8 + part, :, half * SEG : half * SEG + SEG] = jnp.concatenate(
                    pieces, axis=0
                ).astype(bf16)
        return carry

    lax.fori_loop(0, ghosts // 8, source_step, 0)

    def target_step(block, carry):
        tile = gh_ref[pl.ds(pl.multiple_of(block * 8, 8), 8), :]
        columns = jnp.transpose(tile)
        for axis in range(3):
            xb[3 * block + axis] = jnp.broadcast_to(columns[:, axis : axis + 1], (SEG, SEG))
        acc[block] = zero
        return carry

    lax.fori_loop(0, blocks, target_step, 0, unroll=4)

    def pair_step(turn, carry):
        for part in range(UNROLL):
            target = pairs_ref[0, turn * UNROLL + part]
            source = pairs_ref[1, turn * UNROLL + part]
            tile = gh_ref[pl.ds(pl.multiple_of(source * 8, 8), 8), :]
            heads = []
            tails = []
            for first in range(0, SEG, 32):
                dx = xb[3 * target, first : first + 32, :] - tile[0:1]
                dy = xb[3 * target + 1, first : first + 32, :] - tile[1:2]
                dz = xb[3 * target + 2, first : first + 32, :] - tile[2:3]
                inv_one = lax.rsqrt((dx * dx + CORE_SQUARE) + dy * dy + dz * dz)
                inv_two = inv_one * inv_one
                inv_three = inv_two * inv_one
                inv_five = inv_three * inv_two
                head3 = inv_three.astype(bf16)
                head5 = inv_five.astype(bf16)
                heads.append(jnp.concatenate([head3, head5], axis=1))
                tails.append(
                    jnp.concatenate(
                        [
                            (inv_three - head3.astype(f32)).astype(bf16),
                            (inv_five - head5.astype(f32)).astype(bf16),
                        ],
                        axis=1,
                    )
                )
            weight = qt[source]
            piece = lax.dot_general(
                jnp.concatenate(heads, axis=0), weight, TRANSPOSED, preferred_element_type=f32
            ) + lax.dot_general(
                jnp.concatenate(tails, axis=0), weight, TRANSPOSED, preferred_element_type=f32
            )
            acc[target] = acc[target] + piece
        return carry

    lax.fori_loop(0, count_ref[0] // UNROLL, pair_step, 0)

    def force_step(block, carry):
        first = pl.multiple_of(block * 8, 8)
        tile = gh_ref[pl.ds(first, 8), :]
        sums = jnp.transpose(acc[block])
        sums = sums[0:40] + sums[40:80] + sums[80:120]
        place = [tile[axis : axis + 1] for axis in range(3)]
        dline = [tile[3 + axis : 4 + axis] for axis in range(3)]
        burgers = burgers_of(tile[6:7])
        linear = base_ref[:, pl.ds(pl.multiple_of(block * SEG, SEG), SEG)] + (
            sums[0:8] + place[0] * sums[8:16] + place[1] * sums[16:24] + place[2] * sums[24:32]
        )
        outer = [sums[32 + item : 33 + item] for item in range(8)] + [sums[6:7]]
        lone = [sums[14:15], sums[22:23], sums[30:31]]
        twice = {(a, b): place[a] * place[b] for a in range(3) for b in range(a, 3)}
        sigma = []
        for comp in range(6):
            total = linear[comp : comp + 1]
            if comp != 2:
                curved = 0.0
                for sign, i, axes in CUBICS[comp]:
                    value = lone[i] * place[axes[2]] - outer[3 * i + axes[2]]
                    value = value * twice[tuple(sorted(axes[:2]))]
                    value = value - place[axes[2]] * (
                        outer[3 * i + axes[0]] * place[axes[1]]
                        + outer[3 * i + axes[1]] * place[axes[0]]
                    )
                    curved = curved + sign * value
                sigma.append((total, curved))
            else:
                sigma.append((total, -(sigma[0][1] + sigma[1][1])))
        sigma = [total - curved for total, curved in sigma]
        full = [
            [sigma[0], sigma[3], sigma[4]],
            [sigma[3], sigma[1], sigma[5]],
            [sigma[4], sigma[5], sigma[2]],
        ]
        push = [
            full[row][0] * burgers[0] + full[row][1] * burgers[1] + full[row][2] * burgers[2]
            for row in range(3)
        ]
        force = [
            push[1] * dline[2] - push[2] * dline[1],
            push[2] * dline[0] - push[0] * dline[2],
            push[0] * dline[1] - push[1] * dline[0],
        ]
        length = jnp.sqrt(dline[0] * dline[0] + dline[1] * dline[1] + dline[2] * dline[2])
        out_ref[pl.ds(first, 8), :] = 0.5 * jnp.concatenate(
            force + [length] + sigma[0:4], axis=0
        )
        return carry

    lax.fori_loop(0, blocks, force_step, 0, unroll=4)


def near_call(count, pairs, ghosts, base):
    blocks = base.shape[1] // SEG
    number = ghosts.shape[0] // 8
    return pl.pallas_call(
        functools.partial(near_kernel, blocks, number),
        out_shape=jax.ShapeDtypeStruct((blocks * 8, SEG), f32),
        in_specs=[
            pl.BlockSpec(memory_space=pltpu.SMEM),
            pl.BlockSpec(memory_space=pltpu.SMEM),
            pl.BlockSpec(memory_space=pltpu.VMEM),
            pl.BlockSpec(memory_space=pltpu.VMEM),
        ],
        out_specs=pl.BlockSpec(memory_space=pltpu.VMEM),
        scratch_shapes=[
            pltpu.VMEM((3 * blocks, SEG, SEG), f32),
            pltpu.VMEM((number, SEG, 2 * SEG), bf16),
            pltpu.VMEM((blocks, SEG, SEG), f32),
        ],
        compiler_params=pltpu.CompilerParams(vmem_limit_bytes=48 * 1024 * 1024),
    )(count, pairs, ghosts, base)


def wrapped(diff, extent):
    half = extent / 2.0
    return jnp.where(diff > half, diff - extent, jnp.where(diff < -half, diff + extent, diff))


def far_rows(plus, minus, step):
    both = [[plus[3 * i + j] + minus[3 * i + j] for j in range(3)] for i in range(3)]
    odd = [[plus[3 * i + j] - minus[3 * i + j] for j in range(3)] for i in range(3)]

    def curl_of(amat):
        return (amat[1][2] - amat[2][1], amat[2][0] - amat[0][2], amat[0][1] - amat[1][0])

    curl_both = curl_of(both)
    curl_odd = curl_of(odd)
    shear = SHEAR_TERM
    turned = [
        (None, 2.0 * both[2][0], -2.0 * both[1][0]),
        (step * (-2.0 * odd[2][1]), None, 2.0 * both[0][1]),
        (step * (2.0 * odd[1][2]), -2.0 * both[0][2], None),
        (step * -odd[2][0], both[2][1], both[0][0] - both[1][1]),
        (step * odd[1][0], both[2][2] - both[0][0], -both[1][2]),
        (step * (odd[1][1] - odd[2][2]), -both[0][1], both[0][2]),
    ]
    turned = [[None if item is None else shear * item for item in line] for line in turned]
    curls = {
        "ox": BULK_TERM * step * curl_odd[0],
        "oy": BULK_TERM * step * curl_odd[1],
        "oz": BULK_TERM * step * curl_odd[2],
        "bx": BULK_TERM * curl_both[0],
        "by": BULK_TERM * curl_both[1],
        "bz": BULK_TERM * curl_both[2],
        "sx": BULK_TERM * step * step * curl_both[0],
    }
    return turned, curls


def exchange_kernel(
    nx,
    ny,
    off_ref,
    line_ref,
    kind_ref,
    cell_ref,
    applied_ref,
    listx_ref,
    listy_ref,
    gh_ref,
    base_ref,
    products,
    hot,
    pack_x,
    land_x,
    pack_y,
    land_y,
    mine,
    row_land,
    row_block,
    all_land,
    far_acc,
    sem_x,
    sem_y,
    row_send,
    row_recv,
    all_send,
    all_recv,
):
    segs = off_ref.shape[1]
    blocks = segs // SEG
    packet = listx_ref.shape[1]
    cells = hot.shape[0]
    me_x = lax.axis_index("gx")
    me_y = lax.axis_index("gy")
    mesh_ids = pl.DeviceIdType.MESH
    barrier = pltpu.get_barrier_semaphore()

    def greet_x(step, carry):
        pl.semaphore_signal(
            barrier, inc=1, device_id=(lax.rem(me_x + step, nx), me_y), device_id_type=mesh_ids
        )
        return carry

    def greet_y(step, carry):
        pl.semaphore_signal(
            barrier, inc=1, device_id=(me_x, lax.rem(me_y + step, ny)), device_id_type=mesh_ids
        )
        return carry

    lax.fori_loop(1, nx, greet_x, 0)
    lax.fori_loop(1, ny, greet_y, 0)

    cell_iota = lax.broadcasted_iota(jnp.int32, (cells, SEG), 0)
    origin = [0.5 - CENTER[axis] for axis in range(3)]

    def block_step(block, carry):
        lanes = pl.ds(pl.multiple_of(block * SEG, SEG), SEG)
        cell = cell_ref[:, lanes]
        kind = kind_ref[:, lanes]
        dline = line_ref[:, lanes]
        shift = off_ref[:, lanes]
        corner = (cell // (CCY * NCZ), cell // NCZ % CCY, cell % NCZ)
        place = [
            (corner[axis].astype(f32) + origin[axis]) + shift[axis : axis + 1] for axis in range(3)
        ]
        code = kind.astype(f32)
        gh_ref[block] = jnp.concatenate(
            place + [dline, code, jnp.zeros((1, SEG), f32)], axis=0
        )
        burgers = burgers_of(code)
        outer = jnp.concatenate(
            [burgers[0] * dline, burgers[1] * dline, burgers[2] * dline, jnp.zeros((7, SEG), f32)],
            axis=0,
        )
        for part, piece in enumerate(parts_of(outer)):
            products[part * 16 : part * 16 + 16, lanes] = piece.astype(bf16)
        hot[:, lanes] = (cell_iota == cell).astype(f32).astype(bf16)
        return carry

    lax.fori_loop(0, blocks, block_step, 0)

    def pick_x(item, carry):
        for side in range(2):
            source = listx_ref[side, item]
            pack_x[side, item] = gh_ref[source]
        return carry

    lax.fori_loop(0, packet, pick_x, 0)
    pl.semaphore_wait(barrier, nx - 1 + ny - 1)

    copies_x = []
    for side in range(2):
        target = lax.rem(me_x + (nx - 1 if side == 0 else 1), nx)
        copies_x.append(
            pltpu.make_async_remote_copy(
                src_ref=pack_x.at[side],
                dst_ref=land_x.at[1 - side],
                send_sem=sem_x.at[side],
                recv_sem=sem_x.at[2 + side],
                device_id=(target, me_y),
                device_id_type=mesh_ids,
            )
        )
    for copy in copies_x:
        copy.start()

    moments = lax.dot_general(products[...], hot[...], TRANSPOSED, preferred_element_type=f32)
    moments = moments[0:16] + moments[16:32] + moments[32:48]
    mine[...] = jnp.concatenate([moments, jnp.zeros((16, SEG - cells), f32)], axis=1)
    row_land[me_y] = mine[...]

    def row_copy(step):
        return pltpu.make_async_remote_copy(
            src_ref=mine,
            dst_ref=row_land.at[me_y],
            send_sem=row_send.at[step],
            recv_sem=row_recv.at[step],
            device_id=(me_x, lax.rem(me_y + step, ny)),
            device_id_type=mesh_ids,
        )

    def row_start(step, carry):
        row_copy(step).start()
        return carry

    def row_wait(step, carry):
        row_copy(step).wait()
        return carry

    lax.fori_loop(1, ny, row_start, 0)

    row_iota = lax.broadcasted_iota(jnp.int32, (8, SEG), 0)
    for copy in copies_x:
        copy.wait()
    for slot in range(2):
        moved = jnp.where(row_iota == 0, -float(CCX) if slot == 0 else float(CCX), 0.0)

        def take_x(item, carry, slot=slot, moved=moved):
            gh_ref[blocks + slot * packet + item] = land_x[slot, item] + moved
            return carry

        lax.fori_loop(0, packet, take_x, 0)

    def pick_y(item, carry):
        for side in range(2):
            source = listy_ref[side, item]
            pack_y[side, item] = gh_ref[source]
        return carry

    lax.fori_loop(0, packet, pick_y, 0)
    copies_y = []
    for side in range(2):
        target = lax.rem(me_y + (ny - 1 if side == 0 else 1), ny)
        copies_y.append(
            pltpu.make_async_remote_copy(
                src_ref=pack_y.at[side],
                dst_ref=land_y.at[1 - side],
                send_sem=sem_y.at[side],
                recv_sem=sem_y.at[2 + side],
                device_id=(me_x, target),
                device_id_type=mesh_ids,
            )
        )
    for copy in copies_y:
        copy.start()

    lax.fori_loop(1, ny, row_wait, 0)
    lane_iota = lax.broadcasted_iota(jnp.int32, (16, SEG), 1)
    lasts = []
    for tile in range(4):
        first = row_land[2 * tile]
        second = row_land[2 * tile + 1]
        merged = jnp.where(lane_iota < cells, first, pltpu.roll(second, cells, 1))
        row_block[8 * tile : 8 * tile + 8, :] = merged[0:8]
        lasts.append(merged[8:9])
    row_block[32:40, :] = jnp.concatenate(lasts + [jnp.zeros((4, SEG), f32)], axis=0)
    all_land[me_x] = row_block[...]

    def all_copy(step):
        return pltpu.make_async_remote_copy(
            src_ref=row_block,
            dst_ref=all_land.at[me_x],
            send_sem=all_send.at[step],
            recv_sem=all_recv.at[step],
            device_id=(lax.rem(me_x + step, nx), me_y),
            device_id_type=mesh_ids,
        )

    def all_start(step, carry):
        all_copy(step).start()
        return carry

    def all_wait(step, carry):
        all_copy(step).wait()
        return carry

    lax.fori_loop(1, nx, all_start, 0)

    for copy in copies_y:
        copy.wait()
    for slot in range(2):
        moved = jnp.where(row_iota == 1, -float(CCY) if slot == 0 else float(CCY), 0.0)

        def take_y(item, carry, slot=slot, moved=moved):
            gh_ref[blocks + (2 + slot) * packet + item] = land_y[slot, item] + moved
            return carry

        lax.fori_loop(0, packet, take_y, 0)

    far_acc[...] = jnp.zeros_like(far_acc)
    lax.fori_loop(1, nx, all_wait, 0)

    lane = lax.broadcasted_iota(jnp.int32, (8, SEG), 1)
    source_z = (lane % NCZ).astype(f32)
    depth = [
        wrapped((row_iota + 8 * half).astype(f32) - source_z, float(NCZ)) for half in range(2)
    ]
    extent_y = float(CCY * ny)

    def far_step(turn, carry):
        apart = turn // 4
        tile = turn % 4
        step = apart.astype(f32)
        middle = apart == nx // 2
        upper = me_x >= nx // 2
        weight_plus = jnp.where(middle & jnp.logical_not(upper), 0.0, 1.0)
        weight_minus = jnp.where((apart == 0) | (middle & upper), 0.0, 1.0)
        place_plus = lax.rem(me_x - apart + nx, nx)
        place_minus = lax.rem(me_x + apart, nx)
        rows = pl.ds(pl.multiple_of(tile * 8, 8), 8)
        head_plus = all_land[place_plus, rows, :] * weight_plus
        head_minus = all_land[place_minus, rows, :] * weight_minus
        plus = [head_plus[item : item + 1] for item in range(8)]
        minus = [head_minus[item : item + 1] for item in range(8)]
        plus.append(all_land[place_plus, pl.ds(32 + tile, 1), :] * weight_plus)
        minus.append(all_land[place_minus, pl.ds(32 + tile, 1), :] * weight_minus)
        turned, curls = far_rows(plus, minus, step)
        source_y = (lane // NCZ + tile * 8).astype(f32)
        close = apart <= 1
        for quarter in range(CCY):
            ry = wrapped((me_y * CCY + quarter).astype(f32) - source_y, extent_y)
            plane = (ry * ry + CORE_SQUARE) + step * step
            beside = jnp.logical_and(jnp.abs(ry) <= 1.0, close)
            for half in range(2):
                rz = depth[half]
                inv_one = lax.rsqrt(plane + rz * rz)
                keep = jnp.logical_and(beside, jnp.abs(rz) <= 1.0)
                inv_two = inv_one * inv_one
                inv_three = jnp.where(keep, 0.0, inv_two * inv_one)
                inv_five = inv_three * inv_two
                gain = 2.0 * inv_three + (3.0 * CORE_SQUARE) * inv_five
                dot_both = curls["ox"] + ry * curls["by"] + rz * curls["bz"]
                dot_odd = curls["sx"] + ry * curls["oy"] + rz * curls["oz"]
                trace = (inv_three + (3.0 * CORE_SQUARE) * inv_five) * dot_both
                thrice = 3.0 * inv_five
                wave = thrice * dot_both
                wave_odd = thrice * dot_odd
                wave_y = wave * ry
                bends = (
                    2.0 * curls["ox"],
                    2.0 * (ry * curls["by"]),
                    2.0 * (rz * curls["bz"]),
                    ry * curls["bx"] + curls["oy"],
                    rz * curls["bx"] + curls["oz"],
                    rz * curls["by"] + ry * curls["bz"],
                )
                curved = (
                    wave * (step * step),
                    wave_y * ry,
                    (wave * rz) * rz,
                    wave_odd * ry,
                    wave_odd * rz,
                    wave_y * rz,
                )
                spot = 8 * (2 * quarter + half)
                for comp in range(6):
                    swirl = None
                    for factor, item in zip((None, ry, rz), turned[comp]):
                        if item is not None:
                            item = item if factor is None else factor * item
                            swirl = item if swirl is None else swirl + item
                    value = gain * swirl + inv_three * bends[comp] - curved[comp]
                    if comp < 3:
                        value = value - trace
                    far_acc[comp, spot : spot + 8, :] = far_acc[comp, spot : spot + 8, :] + value
        return carry

    lax.fori_loop(0, 4 * (nx // 2 + 1), far_step, 0)

    pick = (
        lax.broadcasted_iota(jnp.int32, (8, 6 * SEG), 1) // SEG
        == lax.broadcasted_iota(jnp.int32, (8, 6 * SEG), 0)
    ).astype(f32)
    far = lax.dot_general(
        pick,
        jnp.concatenate([far_acc[comp] for comp in range(6)], axis=1),
        TRANSPOSED,
        precision=lax.Precision.HIGHEST,
        preferred_element_type=f32,
    )
    far = jnp.concatenate(list(parts_of(far)) + [jnp.zeros((8, cells), f32)], axis=0).astype(bf16)
    outside = jnp.zeros((8, 1), f32)
    comp_iota = lax.broadcasted_iota(jnp.int32, (8, 1), 0)
    for comp in range(6):
        outside = jnp.where(comp_iota == comp, applied_ref[comp], outside)
    width = 8 * SEG

    def base_step(part, carry):
        lanes = pl.ds(pl.multiple_of(part * width, width), width)
        value = jnp.dot(far, hot[:, lanes], preferred_element_type=f32)
        base_ref[:, lanes] = (value[0:8] + value[8:16] + value[16:24]) + outside
        return carry

    lax.fori_loop(0, segs // width, base_step, 0)


def exchange_call(nx, ny, offsets, dline, kind, cell, applied, list_x, list_y):
    segs = offsets.shape[1]
    blocks = segs // SEG
    packet = list_x.shape[1]
    number = blocks + 4 * packet
    cells = CCX * CCY * NCZ
    vmem = pl.BlockSpec(memory_space=pltpu.VMEM)
    smem = pl.BlockSpec(memory_space=pltpu.SMEM)
    return pl.pallas_call(
        functools.partial(exchange_kernel, nx, ny),
        out_shape=(
            jax.ShapeDtypeStruct((number, 8, SEG), f32),
            jax.ShapeDtypeStruct((8, segs), f32),
        ),
        in_specs=[vmem] * 4 + [smem] * 3,
        out_specs=(vmem, vmem),
        scratch_shapes=[
            pltpu.VMEM((48, segs), bf16),
            pltpu.VMEM((cells, segs), bf16),
            pltpu.VMEM((2, packet, 8, SEG), f32),
            pltpu.VMEM((2, packet, 8, SEG), f32),
            pltpu.VMEM((2, packet, 8, SEG), f32),
            pltpu.VMEM((2, packet, 8, SEG), f32),
            pltpu.VMEM((16, SEG), f32),
            pltpu.VMEM((ny, 16, SEG), f32),
            pltpu.VMEM((40, SEG), f32),
            pltpu.VMEM((nx, 40, SEG), f32),
            pltpu.VMEM((6, cells, SEG), f32),
            pltpu.SemaphoreType.DMA((4,)),
            pltpu.SemaphoreType.DMA((4,)),
            pltpu.SemaphoreType.DMA((ny,)),
            pltpu.SemaphoreType.DMA((ny,)),
            pltpu.SemaphoreType.DMA((nx,)),
            pltpu.SemaphoreType.DMA((nx,)),
        ],
        compiler_params=pltpu.CompilerParams(
            collective_id=0, has_side_effects=True, vmem_limit_bytes=32 * 1024 * 1024
        ),
    )(offsets, dline, kind, cell, applied, list_x, list_y)


NODE_COLS = 256
CHUNK = 1024


def nodal_kernel(
    nx,
    ny,
    half_ref,
    node_ref,
    owner_ref,
    drag_ref,
    out_ref,
    column_hot,
    row_hot,
    totals,
    outgoing,
    landing,
    send_sem,
    recv_sem,
):
    segs = node_ref.shape[1]
    rows = drag_ref.shape[0]
    me_x = lax.axis_index("gx")
    me_y = lax.axis_index("gy")
    mesh_ids = pl.DeviceIdType.MESH
    beside = (
        (lax.rem(me_x + nx - 1, nx), me_y),
        (lax.rem(me_x + 1, nx), me_y),
        (me_x, lax.rem(me_y + ny - 1, ny)),
        (me_x, lax.rem(me_y + 1, ny)),
    )
    barrier = pltpu.get_barrier_semaphore()
    for device in beside:
        pl.semaphore_signal(barrier, inc=1, device_id=device, device_id_type=mesh_ids)

    column_iota = lax.broadcasted_iota(jnp.int32, (NODE_COLS, SEG), 0)

    def column_step(block, carry):
        lanes = pl.ds(pl.multiple_of(block * SEG, SEG), SEG)
        for end in range(2):
            column = node_ref[end : end + 1, lanes] % NODE_COLS
            where = pl.ds(pl.multiple_of(end * segs + block * SEG, SEG), SEG)
            column_hot[:, where] = (column_iota == column).astype(f32).astype(bf16)
        return carry

    lax.fori_loop(0, segs // SEG, column_step, 0, unroll=2)

    tiles = CHUNK // SEG
    chunks = 2 * segs // CHUNK

    def add_up(first_row, count):
        row_iota = lax.broadcasted_iota(jnp.int32, (count, SEG), 0) + first_row

        def build(buffer, chunk):
            end = chunk // (segs // CHUNK)
            for tile in range(tiles):
                block = chunk % (segs // CHUNK) * tiles + tile
                lanes = pl.ds(pl.multiple_of(block * SEG, SEG), SEG)
                both = owner_ref[:, lanes] * rows + node_ref[:, lanes] // NODE_COLS
                slot = jnp.where(end == 0, both[0:1], both[1:2])
                mask = (row_iota == slot).astype(f32).astype(bf16)
                values = half_ref[pl.ds(pl.multiple_of(block * 8, 8), 8), :]
                heads = values.astype(bf16).astype(f32)
                tails = values - heads
                for item in range(4):
                    for part, piece in enumerate((heads, tails)):
                        spot = (2 * item + part) * count
                        row = jnp.broadcast_to(piece[item : item + 1], (16, SEG)).astype(bf16)
                        row = jnp.concatenate([row] * (count // 16), axis=0)
                        row_hot[buffer, spot : spot + count, tile * SEG : (tile + 1) * SEG] = (
                            mask * row
                        )

        def add_chunk(buffer, chunk):
            where = pl.ds(pl.multiple_of(chunk * CHUNK, CHUNK), CHUNK)
            totals[0 : 8 * count, :] = totals[0 : 8 * count, :] + lax.dot_general(
                row_hot[buffer, 0 : 8 * count, :],
                column_hot[:, where],
                TRANSPOSED,
                preferred_element_type=f32,
            )

        def chunk_step(turn, carry):
            build(1, 2 * turn + 1)
            add_chunk(0, 2 * turn)
            build(0, jnp.minimum(2 * turn + 2, chunks - 1))
            add_chunk(1, 2 * turn + 1)
            return carry

        totals[0 : 8 * count, :] = jnp.zeros((8 * count, NODE_COLS), f32)
        build(0, jnp.int32(0))
        lax.fori_loop(0, chunks // 2, chunk_step, 0)

    add_up(rows, 4 * rows)
    for side in range(4):
        for item in range(4):
            spot = 2 * item * 4 * rows + side * rows
            outgoing[side, item * rows : (item + 1) * rows, :] = (
                totals[spot : spot + rows, :] + totals[spot + 4 * rows : spot + 5 * rows, :]
            )
    pl.semaphore_wait(barrier, 4)
    copies = []
    for side in range(4):
        copies.append(
            pltpu.make_async_remote_copy(
                src_ref=outgoing.at[side],
                dst_ref=landing.at[side],
                send_sem=send_sem.at[side],
                recv_sem=recv_sem.at[side],
                device_id=beside[side],
                device_id_type=mesh_ids,
            )
        )
    for copy in copies:
        copy.start()
    add_up(0, rows)
    for copy in copies:
        copy.wait()
    sums = []
    for item in range(4):
        spot = 2 * item * rows
        value = totals[spot : spot + rows, :] + totals[spot + rows : spot + 2 * rows, :]
        for side in range(4):
            value = value + landing[side, item * rows : (item + 1) * rows, :]
        sums.append(value)
    scale = drag_ref[...] * (sums[3] + CORE_LENGTH)
    for item in range(3):
        out_ref[item] = sums[item] / scale


def nodal_call(nx, ny, half, node, owner, drag):
    segs = node.shape[1]
    rows = drag.shape[0]
    vmem = pl.BlockSpec(memory_space=pltpu.VMEM)
    return pl.pallas_call(
        functools.partial(nodal_kernel, nx, ny),
        out_shape=jax.ShapeDtypeStruct((3, rows, NODE_COLS), f32),
        in_specs=[vmem] * 4,
        out_specs=vmem,
        scratch_shapes=[
            pltpu.VMEM((NODE_COLS, 2 * segs), bf16),
            pltpu.VMEM((2, 32 * rows, CHUNK), bf16),
            pltpu.VMEM((32 * rows, NODE_COLS), f32),
            pltpu.VMEM((4, 4 * rows, NODE_COLS), f32),
            pltpu.VMEM((4, 4 * rows, NODE_COLS), f32),
            pltpu.SemaphoreType.DMA((4,)),
            pltpu.SemaphoreType.DMA((4,)),
        ],
        compiler_params=pltpu.CompilerParams(
            collective_id=1, has_side_effects=True, vmem_limit_bytes=48 * 1024 * 1024
        ),
    )(half, node, owner, drag)


def on_device(
    offsets,
    line,
    burgers_kind,
    seg_cell,
    end_node,
    end_owner,
    drag,
    applied,
    pair_list,
    ghost_x_list,
    ghost_y_list,
):
    nx = lax.axis_size("gx")
    ny = lax.axis_size("gy")
    pairs = pair_list[0, 0]
    blocks = offsets.shape[-1] // SEG
    ghosts, base = exchange_call(
        nx,
        ny,
        offsets[0, 0],
        line[0, 0],
        burgers_kind[0],
        seg_cell[0],
        applied,
        ghost_x_list[0, 0],
        ghost_y_list[0, 0],
    )
    count = jnp.sum((pairs[0] < blocks).astype(jnp.int32)).reshape(1)
    half = near_call(count, pairs, ghosts.reshape(-1, SEG), base)
    drag_rows = drag[0, 0].reshape(-1, NODE_COLS)
    velocity = nodal_call(nx, ny, half, end_node[0, 0], end_owner[0, 0], drag_rows)
    return velocity.reshape(1, 1, 3, -1)


def solution(mesh):
    return jax.shard_map(
        on_device,
        mesh=mesh,
        in_specs=(
            P("gx", "gy", None, None),
            P("gx", "gy", None, None),
            P("gx", "gy", None),
            P("gx", "gy", None),
            P("gx", "gy", None, None),
            P("gx", "gy", None, None),
            P("gx", "gy", None),
            P(),
            P("gx", "gy", None, None),
            P("gx", "gy", None, None),
            P("gx", "gy", None, None),
        ),
        out_specs=P("gx", "gy", None, None),
        check_vma=False,
    )
```

```python
import functools
import math

import jax
import jax.numpy as jnp
from jax import lax
from jax.experimental import pallas as pl
from jax.experimental.pallas import tpu as pltpu
from jax.sharding import PartitionSpec as P

SEG = 128
CCX = 1
CCY = 4
NCZ = 16
CORE_SQUARE = 0.25
SHEAR_TERM = 1.0 / (8.0 * math.pi)
BULK_TERM = 1.0 / (4.0 * math.pi * 0.7)
CORE_LENGTH = 1.0
COMPONENTS = ((0, 0), (1, 1), (2, 2), (0, 1), (0, 2), (1, 2))
CUBICS = (
    ((1.0, 0, (0, 0, 0)), (1.0, 1, (1, 0, 0)), (1.0, 2, (2, 0, 0))),
    ((1.0, 0, (0, 1, 1)), (1.0, 1, (1, 1, 1)), (1.0, 2, (2, 1, 1))),
    (
        (-1.0, 0, (0, 0, 0)),
        (-1.0, 1, (1, 0, 0)),
        (-1.0, 2, (2, 0, 0)),
        (-1.0, 0, (0, 1, 1)),
        (-1.0, 1, (1, 1, 1)),
        (-1.0, 2, (2, 1, 1)),
    ),
    ((1.0, 0, (0, 0, 1)), (1.0, 1, (1, 0, 1)), (1.0, 2, (2, 0, 1))),
    ((1.0, 0, (0, 0, 2)), (1.0, 1, (0, 1, 2)), (-1.0, 2, (0, 0, 0)), (-1.0, 2, (0, 1, 1))),
    ((1.0, 0, (0, 1, 2)), (1.0, 1, (1, 1, 2)), (-1.0, 2, (0, 0, 1)), (-1.0, 2, (1, 1, 1))),
)
CENTER = (CCX / 2.0, CCY / 2.0, NCZ / 2.0)
UNROLL = 32
PAIR_STEP = 256
TRANSPOSED = (((1,), (1,)), ((), ()))
f32 = jnp.float32
bf16 = jnp.bfloat16


def burgers_of(kind):
    code = kind.astype(jnp.int32)
    return [1.0 - 2.0 * ((code >> bit) & 1).astype(f32) for bit in range(3)]


def source_columns(place, dline, kind):
    burgers = burgers_of(kind)
    amat = [[burgers[i] * dline[j] for j in range(3)] for i in range(3)]
    curl = [
        amat[1][2] - amat[2][1],
        amat[2][0] - amat[0][2],
        amat[0][1] - amat[1][0],
    ]
    turned = {
        (0, 0): (None, 2.0 * amat[2][0], -2.0 * amat[1][0]),
        (1, 1): (-2.0 * amat[2][1], None, 2.0 * amat[0][1]),
        (2, 2): (2.0 * amat[1][2], -2.0 * amat[0][2], None),
        (0, 1): (-amat[2][0], amat[2][1], amat[0][0] - amat[1][1]),
        (0, 2): (amat[1][0], amat[2][2] - amat[0][0], -amat[1][2]),
        (1, 2): (amat[1][1] - amat[2][2], -amat[0][1], amat[0][2]),
    }
    bulk3 = 3.0 * BULK_TERM
    curl_k = [BULK_TERM * item for item in curl]
    curl_3k = [bulk3 * item for item in curl]
    pairs = {(a, b): place[a] * place[b] for a in range(3) for b in range(a, 3)}
    single = [[curl_3k[i] * place[a] for a in range(3)] for i in range(3)]
    double = {}

    def doubled(i, a, b):
        key = (i, min(a, b), max(a, b))
        if key not in double:
            double[key] = curl_3k[i] * pairs[key[1:]]
        return double[key]

    columns = []
    for comp, (a, b) in enumerate(COMPONENTS):
        linear5 = [0.0, 0.0, 0.0]
        linear3 = [0.0, 0.0, 0.0]
        const5 = 0.0
        for sign, i, axes in CUBICS[comp]:
            for spot in range(3):
                rest = axes[:spot] + axes[spot + 1 :]
                linear5[axes[spot]] = linear5[axes[spot]] - sign * doubled(i, *rest)
            const5 = const5 + sign * (doubled(i, axes[0], axes[1]) * place[axes[2]])
        for axis in range(3):
            alpha3 = 0.0
            alpha5 = 0.0
            if turned[(a, b)][axis] is not None:
                alpha3 = (2.0 * SHEAR_TERM) * turned[(a, b)][axis]
                alpha5 = (3.0 * CORE_SQUARE * SHEAR_TERM) * turned[(a, b)][axis]
            if axis == b:
                alpha3 = alpha3 + curl_k[a]
            if axis == a:
                alpha3 = alpha3 + curl_k[b]
            if a == b:
                alpha3 = alpha3 - curl_k[axis]
                alpha5 = alpha5 - (3.0 * CORE_SQUARE) * curl_k[axis]
            if (a, b) == (2, 2):
                alpha3 = alpha3 - curl_3k[axis]
                alpha5 = alpha5 + CORE_SQUARE * curl_3k[axis]
            if b == 2 and a == axis and a < 2:
                alpha3 = alpha3 - curl_3k[2]
                alpha5 = alpha5 + CORE_SQUARE * curl_3k[2]
            linear3[axis] = alpha3
            linear5[axis] = linear5[axis] + alpha5
            const5 = const5 - alpha5 * place[axis]
        const3 = -(linear3[0] * place[0] + linear3[1] * place[1] + linear3[2] * place[2])
        columns.append((comp, const3, const5))
        for axis in range(3):
            columns.append((8 * (axis + 1) + comp, linear3[axis], linear5[axis]))
    spots = (32, 33, 34, 35, 36, 37, 38, 39, 6)
    for i in range(3):
        for a in range(3):
            columns.append((spots[3 * i + a], None, single[i][a]))
        columns.append((8 * (i + 1) + 6, None, curl_3k[i]))
    return columns


def parts_of(value):
    head = value.astype(bf16).astype(f32)
    rest = value - head
    middle = rest.astype(bf16).astype(f32)
    return head, middle, rest - middle


def near_kernel(
    blocks, ghosts, pairs_ref, gh_ref, base_ref, out_ref, xb, qt, acc
):
    zero = jnp.zeros((SEG, SEG), f32)
    blank = jnp.zeros((8, SEG), f32)

    def source_step(group, carry):
        first = pl.multiple_of(group * 64, 64)
        rows = [gh_ref[pl.ds(first + row, 8, stride=8), :] for row in range(7)]
        spots3 = [blank] * 40
        spots5 = [blank] * 40
        for spot, term3, term5 in source_columns(rows[0:3], rows[3:6], rows[6]):
            spots5[spot] = term5
            if term3 is not None:
                spots3[spot] = term3
        for half, spots, size in ((0, spots3, 32), (1, spots5, 40)):
            swapped = jnp.transpose(jnp.stack(spots[:size], axis=0), (1, 0, 2))
            for part in range(8):
                pieces = []
                for piece in parts_of(swapped[part]):
                    pieces.append(piece)
                    if size < 40:
                        pieces.append(blank)
                pieces.append(blank)
                qt[group * 8 + part, :, half * SEG : half * SEG + SEG] = jnp.concatenate(
                    pieces, axis=0
                ).astype(bf16)
        return carry

    def target_step(block):
        tile = gh_ref[pl.ds(pl.multiple_of(block * 8, 8), 8), :]
        columns = jnp.transpose(tile)
        for axis in range(3):
            xb[3 * block + axis] = jnp.broadcast_to(columns[:, axis : axis + 1], (SEG, SEG))
        acc[block] = zero

    def both_step(group, carry):
        for part in range(8):
            target_step(group * 8 + part)
        return source_step(group, carry)

    lax.fori_loop(0, blocks // 8, both_step, 0)
    lax.fori_loop(blocks // 8, ghosts // 8, source_step, 0)

    def pair_step(turn, carry):
        for part in range(UNROLL):
            target = pairs_ref[0, turn * UNROLL + part]
            source = pairs_ref[1, turn * UNROLL + part]
            tile = gh_ref[pl.ds(pl.multiple_of(source * 8, 8), 8), :]
            heads = []
            tails = []
            for first in range(0, SEG, 32):
                dx = xb[3 * target, first : first + 32, :] - tile[0:1]
                dy = xb[3 * target + 1, first : first + 32, :] - tile[1:2]
                dz = xb[3 * target + 2, first : first + 32, :] - tile[2:3]
                inv_one = lax.rsqrt((dx * dx + CORE_SQUARE) + dy * dy + dz * dz)
                inv_two = inv_one * inv_one
                inv_three = inv_two * inv_one
                inv_five = inv_three * inv_two
                head3 = inv_three.astype(bf16)
                head5 = inv_five.astype(bf16)
                heads.append(jnp.concatenate([head3, head5], axis=1))
                tails.append(
                    jnp.concatenate(
                        [
                            (inv_three - head3.astype(f32)).astype(bf16),
                            (inv_five - head5.astype(f32)).astype(bf16),
                        ],
                        axis=1,
                    )
                )
            weight = qt[source]
            piece = lax.dot_general(
                jnp.concatenate(heads, axis=0), weight, TRANSPOSED, preferred_element_type=f32
            ) + lax.dot_general(
                jnp.concatenate(tails, axis=0), weight, TRANSPOSED, preferred_element_type=f32
            )
            acc[target] = acc[target] + piece
        return carry

    turns = jnp.int32(0)
    for first in range(0, pairs_ref.shape[1], PAIR_STEP):
        turns = turns + jnp.where(pairs_ref[0, first] < blocks, PAIR_STEP // UNROLL, 0)
    lax.fori_loop(0, turns, pair_step, 0)

    def force_step(block, carry):
        first = pl.multiple_of(block * 8, 8)
        tile = gh_ref[pl.ds(first, 8), :]
        sums = jnp.transpose(acc[block])
        sums = sums[0:40] + sums[40:80] + sums[80:120]
        place = [tile[axis : axis + 1] for axis in range(3)]
        dline = [tile[3 + axis : 4 + axis] for axis in range(3)]
        burgers = burgers_of(tile[6:7])
        linear = base_ref[:, pl.ds(pl.multiple_of(block * SEG, SEG), SEG)] + (
            sums[0:8] + place[0] * sums[8:16] + place[1] * sums[16:24] + place[2] * sums[24:32]
        )
        outer = [sums[32 + item : 33 + item] for item in range(8)] + [sums[6:7]]
        lone = [sums[14:15], sums[22:23], sums[30:31]]
        twice = {(a, b): place[a] * place[b] for a in range(3) for b in range(a, 3)}
        sigma = []
        for comp in range(6):
            total = linear[comp : comp + 1]
            if comp != 2:
                curved = 0.0
                for sign, i, axes in CUBICS[comp]:
                    value = lone[i] * place[axes[2]] - outer[3 * i + axes[2]]
                    value = value * twice[tuple(sorted(axes[:2]))]
                    value = value - place[axes[2]] * (
                        outer[3 * i + axes[0]] * place[axes[1]]
                        + outer[3 * i + axes[1]] * place[axes[0]]
                    )
                    curved = curved + sign * value
                sigma.append((total, curved))
            else:
                sigma.append((total, -(sigma[0][1] + sigma[1][1])))
        sigma = [total - curved for total, curved in sigma]
        full = [
            [sigma[0], sigma[3], sigma[4]],
            [sigma[3], sigma[1], sigma[5]],
            [sigma[4], sigma[5], sigma[2]],
        ]
        push = [
            full[row][0] * burgers[0] + full[row][1] * burgers[1] + full[row][2] * burgers[2]
            for row in range(3)
        ]
        force = [
            push[1] * dline[2] - push[2] * dline[1],
            push[2] * dline[0] - push[0] * dline[2],
            push[0] * dline[1] - push[1] * dline[0],
        ]
        length = jnp.sqrt(dline[0] * dline[0] + dline[1] * dline[1] + dline[2] * dline[2])
        out_ref[pl.ds(first, 8), :] = 0.5 * jnp.concatenate(
            force + [length] + sigma[0:4], axis=0
        )
        return carry

    lax.fori_loop(0, blocks, force_step, 0, unroll=8)


def near_call(pairs, ghosts, base):
    blocks = base.shape[1] // SEG
    number = ghosts.shape[0] // 8
    return pl.pallas_call(
        functools.partial(near_kernel, blocks, number),
        out_shape=jax.ShapeDtypeStruct((blocks * 8, SEG), f32),
        in_specs=[
            pl.BlockSpec(memory_space=pltpu.SMEM),
            pl.BlockSpec(memory_space=pltpu.VMEM),
            pl.BlockSpec(memory_space=pltpu.VMEM),
        ],
        out_specs=pl.BlockSpec(memory_space=pltpu.VMEM),
        scratch_shapes=[
            pltpu.VMEM((3 * blocks, SEG, SEG), f32),
            pltpu.VMEM((number, SEG, 2 * SEG), bf16),
            pltpu.VMEM((blocks, SEG, SEG), f32),
        ],
        compiler_params=pltpu.CompilerParams(vmem_limit_bytes=48 * 1024 * 1024),
    )(pairs, ghosts, base)


def wrapped(diff, extent):
    half = extent / 2.0
    return jnp.where(diff > half, diff - extent, jnp.where(diff < -half, diff + extent, diff))


def far_rows(plus, minus, step):
    both = [[plus[3 * i + j] + minus[3 * i + j] for j in range(3)] for i in range(3)]
    odd = [[plus[3 * i + j] - minus[3 * i + j] for j in range(3)] for i in range(3)]

    def curl_of(amat):
        return (amat[1][2] - amat[2][1], amat[2][0] - amat[0][2], amat[0][1] - amat[1][0])

    curl_both = curl_of(both)
    curl_odd = curl_of(odd)
    shear = SHEAR_TERM
    turned = [
        (None, 2.0 * both[2][0], -2.0 * both[1][0]),
        (step * (-2.0 * odd[2][1]), None, 2.0 * both[0][1]),
        (step * (2.0 * odd[1][2]), -2.0 * both[0][2], None),
        (step * -odd[2][0], both[2][1], both[0][0] - both[1][1]),
        (step * odd[1][0], both[2][2] - both[0][0], -both[1][2]),
        (step * (odd[1][1] - odd[2][2]), -both[0][1], both[0][2]),
    ]
    turned = [[None if item is None else shear * item for item in line] for line in turned]
    curls = {
        "ox": BULK_TERM * step * curl_odd[0],
        "oy": BULK_TERM * step * curl_odd[1],
        "oz": BULK_TERM * step * curl_odd[2],
        "bx": BULK_TERM * curl_both[0],
        "by": BULK_TERM * curl_both[1],
        "bz": BULK_TERM * curl_both[2],
        "sx": BULK_TERM * step * step * curl_both[0],
    }
    return turned, curls


def exchange_kernel(
    nx,
    ny,
    off_ref,
    line_ref,
    kind_ref,
    cell_ref,
    applied_ref,
    listx_ref,
    listy_ref,
    gh_ref,
    base_ref,
    products,
    hot,
    pack_x,
    land_x,
    pack_y,
    land_y,
    mine,
    row_land,
    row_block,
    all_land,
    far_acc,
    sem_x,
    sem_y,
    row_send,
    row_recv,
    all_send,
    all_recv,
):
    segs = off_ref.shape[1]
    blocks = segs // SEG
    packet = listx_ref.shape[1]
    cells = hot.shape[0]
    me_x = lax.axis_index("gx")
    me_y = lax.axis_index("gy")
    mesh_ids = pl.DeviceIdType.MESH
    barrier = pltpu.get_barrier_semaphore()

    half_x = nx // 2
    high = me_x // half_x
    spot = me_x % half_x
    column = high * ny + me_y
    depth_count = 2 * ny

    def column_device(step):
        other = lax.rem(column + step, depth_count)
        return (other // ny * half_x + spot, other % ny)

    def plane_device(step):
        return (high * half_x + lax.rem(spot + step, half_x), me_y)

    def greet(device):
        pl.semaphore_signal(barrier, inc=1, device_id=device, device_id_type=mesh_ids)

    def greet_column(step, carry):
        greet(column_device(step))
        return carry

    def greet_plane(step, carry):
        greet(plane_device(step))
        return carry

    lax.fori_loop(1, depth_count, greet_column, 0)
    lax.fori_loop(1, half_x, greet_plane, 0)
    greet((lax.rem(me_x + nx - 1, nx), me_y))
    greet((lax.rem(me_x + 1, nx), me_y))

    cell_iota = lax.broadcasted_iota(jnp.int32, (cells, SEG), 0)
    origin = [0.5 - CENTER[axis] for axis in range(3)]

    def block_step(block, carry):
        lanes = pl.ds(pl.multiple_of(block * SEG, SEG), SEG)
        cell = cell_ref[:, lanes]
        kind = kind_ref[:, lanes]
        dline = line_ref[:, lanes]
        shift = off_ref[:, lanes]
        corner = (cell // (CCY * NCZ), cell // NCZ % CCY, cell % NCZ)
        place = [
            (corner[axis].astype(f32) + origin[axis]) + shift[axis : axis + 1] for axis in range(3)
        ]
        code = kind.astype(f32)
        gh_ref[block] = jnp.concatenate(
            place + [dline, code, jnp.zeros((1, SEG), f32)], axis=0
        )
        burgers = burgers_of(code)
        outer = jnp.concatenate(
            [burgers[0] * dline, burgers[1] * dline, burgers[2] * dline, jnp.zeros((7, SEG), f32)],
            axis=0,
        )
        for part, piece in enumerate(parts_of(outer)):
            products[part * 16 : part * 16 + 16, lanes] = piece.astype(bf16)
        hot[:, lanes] = (cell_iota == cell).astype(f32).astype(bf16)
        return carry

    lax.fori_loop(0, blocks, block_step, 0, unroll=4)

    def pick_x(item, carry):
        for side in range(2):
            source = listx_ref[side, item]
            pack_x[side, item] = gh_ref[source]
        return carry

    lax.fori_loop(0, packet, pick_x, 0, unroll=8)
    moments = lax.dot_general(products[...], hot[...], TRANSPOSED, preferred_element_type=f32)
    moments = moments[0:16] + moments[16:32] + moments[32:48]
    mine[...] = jnp.concatenate([moments, jnp.zeros((16, SEG - cells), f32)], axis=1)
    row_land[column] = mine[...]

    pl.semaphore_wait(barrier, depth_count - 1 + half_x - 1 + 2)

    copies_x = []
    for side in range(2):
        target = lax.rem(me_x + (nx - 1 if side == 0 else 1), nx)
        copies_x.append(
            pltpu.make_async_remote_copy(
                src_ref=pack_x.at[side],
                dst_ref=land_x.at[1 - side],
                send_sem=sem_x.at[side],
                recv_sem=sem_x.at[2 + side],
                device_id=(target, me_y),
                device_id_type=mesh_ids,
            )
        )
    for copy in copies_x:
        copy.start()

    def row_copy(step):
        return pltpu.make_async_remote_copy(
            src_ref=mine,
            dst_ref=row_land.at[column],
            send_sem=row_send.at[step],
            recv_sem=row_recv.at[step],
            device_id=column_device(step),
            device_id_type=mesh_ids,
        )

    def row_start(step, carry):
        row_copy(step).start()
        return carry

    def row_wait(step, carry):
        row_copy(step).wait()
        return carry

    lax.fori_loop(1, depth_count, row_start, 0)

    row_iota = lax.broadcasted_iota(jnp.int32, (8, SEG), 0)
    for copy in copies_x:
        copy.wait()
    for slot in range(2):
        moved = jnp.where(row_iota == 0, -float(CCX) if slot == 0 else float(CCX), 0.0)

        def take_x(item, carry, slot=slot, moved=moved):
            gh_ref[blocks + slot * packet + item] = land_x[slot, item] + moved
            return carry

        lax.fori_loop(0, packet, take_x, 0, unroll=8)

    def pick_y(item, carry):
        for side in range(2):
            source = listy_ref[side, item]
            pack_y[side, item] = gh_ref[source]
        return carry

    lax.fori_loop(0, packet, pick_y, 0, unroll=8)
    copies_y = []
    for side in range(2):
        target = lax.rem(me_y + (ny - 1 if side == 0 else 1), ny)
        copies_y.append(
            pltpu.make_async_remote_copy(
                src_ref=pack_y.at[side],
                dst_ref=land_y.at[1 - side],
                send_sem=sem_y.at[side],
                recv_sem=sem_y.at[2 + side],
                device_id=(me_x, target),
                device_id_type=mesh_ids,
            )
        )
    for copy in copies_y:
        copy.start()

    lax.fori_loop(1, depth_count, row_wait, 0)
    lane_iota = lax.broadcasted_iota(jnp.int32, (16, SEG), 1)
    for part in range(2):
        lasts = []
        for tile in range(4):
            first = row_land[part * ny + 2 * tile]
            second = row_land[part * ny + 2 * tile + 1]
            merged = jnp.where(lane_iota < cells, first, pltpu.roll(second, cells, 1))
            row_block[40 * part + 8 * tile : 40 * part + 8 * tile + 8, :] = merged[0:8]
            lasts.append(merged[8:9])
        row_block[40 * part + 32 : 40 * part + 40, :] = jnp.concatenate(
            lasts + [jnp.zeros((4, SEG), f32)], axis=0
        )
    all_land[spot] = row_block[...]

    def all_copy(step):
        return pltpu.make_async_remote_copy(
            src_ref=row_block,
            dst_ref=all_land.at[spot],
            send_sem=all_send.at[step],
            recv_sem=all_recv.at[step],
            device_id=plane_device(step),
            device_id_type=mesh_ids,
        )

    def all_start(step, carry):
        all_copy(step).start()
        all_copy(half_x - step).start()
        return carry

    def all_sent(step, carry):
        all_copy(step).wait_send()
        return carry

    lax.fori_loop(1, half_x // 2, all_start, 0)
    all_copy(half_x // 2).start()

    for copy in copies_y:
        copy.wait()
    for slot in range(2):
        moved = jnp.where(row_iota == 1, -float(CCY) if slot == 0 else float(CCY), 0.0)

        def take_y(item, carry, slot=slot, moved=moved):
            gh_ref[blocks + (2 + slot) * packet + item] = land_y[slot, item] + moved
            return carry

        lax.fori_loop(0, packet, take_y, 0, unroll=8)

    far_acc[...] = jnp.zeros_like(far_acc)

    lane = lax.broadcasted_iota(jnp.int32, (8, SEG), 1)
    source_z = (lane % NCZ).astype(f32)
    depth = [
        wrapped((row_iota + 8 * half).astype(f32) - source_z, float(NCZ)) for half in range(2)
    ]
    extent_y = float(CCY * ny)

    def far_step(apart, tile):
        step = apart.astype(f32)
        middle = apart == nx // 2
        upper = me_x >= nx // 2
        weight_plus = jnp.where(middle & jnp.logical_not(upper), 0.0, 1.0)
        weight_minus = jnp.where((apart == 0) | (middle & upper), 0.0, 1.0)
        place_plus = lax.rem(me_x - apart + nx, nx)
        place_minus = lax.rem(me_x + apart, nx)
        spot_plus = place_plus % half_x
        spot_minus = place_minus % half_x
        row_plus = place_plus // half_x * 40
        row_minus = place_minus // half_x * 40
        head_plus = (
            all_land[spot_plus, pl.ds(pl.multiple_of(row_plus + tile * 8, 8), 8), :] * weight_plus
        )
        head_minus = (
            all_land[spot_minus, pl.ds(pl.multiple_of(row_minus + tile * 8, 8), 8), :]
            * weight_minus
        )
        plus = [head_plus[item : item + 1] for item in range(8)]
        minus = [head_minus[item : item + 1] for item in range(8)]
        plus.append(all_land[spot_plus, pl.ds(row_plus + 32 + tile, 1), :] * weight_plus)
        minus.append(all_land[spot_minus, pl.ds(row_minus + 32 + tile, 1), :] * weight_minus)
        turned, curls = far_rows(plus, minus, step)
        source_y = (lane // NCZ + tile * 8).astype(f32)
        close = apart <= 1
        for quarter in range(CCY):
            ry = wrapped((me_y * CCY + quarter).astype(f32) - source_y, extent_y)
            plane = (ry * ry + CORE_SQUARE) + step * step
            beside = jnp.logical_and(jnp.abs(ry) <= 1.0, close)
            for half in range(2):
                rz = depth[half]
                inv_one = lax.rsqrt(plane + rz * rz)
                keep = jnp.logical_and(beside, jnp.abs(rz) <= 1.0)
                inv_two = inv_one * inv_one
                inv_three = jnp.where(keep, 0.0, inv_two * inv_one)
                inv_five = inv_three * inv_two
                gain = 2.0 * inv_three + (3.0 * CORE_SQUARE) * inv_five
                dot_both = curls["ox"] + ry * curls["by"] + rz * curls["bz"]
                dot_odd = curls["sx"] + ry * curls["oy"] + rz * curls["oz"]
                trace = (inv_three + (3.0 * CORE_SQUARE) * inv_five) * dot_both
                thrice = 3.0 * inv_five
                wave = thrice * dot_both
                wave_odd = thrice * dot_odd
                wave_y = wave * ry
                bends = (
                    2.0 * curls["ox"],
                    2.0 * (ry * curls["by"]),
                    2.0 * (rz * curls["bz"]),
                    ry * curls["bx"] + curls["oy"],
                    rz * curls["bx"] + curls["oz"],
                    rz * curls["by"] + ry * curls["bz"],
                )
                curved = (
                    wave * (step * step),
                    wave_y * ry,
                    (wave * rz) * rz,
                    wave_odd * ry,
                    wave_odd * rz,
                    wave_y * rz,
                )
                first = 8 * (2 * quarter + half)
                for comp in range(6):
                    swirl = None
                    for factor, item in zip((None, ry, rz), turned[comp]):
                        if item is not None:
                            item = item if factor is None else factor * item
                            swirl = item if swirl is None else swirl + item
                    value = gain * swirl + inv_three * bends[comp] - curved[comp]
                    if comp < 3:
                        value = value - trace
                    far_acc[comp, first : first + 8, :] = far_acc[comp, first : first + 8, :] + value

    def far_own(turn, carry):
        far_step(turn // 4 * half_x, turn % 4)
        return carry

    def far_columns(near_by, carry):
        all_copy(near_by).wait_recv()
        all_copy(half_x - near_by).wait_recv()

        def far_two(turn, inner):
            far_step(jnp.where(turn < 4, near_by, half_x - near_by), turn % 4)
            return inner

        return lax.fori_loop(0, 8, far_two, carry)

    def far_last(turn, carry):
        far_step(jnp.int32(half_x // 2), turn)
        return carry

    lax.fori_loop(0, 8, far_own, 0)
    lax.fori_loop(1, half_x // 2, far_columns, 0)
    all_copy(half_x // 2).wait_recv()
    lax.fori_loop(0, 4, far_last, 0)
    lax.fori_loop(1, half_x, all_sent, 0)

    pick = (
        lax.broadcasted_iota(jnp.int32, (8, 6 * SEG), 1) // SEG
        == lax.broadcasted_iota(jnp.int32, (8, 6 * SEG), 0)
    ).astype(f32)
    far = lax.dot_general(
        pick,
        jnp.concatenate([far_acc[comp] for comp in range(6)], axis=1),
        TRANSPOSED,
        precision=lax.Precision.HIGHEST,
        preferred_element_type=f32,
    )
    far = jnp.concatenate(list(parts_of(far)) + [jnp.zeros((8, cells), f32)], axis=0).astype(bf16)
    outside = jnp.zeros((8, 1), f32)
    comp_iota = lax.broadcasted_iota(jnp.int32, (8, 1), 0)
    for comp in range(6):
        outside = jnp.where(comp_iota == comp, applied_ref[comp], outside)
    width = 8 * SEG

    def base_step(part, carry):
        lanes = pl.ds(pl.multiple_of(part * width, width), width)
        value = jnp.dot(far, hot[:, lanes], preferred_element_type=f32)
        base_ref[:, lanes] = (value[0:8] + value[8:16] + value[16:24]) + outside
        return carry

    lax.fori_loop(0, segs // width, base_step, 0)


def exchange_call(nx, ny, offsets, dline, kind, cell, applied, list_x, list_y):
    segs = offsets.shape[1]
    blocks = segs // SEG
    packet = list_x.shape[1]
    number = blocks + 4 * packet
    cells = CCX * CCY * NCZ
    vmem = pl.BlockSpec(memory_space=pltpu.VMEM)
    smem = pl.BlockSpec(memory_space=pltpu.SMEM)
    return pl.pallas_call(
        functools.partial(exchange_kernel, nx, ny),
        out_shape=(
            jax.ShapeDtypeStruct((number, 8, SEG), f32),
            jax.ShapeDtypeStruct((8, segs), f32),
        ),
        in_specs=[vmem] * 4 + [smem] * 3,
        out_specs=(vmem, vmem),
        scratch_shapes=[
            pltpu.VMEM((48, segs), bf16),
            pltpu.VMEM((cells, segs), bf16),
            pltpu.VMEM((2, packet, 8, SEG), f32),
            pltpu.VMEM((2, packet, 8, SEG), f32),
            pltpu.VMEM((2, packet, 8, SEG), f32),
            pltpu.VMEM((2, packet, 8, SEG), f32),
            pltpu.VMEM((16, SEG), f32),
            pltpu.VMEM((2 * ny, 16, SEG), f32),
            pltpu.VMEM((80, SEG), f32),
            pltpu.VMEM((nx // 2, 80, SEG), f32),
            pltpu.VMEM((6, cells, SEG), f32),
            pltpu.SemaphoreType.DMA((4,)),
            pltpu.SemaphoreType.DMA((4,)),
            pltpu.SemaphoreType.DMA((2 * ny,)),
            pltpu.SemaphoreType.DMA((2 * ny,)),
            pltpu.SemaphoreType.DMA((nx // 2,)),
            pltpu.SemaphoreType.DMA((nx // 2,)),
        ],
        compiler_params=pltpu.CompilerParams(
            collective_id=0, has_side_effects=True, vmem_limit_bytes=32 * 1024 * 1024
        ),
    )(offsets, dline, kind, cell, applied, list_x, list_y)


NODE_COLS = 256
CHUNK = 1024


def nodal_kernel(
    nx,
    ny,
    half_ref,
    node_ref,
    owner_ref,
    drag_ref,
    out_ref,
    column_hot,
    row_hot,
    totals,
    outgoing,
    landing,
    send_sem,
    recv_sem,
):
    segs = node_ref.shape[1]
    rows = drag_ref.shape[1] // NODE_COLS
    me_x = lax.axis_index("gx")
    me_y = lax.axis_index("gy")
    mesh_ids = pl.DeviceIdType.MESH
    beside = (
        (lax.rem(me_x + nx - 1, nx), me_y),
        (lax.rem(me_x + 1, nx), me_y),
        (me_x, lax.rem(me_y + ny - 1, ny)),
        (me_x, lax.rem(me_y + 1, ny)),
    )
    barrier = pltpu.get_barrier_semaphore()
    for device in beside:
        pl.semaphore_signal(barrier, inc=1, device_id=device, device_id_type=mesh_ids)

    column_iota = lax.broadcasted_iota(jnp.int32, (NODE_COLS, SEG), 0)

    def column_step(block, carry):
        lanes = pl.ds(pl.multiple_of(block * SEG, SEG), SEG)
        for end in range(2):
            column = node_ref[end : end + 1, lanes] % NODE_COLS
            where = pl.ds(pl.multiple_of(end * segs + block * SEG, SEG), SEG)
            column_hot[:, where] = (column_iota == column).astype(f32).astype(bf16)
        return carry

    lax.fori_loop(0, segs // SEG, column_step, 0, unroll=2)

    tiles = CHUNK // SEG
    chunks = 2 * segs // CHUNK

    def add_up(first_row, count):
        row_iota = lax.broadcasted_iota(jnp.int32, (count, SEG), 0) + first_row

        def build(buffer, chunk):
            end = chunk // (segs // CHUNK)
            for tile in range(tiles):
                block = chunk % (segs // CHUNK) * tiles + tile
                lanes = pl.ds(pl.multiple_of(block * SEG, SEG), SEG)
                both = owner_ref[:, lanes] * rows + node_ref[:, lanes] // NODE_COLS
                slot = jnp.where(end == 0, both[0:1], both[1:2])
                mask = (row_iota == slot).astype(f32).astype(bf16)
                values = half_ref[pl.ds(pl.multiple_of(block * 8, 8), 8), :]
                heads = values.astype(bf16).astype(f32)
                tails = values - heads
                for item in range(4):
                    for part, piece in enumerate((heads, tails)):
                        spot = (2 * item + part) * count
                        row = jnp.broadcast_to(piece[item : item + 1], (16, SEG)).astype(bf16)
                        row = jnp.concatenate([row] * (count // 16), axis=0)
                        row_hot[buffer, spot : spot + count, tile * SEG : (tile + 1) * SEG] = (
                            mask * row
                        )

        def add_chunk(buffer, chunk):
            where = pl.ds(pl.multiple_of(chunk * CHUNK, CHUNK), CHUNK)
            totals[0 : 8 * count, :] = totals[0 : 8 * count, :] + lax.dot_general(
                row_hot[buffer, 0 : 8 * count, :],
                column_hot[:, where],
                TRANSPOSED,
                preferred_element_type=f32,
            )

        def chunk_step(turn, carry):
            build(1, 2 * turn + 1)
            add_chunk(0, 2 * turn)
            build(0, jnp.minimum(2 * turn + 2, chunks - 1))
            add_chunk(1, 2 * turn + 1)
            return carry

        totals[0 : 8 * count, :] = jnp.zeros((8 * count, NODE_COLS), f32)
        build(0, jnp.int32(0))
        lax.fori_loop(0, chunks // 2, chunk_step, 0)

    add_up(rows, 4 * rows)
    for side in range(4):
        for item in range(4):
            spot = 2 * item * 4 * rows + side * rows
            outgoing[side, item * rows : (item + 1) * rows, :] = (
                totals[spot : spot + rows, :] + totals[spot + 4 * rows : spot + 5 * rows, :]
            )
    pl.semaphore_wait(barrier, 4)
    copies = []
    for side in range(4):
        copies.append(
            pltpu.make_async_remote_copy(
                src_ref=outgoing.at[side],
                dst_ref=landing.at[side],
                send_sem=send_sem.at[side],
                recv_sem=recv_sem.at[side],
                device_id=beside[side],
                device_id_type=mesh_ids,
            )
        )
    for copy in copies:
        copy.start()
    add_up(0, rows)
    for copy in copies:
        copy.wait()
    sums = []
    for item in range(4):
        spot = 2 * item * rows
        value = totals[spot : spot + rows, :] + totals[spot + rows : spot + 2 * rows, :]
        for side in range(4):
            value = value + landing[side, item * rows : (item + 1) * rows, :]
        sums.append(value)
    drag = jnp.concatenate(
        [drag_ref[:, row * NODE_COLS : (row + 1) * NODE_COLS] for row in range(rows)], axis=0
    )
    scale = 1.0 / (drag * (sums[3] + CORE_LENGTH))
    speed = [sums[item] * scale for item in range(3)]
    for row in range(rows):
        out_ref[:, row * NODE_COLS : (row + 1) * NODE_COLS] = jnp.concatenate(
            [piece[row : row + 1] for piece in speed], axis=0
        )


def nodal_call(nx, ny, half, node, owner, drag):
    segs = node.shape[1]
    rows = drag.shape[1] // NODE_COLS
    vmem = pl.BlockSpec(memory_space=pltpu.VMEM)
    return pl.pallas_call(
        functools.partial(nodal_kernel, nx, ny),
        out_shape=jax.ShapeDtypeStruct((3, drag.shape[1]), f32),
        in_specs=[vmem] * 4,
        out_specs=vmem,
        scratch_shapes=[
            pltpu.VMEM((NODE_COLS, 2 * segs), bf16),
            pltpu.VMEM((2, 32 * rows, CHUNK), bf16),
            pltpu.VMEM((32 * rows, NODE_COLS), f32),
            pltpu.VMEM((4, 4 * rows, NODE_COLS), f32),
            pltpu.VMEM((4, 4 * rows, NODE_COLS), f32),
            pltpu.SemaphoreType.DMA((4,)),
            pltpu.SemaphoreType.DMA((4,)),
        ],
        compiler_params=pltpu.CompilerParams(
            collective_id=1, has_side_effects=True, vmem_limit_bytes=48 * 1024 * 1024
        ),
    )(half, node, owner, drag)


def on_device(
    offsets,
    line,
    burgers_kind,
    seg_cell,
    end_node,
    end_owner,
    drag,
    applied,
    pair_list,
    ghost_x_list,
    ghost_y_list,
):
    nx = lax.axis_size("gx")
    ny = lax.axis_size("gy")
    pairs = pair_list[0, 0]
    ghosts, base = exchange_call(
        nx,
        ny,
        offsets[0, 0],
        line[0, 0],
        burgers_kind[0],
        seg_cell[0],
        applied,
        ghost_x_list[0, 0],
        ghost_y_list[0, 0],
    )
    half = near_call(pairs, ghosts.reshape(-1, SEG), base)
    velocity = nodal_call(nx, ny, half, end_node[0, 0], end_owner[0, 0], drag[0])
    return velocity[None, None]


def solution(mesh):
    return jax.shard_map(
        on_device,
        mesh=mesh,
        in_specs=(
            P("gx", "gy", None, None),
            P("gx", "gy", None, None),
            P("gx", "gy", None),
            P("gx", "gy", None),
            P("gx", "gy", None, None),
            P("gx", "gy", None, None),
            P("gx", "gy", None),
            P(),
            P("gx", "gy", None, None),
            P("gx", "gy", None, None),
            P("gx", "gy", None, None),
        ),
        out_specs=P("gx", "gy", None, None),
        check_vma=False,
    )
```

```python
import functools
import math

import jax
import jax.numpy as jnp
from jax import lax
from jax.experimental import pallas as pl
from jax.experimental.pallas import tpu as pltpu
from jax.sharding import PartitionSpec as P

SEG = 128
CCX = 1
CCY = 4
NCZ = 16
CORE_SQUARE = 0.25
SHEAR_TERM = 1.0 / (8.0 * math.pi)
BULK_TERM = 1.0 / (4.0 * math.pi * 0.7)
CORE_LENGTH = 1.0
COMPONENTS = ((0, 0), (1, 1), (2, 2), (0, 1), (0, 2), (1, 2))
CUBICS = (
    ((1.0, 0, (0, 0, 0)), (1.0, 1, (1, 0, 0)), (1.0, 2, (2, 0, 0))),
    ((1.0, 0, (0, 1, 1)), (1.0, 1, (1, 1, 1)), (1.0, 2, (2, 1, 1))),
    (
        (-1.0, 0, (0, 0, 0)),
        (-1.0, 1, (1, 0, 0)),
        (-1.0, 2, (2, 0, 0)),
        (-1.0, 0, (0, 1, 1)),
        (-1.0, 1, (1, 1, 1)),
        (-1.0, 2, (2, 1, 1)),
    ),
    ((1.0, 0, (0, 0, 1)), (1.0, 1, (1, 0, 1)), (1.0, 2, (2, 0, 1))),
    ((1.0, 0, (0, 0, 2)), (1.0, 1, (0, 1, 2)), (-1.0, 2, (0, 0, 0)), (-1.0, 2, (0, 1, 1))),
    ((1.0, 0, (0, 1, 2)), (1.0, 1, (1, 1, 2)), (-1.0, 2, (0, 0, 1)), (-1.0, 2, (1, 1, 1))),
)
CENTER = (CCX / 2.0, CCY / 2.0, NCZ / 2.0)
UNROLL = 64
PAIR_STEP = 256
TRANSPOSED = (((1,), (1,)), ((), ()))
f32 = jnp.float32
bf16 = jnp.bfloat16


def burgers_of(kind):
    code = kind.astype(jnp.int32)
    return [1.0 - 2.0 * ((code >> bit) & 1).astype(f32) for bit in range(3)]


def source_columns(place, dline, kind):
    burgers = burgers_of(kind)
    amat = [[burgers[i] * dline[j] for j in range(3)] for i in range(3)]
    curl = [
        amat[1][2] - amat[2][1],
        amat[2][0] - amat[0][2],
        amat[0][1] - amat[1][0],
    ]
    turned = {
        (0, 0): (None, 2.0 * amat[2][0], -2.0 * amat[1][0]),
        (1, 1): (-2.0 * amat[2][1], None, 2.0 * amat[0][1]),
        (2, 2): (2.0 * amat[1][2], -2.0 * amat[0][2], None),
        (0, 1): (-amat[2][0], amat[2][1], amat[0][0] - amat[1][1]),
        (0, 2): (amat[1][0], amat[2][2] - amat[0][0], -amat[1][2]),
        (1, 2): (amat[1][1] - amat[2][2], -amat[0][1], amat[0][2]),
    }
    bulk3 = 3.0 * BULK_TERM
    curl_k = [BULK_TERM * item for item in curl]
    curl_3k = [bulk3 * item for item in curl]
    pairs = {(a, b): place[a] * place[b] for a in range(3) for b in range(a, 3)}
    single = [[curl_3k[i] * place[a] for a in range(3)] for i in range(3)]
    double = {}

    def doubled(i, a, b):
        key = (i, min(a, b), max(a, b))
        if key not in double:
            double[key] = curl_3k[i] * pairs[key[1:]]
        return double[key]

    columns = []
    for comp, (a, b) in enumerate(COMPONENTS):
        linear5 = [0.0, 0.0, 0.0]
        linear3 = [0.0, 0.0, 0.0]
        const5 = 0.0
        for sign, i, axes in CUBICS[comp]:
            for spot in range(3):
                rest = axes[:spot] + axes[spot + 1 :]
                linear5[axes[spot]] = linear5[axes[spot]] - sign * doubled(i, *rest)
            const5 = const5 + sign * (doubled(i, axes[0], axes[1]) * place[axes[2]])
        for axis in range(3):
            alpha3 = 0.0
            alpha5 = 0.0
            if turned[(a, b)][axis] is not None:
                alpha3 = (2.0 * SHEAR_TERM) * turned[(a, b)][axis]
                alpha5 = (3.0 * CORE_SQUARE * SHEAR_TERM) * turned[(a, b)][axis]
            if axis == b:
                alpha3 = alpha3 + curl_k[a]
            if axis == a:
                alpha3 = alpha3 + curl_k[b]
            if a == b:
                alpha3 = alpha3 - curl_k[axis]
                alpha5 = alpha5 - (3.0 * CORE_SQUARE) * curl_k[axis]
            if (a, b) == (2, 2):
                alpha3 = alpha3 - curl_3k[axis]
                alpha5 = alpha5 + CORE_SQUARE * curl_3k[axis]
            if b == 2 and a == axis and a < 2:
                alpha3 = alpha3 - curl_3k[2]
                alpha5 = alpha5 + CORE_SQUARE * curl_3k[2]
            linear3[axis] = alpha3
            linear5[axis] = linear5[axis] + alpha5
            const5 = const5 - alpha5 * place[axis]
        const3 = -(linear3[0] * place[0] + linear3[1] * place[1] + linear3[2] * place[2])
        columns.append((comp, const3, const5))
        for axis in range(3):
            columns.append((8 * (axis + 1) + comp, linear3[axis], linear5[axis]))
    spots = (32, 33, 34, 35, 36, 37, 38, 39, 6)
    for i in range(3):
        for a in range(3):
            columns.append((spots[3 * i + a], None, single[i][a]))
        columns.append((8 * (i + 1) + 6, None, curl_3k[i]))
    return columns


def parts_of(value):
    head = value.astype(bf16).astype(f32)
    rest = value - head
    middle = rest.astype(bf16).astype(f32)
    return head, middle, rest - middle


def near_kernel(
    blocks, ghosts, pairs_ref, gh_ref, base_ref, out_ref, xb, qt, acc
):
    zero = jnp.zeros((SEG, SEG), f32)
    blank = jnp.zeros((8, SEG), f32)

    def source_step(group, carry):
        first = pl.multiple_of(group * 64, 64)
        rows = [gh_ref[pl.ds(first + row, 8, stride=8), :] for row in range(7)]
        spots3 = [blank] * 40
        spots5 = [blank] * 40
        for spot, term3, term5 in source_columns(rows[0:3], rows[3:6], rows[6]):
            spots5[spot] = term5
            if term3 is not None:
                spots3[spot] = term3
        for half, spots, size in ((0, spots3, 32), (1, spots5, 40)):
            swapped = jnp.transpose(jnp.stack(spots[:size], axis=0), (1, 0, 2))
            for part in range(8):
                pieces = []
                for piece in parts_of(swapped[part]):
                    pieces.append(piece)
                    if size < 40:
                        pieces.append(blank)
                pieces.append(blank)
                qt[group * 8 + part, :, half * SEG : half * SEG + SEG] = jnp.concatenate(
                    pieces, axis=0
                ).astype(bf16)
        return carry

    def target_step(block):
        tile = gh_ref[pl.ds(pl.multiple_of(block * 8, 8), 8), :]
        columns = jnp.transpose(tile)
        for axis in range(3):
            xb[3 * block + axis] = jnp.broadcast_to(columns[:, axis : axis + 1], (SEG, SEG))
        acc[block] = zero

    def both_step(group, carry):
        for part in range(8):
            target_step(group * 8 + part)
        return source_step(group, carry)

    lax.fori_loop(0, blocks // 8, both_step, 0)
    lax.fori_loop(blocks // 8, ghosts // 8, source_step, 0)

    def pair_step(turn, carry):
        for part in range(UNROLL):
            target = pairs_ref[0, turn * UNROLL + part]
            source = pairs_ref[1, turn * UNROLL + part]
            tile = gh_ref[pl.ds(pl.multiple_of(source * 8, 8), 8), :]
            heads = []
            tails = []
            for first in range(0, SEG, 32):
                dx = xb[3 * target, first : first + 32, :] - tile[0:1]
                dy = xb[3 * target + 1, first : first + 32, :] - tile[1:2]
                dz = xb[3 * target + 2, first : first + 32, :] - tile[2:3]
                inv_one = lax.rsqrt((dx * dx + CORE_SQUARE) + dy * dy + dz * dz)
                inv_two = inv_one * inv_one
                inv_three = inv_two * inv_one
                inv_five = inv_three * inv_two
                head3 = inv_three.astype(bf16)
                head5 = inv_five.astype(bf16)
                heads.append(jnp.concatenate([head3, head5], axis=1))
                tails.append(
                    jnp.concatenate(
                        [
                            (inv_three - head3.astype(f32)).astype(bf16),
                            (inv_five - head5.astype(f32)).astype(bf16),
                        ],
                        axis=1,
                    )
                )
            weight = qt[source]
            piece = lax.dot_general(
                jnp.concatenate(heads, axis=0), weight, TRANSPOSED, preferred_element_type=f32
            ) + lax.dot_general(
                jnp.concatenate(tails, axis=0), weight, TRANSPOSED, preferred_element_type=f32
            )
            acc[target] = acc[target] + piece
        return carry

    turns = jnp.int32(0)
    for first in range(0, pairs_ref.shape[1], PAIR_STEP):
        turns = turns + jnp.where(pairs_ref[0, first] < blocks, PAIR_STEP // UNROLL, 0)
    lax.fori_loop(0, turns, pair_step, 0)

    def force_step(block, carry):
        first = pl.multiple_of(block * 8, 8)
        tile = gh_ref[pl.ds(first, 8), :]
        sums = jnp.transpose(acc[block])
        sums = sums[0:40] + sums[40:80] + sums[80:120]
        place = [tile[axis : axis + 1] for axis in range(3)]
        dline = [tile[3 + axis : 4 + axis] for axis in range(3)]
        burgers = burgers_of(tile[6:7])
        linear = base_ref[:, pl.ds(pl.multiple_of(block * SEG, SEG), SEG)] + (
            sums[0:8] + place[0] * sums[8:16] + place[1] * sums[16:24] + place[2] * sums[24:32]
        )
        outer = [sums[32 + item : 33 + item] for item in range(8)] + [sums[6:7]]
        lone = [sums[14:15], sums[22:23], sums[30:31]]
        twice = {(a, b): place[a] * place[b] for a in range(3) for b in range(a, 3)}
        sigma = []
        for comp in range(6):
            total = linear[comp : comp + 1]
            if comp != 2:
                curved = 0.0
                for sign, i, axes in CUBICS[comp]:
                    value = lone[i] * place[axes[2]] - outer[3 * i + axes[2]]
                    value = value * twice[tuple(sorted(axes[:2]))]
                    value = value - place[axes[2]] * (
                        outer[3 * i + axes[0]] * place[axes[1]]
                        + outer[3 * i + axes[1]] * place[axes[0]]
                    )
                    curved = curved + sign * value
                sigma.append((total, curved))
            else:
                sigma.append((total, -(sigma[0][1] + sigma[1][1])))
        sigma = [total - curved for total, curved in sigma]
        full = [
            [sigma[0], sigma[3], sigma[4]],
            [sigma[3], sigma[1], sigma[5]],
            [sigma[4], sigma[5], sigma[2]],
        ]
        push = [
            full[row][0] * burgers[0] + full[row][1] * burgers[1] + full[row][2] * burgers[2]
            for row in range(3)
        ]
        force = [
            push[1] * dline[2] - push[2] * dline[1],
            push[2] * dline[0] - push[0] * dline[2],
            push[0] * dline[1] - push[1] * dline[0],
        ]
        length = jnp.sqrt(dline[0] * dline[0] + dline[1] * dline[1] + dline[2] * dline[2])
        out_ref[pl.ds(first, 8), :] = 0.5 * jnp.concatenate(
            force + [length] + sigma[0:4], axis=0
        )
        return carry

    lax.fori_loop(0, blocks, force_step, 0, unroll=8)


def near_call(pairs, ghosts, base):
    blocks = base.shape[1] // SEG
    number = ghosts.shape[0] // 8
    return pl.pallas_call(
        functools.partial(near_kernel, blocks, number),
        out_shape=jax.ShapeDtypeStruct((blocks * 8, SEG), f32),
        in_specs=[
            pl.BlockSpec(memory_space=pltpu.SMEM),
            pl.BlockSpec(memory_space=pltpu.VMEM),
            pl.BlockSpec(memory_space=pltpu.VMEM),
        ],
        out_specs=pl.BlockSpec(memory_space=pltpu.VMEM),
        scratch_shapes=[
            pltpu.VMEM((3 * blocks, SEG, SEG), f32),
            pltpu.VMEM((number, SEG, 2 * SEG), bf16),
            pltpu.VMEM((blocks, SEG, SEG), f32),
        ],
        compiler_params=pltpu.CompilerParams(vmem_limit_bytes=48 * 1024 * 1024),
    )(pairs, ghosts, base)


def wrapped(diff, extent):
    half = extent / 2.0
    return jnp.where(diff > half, diff - extent, jnp.where(diff < -half, diff + extent, diff))


def far_rows(plus, minus, step):
    both = [[plus[3 * i + j] + minus[3 * i + j] for j in range(3)] for i in range(3)]
    odd = [[plus[3 * i + j] - minus[3 * i + j] for j in range(3)] for i in range(3)]

    def curl_of(amat):
        return (amat[1][2] - amat[2][1], amat[2][0] - amat[0][2], amat[0][1] - amat[1][0])

    curl_both = curl_of(both)
    curl_odd = curl_of(odd)
    shear = SHEAR_TERM
    turned = [
        (None, 2.0 * both[2][0], -2.0 * both[1][0]),
        (step * (-2.0 * odd[2][1]), None, 2.0 * both[0][1]),
        (step * (2.0 * odd[1][2]), -2.0 * both[0][2], None),
        (step * -odd[2][0], both[2][1], both[0][0] - both[1][1]),
        (step * odd[1][0], both[2][2] - both[0][0], -both[1][2]),
        (step * (odd[1][1] - odd[2][2]), -both[0][1], both[0][2]),
    ]
    turned = [[None if item is None else shear * item for item in line] for line in turned]
    curls = {
        "ox": BULK_TERM * step * curl_odd[0],
        "oy": BULK_TERM * step * curl_odd[1],
        "oz": BULK_TERM * step * curl_odd[2],
        "bx": BULK_TERM * curl_both[0],
        "by": BULK_TERM * curl_both[1],
        "bz": BULK_TERM * curl_both[2],
        "sx": BULK_TERM * step * step * curl_both[0],
    }
    return turned, curls


def exchange_kernel(
    nx,
    ny,
    off_ref,
    line_ref,
    kind_ref,
    cell_ref,
    applied_ref,
    listx_ref,
    listy_ref,
    gh_ref,
    base_ref,
    products,
    hot,
    pack_x,
    land_x,
    pack_y,
    land_y,
    mine,
    row_land,
    row_block,
    all_land,
    far_acc,
    sem_x,
    sem_y,
    row_send,
    row_recv,
    all_send,
    all_recv,
):
    segs = cell_ref.shape[1]
    blocks = segs // SEG
    packet = listx_ref.shape[1]
    cells = hot.shape[0]
    me_x = lax.axis_index("gx")
    me_y = lax.axis_index("gy")
    mesh_ids = pl.DeviceIdType.MESH
    barrier = pltpu.get_barrier_semaphore()

    half_x = nx // 2
    high = me_x // half_x
    spot = me_x % half_x
    column = high * ny + me_y
    depth_count = 2 * ny

    def column_device(step):
        other = lax.rem(column + step, depth_count)
        return (other // ny * half_x + spot, other % ny)

    def plane_device(step):
        return (high * half_x + lax.rem(spot + step, half_x), me_y)

    def greet(device):
        pl.semaphore_signal(barrier, inc=1, device_id=device, device_id_type=mesh_ids)

    def greet_column(step, carry):
        greet(column_device(step))
        return carry

    def greet_plane(step, carry):
        greet(plane_device(step))
        return carry

    lax.fori_loop(1, depth_count, greet_column, 0)
    lax.fori_loop(1, half_x, greet_plane, 0)
    greet((lax.rem(me_x + nx - 1, nx), me_y))
    greet((lax.rem(me_x + 1, nx), me_y))

    cell_iota = lax.broadcasted_iota(jnp.int32, (cells, SEG), 0)
    origin = [0.5 - CENTER[axis] for axis in range(3)]

    def block_step(block, carry):
        lanes = pl.ds(pl.multiple_of(block * SEG, SEG), SEG)
        cell = cell_ref[:, lanes]
        kind = kind_ref[:, lanes]
        spots = [
            pl.ds(pl.multiple_of(axis * segs + block * SEG, SEG), SEG) for axis in range(3)
        ]
        dline = jnp.concatenate([line_ref[:, where] for where in spots], axis=0)
        corner = (cell // (CCY * NCZ), cell // NCZ % CCY, cell % NCZ)
        place = [
            (corner[axis].astype(f32) + origin[axis]) + off_ref[:, spots[axis]]
            for axis in range(3)
        ]
        code = kind.astype(f32)
        gh_ref[block] = jnp.concatenate(
            place + [dline, code, jnp.zeros((1, SEG), f32)], axis=0
        )
        burgers = burgers_of(code)
        outer = jnp.concatenate(
            [burgers[0] * dline, burgers[1] * dline, burgers[2] * dline, jnp.zeros((7, SEG), f32)],
            axis=0,
        )
        for part, piece in enumerate(parts_of(outer)):
            products[part * 16 : part * 16 + 16, lanes] = piece.astype(bf16)
        hot[:, lanes] = (cell_iota == cell).astype(f32).astype(bf16)
        return carry

    lax.fori_loop(0, blocks, block_step, 0, unroll=4)

    def pick_x(item, carry):
        for side in range(2):
            source = listx_ref[side, item]
            pack_x[side, item] = gh_ref[source]
        return carry

    lax.fori_loop(0, packet, pick_x, 0, unroll=8)
    moments = lax.dot_general(products[...], hot[...], TRANSPOSED, preferred_element_type=f32)
    moments = moments[0:16] + moments[16:32] + moments[32:48]
    mine[...] = jnp.concatenate([moments, jnp.zeros((16, SEG - cells), f32)], axis=1)
    row_land[column] = mine[...]

    pl.semaphore_wait(barrier, depth_count - 1 + half_x - 1 + 2)

    copies_x = []
    for side in range(2):
        target = lax.rem(me_x + (nx - 1 if side == 0 else 1), nx)
        copies_x.append(
            pltpu.make_async_remote_copy(
                src_ref=pack_x.at[side],
                dst_ref=land_x.at[1 - side],
                send_sem=sem_x.at[side],
                recv_sem=sem_x.at[2 + side],
                device_id=(target, me_y),
                device_id_type=mesh_ids,
            )
        )
    def row_copy(step):
        return pltpu.make_async_remote_copy(
            src_ref=mine,
            dst_ref=row_land.at[column],
            send_sem=row_send.at[step],
            recv_sem=row_recv.at[step],
            device_id=column_device(step),
            device_id_type=mesh_ids,
        )

    def row_start(step, carry):
        row_copy(step).start()
        return carry

    def row_wait(step, carry):
        row_copy(step).wait()
        return carry

    lax.fori_loop(1, depth_count, row_start, 0)
    for copy in copies_x:
        copy.start()

    row_iota = lax.broadcasted_iota(jnp.int32, (8, SEG), 0)

    lax.fori_loop(1, depth_count, row_wait, 0)
    lane_iota = lax.broadcasted_iota(jnp.int32, (16, SEG), 1)
    for part in range(2):
        lasts = []
        for tile in range(4):
            first = row_land[part * ny + 2 * tile]
            second = row_land[part * ny + 2 * tile + 1]
            merged = jnp.where(lane_iota < cells, first, pltpu.roll(second, cells, 1))
            row_block[40 * part + 8 * tile : 40 * part + 8 * tile + 8, :] = merged[0:8]
            lasts.append(merged[8:9])
        row_block[40 * part + 32 : 40 * part + 40, :] = jnp.concatenate(
            lasts + [jnp.zeros((4, SEG), f32)], axis=0
        )
    all_land[spot] = row_block[...]

    def all_copy(step):
        return pltpu.make_async_remote_copy(
            src_ref=row_block,
            dst_ref=all_land.at[spot],
            send_sem=all_send.at[step],
            recv_sem=all_recv.at[step],
            device_id=plane_device(step),
            device_id_type=mesh_ids,
        )

    def all_start(step, carry):
        all_copy(step).start()
        all_copy(half_x - step).start()
        return carry

    def all_sent(step, carry):
        all_copy(step).wait_send()
        return carry

    lax.fori_loop(1, half_x // 2, all_start, 0)
    all_copy(half_x // 2).start()

    far_acc[...] = jnp.zeros_like(far_acc)

    lane = lax.broadcasted_iota(jnp.int32, (8, SEG), 1)
    source_z = (lane % NCZ).astype(f32)
    depth = [
        wrapped((row_iota + 8 * half).astype(f32) - source_z, float(NCZ)) for half in range(2)
    ]
    extent_y = float(CCY * ny)

    def far_step(apart, tile):
        step = apart.astype(f32)
        middle = apart == nx // 2
        upper = me_x >= nx // 2
        weight_plus = jnp.where(middle & jnp.logical_not(upper), 0.0, 1.0)
        weight_minus = jnp.where((apart == 0) | (middle & upper), 0.0, 1.0)
        place_plus = lax.rem(me_x - apart + nx, nx)
        place_minus = lax.rem(me_x + apart, nx)
        spot_plus = place_plus % half_x
        spot_minus = place_minus % half_x
        row_plus = place_plus // half_x * 40
        row_minus = place_minus // half_x * 40
        head_plus = (
            all_land[spot_plus, pl.ds(pl.multiple_of(row_plus + tile * 8, 8), 8), :] * weight_plus
        )
        head_minus = (
            all_land[spot_minus, pl.ds(pl.multiple_of(row_minus + tile * 8, 8), 8), :]
            * weight_minus
        )
        plus = [head_plus[item : item + 1] for item in range(8)]
        minus = [head_minus[item : item + 1] for item in range(8)]
        plus.append(all_land[spot_plus, pl.ds(row_plus + 32 + tile, 1), :] * weight_plus)
        minus.append(all_land[spot_minus, pl.ds(row_minus + 32 + tile, 1), :] * weight_minus)
        turned, curls = far_rows(plus, minus, step)
        source_y = (lane // NCZ + tile * 8).astype(f32)
        close = apart <= 1
        for quarter in range(CCY):
            ry = wrapped((me_y * CCY + quarter).astype(f32) - source_y, extent_y)
            plane = (ry * ry + CORE_SQUARE) + step * step
            beside = jnp.logical_and(jnp.abs(ry) <= 1.0, close)
            for half in range(2):
                rz = depth[half]
                inv_one = lax.rsqrt(plane + rz * rz)
                keep = jnp.logical_and(beside, jnp.abs(rz) <= 1.0)
                inv_two = inv_one * inv_one
                inv_three = jnp.where(keep, 0.0, inv_two * inv_one)
                inv_five = inv_three * inv_two
                gain = 2.0 * inv_three + (3.0 * CORE_SQUARE) * inv_five
                dot_both = curls["ox"] + ry * curls["by"] + rz * curls["bz"]
                dot_odd = curls["sx"] + ry * curls["oy"] + rz * curls["oz"]
                trace = (inv_three + (3.0 * CORE_SQUARE) * inv_five) * dot_both
                thrice = 3.0 * inv_five
                wave = thrice * dot_both
                wave_odd = thrice * dot_odd
                wave_y = wave * ry
                bends = (
                    2.0 * curls["ox"],
                    2.0 * (ry * curls["by"]),
                    2.0 * (rz * curls["bz"]),
                    ry * curls["bx"] + curls["oy"],
                    rz * curls["bx"] + curls["oz"],
                    rz * curls["by"] + ry * curls["bz"],
                )
                curved = (
                    wave * (step * step),
                    wave_y * ry,
                    (wave * rz) * rz,
                    wave_odd * ry,
                    wave_odd * rz,
                    wave_y * rz,
                )
                first = 8 * (2 * quarter + half)
                for comp in range(6):
                    swirl = None
                    for factor, item in zip((None, ry, rz), turned[comp]):
                        if item is not None:
                            item = item if factor is None else factor * item
                            swirl = item if swirl is None else swirl + item
                    value = gain * swirl + inv_three * bends[comp] - curved[comp]
                    if comp < 3:
                        value = value - trace
                    far_acc[comp, first : first + 8, :] = far_acc[comp, first : first + 8, :] + value

    def far_own(turn, carry):
        far_step(turn // 4 * half_x, turn % 4)
        return carry

    def far_columns(near_by, carry):
        all_copy(near_by).wait_recv()
        all_copy(half_x - near_by).wait_recv()

        def far_two(turn, inner):
            far_step(jnp.where(turn < 4, near_by, half_x - near_by), turn % 4)
            return inner

        return lax.fori_loop(0, 8, far_two, carry)

    def far_last(turn, carry):
        far_step(jnp.int32(half_x // 2), turn)
        return carry

    lax.fori_loop(0, 8, far_own, 0)

    for copy in copies_x:
        copy.wait()
    for slot in range(2):
        moved = jnp.where(row_iota == 0, -float(CCX) if slot == 0 else float(CCX), 0.0)

        def take_x(item, carry, slot=slot, moved=moved):
            gh_ref[blocks + slot * packet + item] = land_x[slot, item] + moved
            return carry

        lax.fori_loop(0, packet, take_x, 0, unroll=8)

    def pick_y(item, carry):
        for side in range(2):
            source = listy_ref[side, item]
            pack_y[side, item] = gh_ref[source]
        return carry

    lax.fori_loop(0, packet, pick_y, 0, unroll=8)
    copies_y = []
    for side in range(2):
        target = lax.rem(me_y + (ny - 1 if side == 0 else 1), ny)
        copies_y.append(
            pltpu.make_async_remote_copy(
                src_ref=pack_y.at[side],
                dst_ref=land_y.at[1 - side],
                send_sem=sem_y.at[side],
                recv_sem=sem_y.at[2 + side],
                device_id=(me_x, target),
                device_id_type=mesh_ids,
            )
        )
    for copy in copies_y:
        copy.start()


    lax.fori_loop(1, half_x // 2, far_columns, 0)
    all_copy(half_x // 2).wait_recv()
    lax.fori_loop(0, 4, far_last, 0)
    lax.fori_loop(1, half_x, all_sent, 0)

    pick = (
        lax.broadcasted_iota(jnp.int32, (8, 6 * SEG), 1) // SEG
        == lax.broadcasted_iota(jnp.int32, (8, 6 * SEG), 0)
    ).astype(f32)
    far = lax.dot_general(
        pick,
        jnp.concatenate([far_acc[comp] for comp in range(6)], axis=1),
        TRANSPOSED,
        precision=lax.Precision.HIGHEST,
        preferred_element_type=f32,
    )
    far = jnp.concatenate(list(parts_of(far)) + [jnp.zeros((8, cells), f32)], axis=0).astype(bf16)
    outside = jnp.zeros((8, 1), f32)
    comp_iota = lax.broadcasted_iota(jnp.int32, (8, 1), 0)
    for comp in range(6):
        outside = jnp.where(comp_iota == comp, applied_ref[comp], outside)
    width = 8 * SEG

    def base_step(part, carry):
        lanes = pl.ds(pl.multiple_of(part * width, width), width)
        value = jnp.dot(far, hot[:, lanes], preferred_element_type=f32)
        base_ref[:, lanes] = (value[0:8] + value[8:16] + value[16:24]) + outside
        return carry

    lax.fori_loop(0, segs // width, base_step, 0)

    for copy in copies_y:
        copy.wait()
    for slot in range(2):
        moved = jnp.where(row_iota == 1, -float(CCY) if slot == 0 else float(CCY), 0.0)

        def take_y(item, carry, slot=slot, moved=moved):
            gh_ref[blocks + (2 + slot) * packet + item] = land_y[slot, item] + moved
            return carry

        lax.fori_loop(0, packet, take_y, 0, unroll=8)


def exchange_call(nx, ny, offsets, dline, kind, cell, applied, list_x, list_y):
    segs = cell.shape[1]
    blocks = segs // SEG
    packet = list_x.shape[1]
    number = blocks + 4 * packet
    cells = CCX * CCY * NCZ
    vmem = pl.BlockSpec(memory_space=pltpu.VMEM)
    smem = pl.BlockSpec(memory_space=pltpu.SMEM)
    return pl.pallas_call(
        functools.partial(exchange_kernel, nx, ny),
        out_shape=(
            jax.ShapeDtypeStruct((number, 8, SEG), f32),
            jax.ShapeDtypeStruct((8, segs), f32),
        ),
        in_specs=[vmem] * 4 + [smem] * 3,
        out_specs=(vmem, vmem),
        scratch_shapes=[
            pltpu.VMEM((48, segs), bf16),
            pltpu.VMEM((cells, segs), bf16),
            pltpu.VMEM((2, packet, 8, SEG), f32),
            pltpu.VMEM((2, packet, 8, SEG), f32),
            pltpu.VMEM((2, packet, 8, SEG), f32),
            pltpu.VMEM((2, packet, 8, SEG), f32),
            pltpu.VMEM((16, SEG), f32),
            pltpu.VMEM((2 * ny, 16, SEG), f32),
            pltpu.VMEM((80, SEG), f32),
            pltpu.VMEM((nx // 2, 80, SEG), f32),
            pltpu.VMEM((6, cells, SEG), f32),
            pltpu.SemaphoreType.DMA((4,)),
            pltpu.SemaphoreType.DMA((4,)),
            pltpu.SemaphoreType.DMA((2 * ny,)),
            pltpu.SemaphoreType.DMA((2 * ny,)),
            pltpu.SemaphoreType.DMA((nx // 2,)),
            pltpu.SemaphoreType.DMA((nx // 2,)),
        ],
        compiler_params=pltpu.CompilerParams(
            collective_id=0, has_side_effects=True, vmem_limit_bytes=32 * 1024 * 1024
        ),
    )(offsets, dline, kind, cell, applied, list_x, list_y)


NODE_COLS = 256
CHUNK = 1024


def nodal_kernel(
    nx,
    ny,
    half_ref,
    node_ref,
    owner_ref,
    drag_ref,
    out_ref,
    column_hot,
    row_hot,
    totals,
    outgoing,
    landing,
    send_sem,
    recv_sem,
):
    segs = node_ref.shape[1]
    rows = drag_ref.shape[1] // NODE_COLS
    me_x = lax.axis_index("gx")
    me_y = lax.axis_index("gy")
    mesh_ids = pl.DeviceIdType.MESH
    beside = (
        (lax.rem(me_x + nx - 1, nx), me_y),
        (lax.rem(me_x + 1, nx), me_y),
        (me_x, lax.rem(me_y + ny - 1, ny)),
        (me_x, lax.rem(me_y + 1, ny)),
    )
    barrier = pltpu.get_barrier_semaphore()
    for device in beside:
        pl.semaphore_signal(barrier, inc=1, device_id=device, device_id_type=mesh_ids)

    column_iota = lax.broadcasted_iota(jnp.int32, (NODE_COLS, SEG), 0)

    def column_step(block, carry):
        lanes = pl.ds(pl.multiple_of(block * SEG, SEG), SEG)
        for end in range(2):
            column = node_ref[end : end + 1, lanes] % NODE_COLS
            where = pl.ds(pl.multiple_of(end * segs + block * SEG, SEG), SEG)
            column_hot[:, where] = (column_iota == column).astype(f32).astype(bf16)
        return carry

    lax.fori_loop(0, segs // SEG, column_step, 0, unroll=2)

    tiles = CHUNK // SEG
    chunks = 2 * segs // CHUNK

    def add_up(first_row, count):
        row_iota = lax.broadcasted_iota(jnp.int32, (count, SEG), 0) + first_row

        def build(buffer, chunk):
            end = chunk // (segs // CHUNK)
            for tile in range(tiles):
                block = chunk % (segs // CHUNK) * tiles + tile
                lanes = pl.ds(pl.multiple_of(block * SEG, SEG), SEG)
                both = owner_ref[:, lanes] * rows + node_ref[:, lanes] // NODE_COLS
                slot = jnp.where(end == 0, both[0:1], both[1:2])
                mask = (row_iota == slot).astype(f32).astype(bf16)
                values = half_ref[pl.ds(pl.multiple_of(block * 8, 8), 8), :]
                heads = values.astype(bf16).astype(f32)
                tails = values - heads
                for item in range(4):
                    for part, piece in enumerate((heads, tails)):
                        spot = (2 * item + part) * count
                        row = jnp.broadcast_to(piece[item : item + 1], (16, SEG)).astype(bf16)
                        row = jnp.concatenate([row] * (count // 16), axis=0)
                        row_hot[buffer, spot : spot + count, tile * SEG : (tile + 1) * SEG] = (
                            mask * row
                        )

        def add_chunk(buffer, chunk):
            where = pl.ds(pl.multiple_of(chunk * CHUNK, CHUNK), CHUNK)
            totals[0 : 8 * count, :] = totals[0 : 8 * count, :] + lax.dot_general(
                row_hot[buffer, 0 : 8 * count, :],
                column_hot[:, where],
                TRANSPOSED,
                preferred_element_type=f32,
            )

        def chunk_step(turn, carry):
            build(1, 2 * turn + 1)
            add_chunk(0, 2 * turn)
            build(0, jnp.minimum(2 * turn + 2, chunks - 1))
            add_chunk(1, 2 * turn + 1)
            return carry

        totals[0 : 8 * count, :] = jnp.zeros((8 * count, NODE_COLS), f32)
        build(0, jnp.int32(0))
        lax.fori_loop(0, chunks // 2, chunk_step, 0)

    add_up(rows, 4 * rows)
    for side in range(4):
        for item in range(4):
            spot = 2 * item * 4 * rows + side * rows
            outgoing[side, item * rows : (item + 1) * rows, :] = (
                totals[spot : spot + rows, :] + totals[spot + 4 * rows : spot + 5 * rows, :]
            )
    pl.semaphore_wait(barrier, 4)
    copies = []
    for side in range(4):
        copies.append(
            pltpu.make_async_remote_copy(
                src_ref=outgoing.at[side],
                dst_ref=landing.at[side],
                send_sem=send_sem.at[side],
                recv_sem=recv_sem.at[side],
                device_id=beside[side],
                device_id_type=mesh_ids,
            )
        )
    for copy in copies:
        copy.start()
    add_up(0, rows)
    for copy in copies:
        copy.wait()
    sums = []
    for item in range(4):
        spot = 2 * item * rows
        value = totals[spot : spot + rows, :] + totals[spot + rows : spot + 2 * rows, :]
        for side in range(4):
            value = value + landing[side, item * rows : (item + 1) * rows, :]
        sums.append(value)
    drag = jnp.concatenate(
        [drag_ref[:, row * NODE_COLS : (row + 1) * NODE_COLS] for row in range(rows)], axis=0
    )
    scale = 1.0 / (drag * (sums[3] + CORE_LENGTH))
    speed = [sums[item] * scale for item in range(3)]
    for item in range(3):
        for row in range(rows):
            first = (item * rows + row) * NODE_COLS
            out_ref[:, first : first + NODE_COLS] = speed[item][row : row + 1]


def nodal_call(nx, ny, half, node, owner, drag):
    segs = node.shape[1]
    rows = drag.shape[1] // NODE_COLS
    vmem = pl.BlockSpec(memory_space=pltpu.VMEM)
    return pl.pallas_call(
        functools.partial(nodal_kernel, nx, ny),
        out_shape=jax.ShapeDtypeStruct((1, 3 * drag.shape[1]), f32),
        in_specs=[vmem] * 4,
        out_specs=vmem,
        scratch_shapes=[
            pltpu.VMEM((NODE_COLS, 2 * segs), bf16),
            pltpu.VMEM((2, 32 * rows, CHUNK), bf16),
            pltpu.VMEM((32 * rows, NODE_COLS), f32),
            pltpu.VMEM((4, 4 * rows, NODE_COLS), f32),
            pltpu.VMEM((4, 4 * rows, NODE_COLS), f32),
            pltpu.SemaphoreType.DMA((4,)),
            pltpu.SemaphoreType.DMA((4,)),
        ],
        compiler_params=pltpu.CompilerParams(
            collective_id=1, has_side_effects=True, vmem_limit_bytes=48 * 1024 * 1024
        ),
    )(half, node, owner, drag)


def on_device(
    offsets,
    line,
    burgers_kind,
    seg_cell,
    end_node,
    end_owner,
    drag,
    applied,
    pair_list,
    ghost_x_list,
    ghost_y_list,
):
    nx = lax.axis_size("gx")
    ny = lax.axis_size("gy")
    pairs = pair_list[0, 0]
    ghosts, base = exchange_call(
        nx,
        ny,
        offsets.reshape(1, -1),
        line.reshape(1, -1),
        burgers_kind[0],
        seg_cell[0],
        applied,
        ghost_x_list[0, 0],
        ghost_y_list[0, 0],
    )
    half = near_call(pairs, ghosts.reshape(-1, SEG), base)
    velocity = nodal_call(nx, ny, half, end_node[0, 0], end_owner[0, 0], drag[0])
    return velocity.reshape(1, 1, 3, -1)


def solution(mesh):
    return jax.shard_map(
        on_device,
        mesh=mesh,
        in_specs=(
            P("gx", "gy", None, None),
            P("gx", "gy", None, None),
            P("gx", "gy", None),
            P("gx", "gy", None),
            P("gx", "gy", None, None),
            P("gx", "gy", None, None),
            P("gx", "gy", None),
            P(),
            P("gx", "gy", None, None),
            P("gx", "gy", None, None),
            P("gx", "gy", None, None),
        ),
        out_specs=P("gx", "gy", None, None),
        check_vma=False,
    )
```

```python
import functools
import math

import jax
import jax.numpy as jnp
from jax import lax
from jax.experimental import pallas as pl
from jax.experimental.pallas import tpu as pltpu
from jax.sharding import PartitionSpec as P

SEG = 128
CCX = 1
CCY = 4
NCZ = 16
CORE_SQUARE = 0.25
SHEAR_TERM = 1.0 / (8.0 * math.pi)
BULK_TERM = 1.0 / (4.0 * math.pi * 0.7)
CORE_LENGTH = 1.0
COMPONENTS = ((0, 0), (1, 1), (2, 2), (0, 1), (0, 2), (1, 2))
CUBICS = (
    ((1.0, 0, (0, 0, 0)), (1.0, 1, (1, 0, 0)), (1.0, 2, (2, 0, 0))),
    ((1.0, 0, (0, 1, 1)), (1.0, 1, (1, 1, 1)), (1.0, 2, (2, 1, 1))),
    (
        (-1.0, 0, (0, 0, 0)),
        (-1.0, 1, (1, 0, 0)),
        (-1.0, 2, (2, 0, 0)),
        (-1.0, 0, (0, 1, 1)),
        (-1.0, 1, (1, 1, 1)),
        (-1.0, 2, (2, 1, 1)),
    ),
    ((1.0, 0, (0, 0, 1)), (1.0, 1, (1, 0, 1)), (1.0, 2, (2, 0, 1))),
    ((1.0, 0, (0, 0, 2)), (1.0, 1, (0, 1, 2)), (-1.0, 2, (0, 0, 0)), (-1.0, 2, (0, 1, 1))),
    ((1.0, 0, (0, 1, 2)), (1.0, 1, (1, 1, 2)), (-1.0, 2, (0, 0, 1)), (-1.0, 2, (1, 1, 1))),
)
CENTER = (CCX / 2.0, CCY / 2.0, NCZ / 2.0)
UNROLL = 64
PAIR_STEP = 256
TRANSPOSED = (((1,), (1,)), ((), ()))
f32 = jnp.float32
bf16 = jnp.bfloat16


def burgers_of(kind):
    code = kind.astype(jnp.int32)
    return [1.0 - 2.0 * ((code >> bit) & 1).astype(f32) for bit in range(3)]


def source_columns(place, dline, kind):
    burgers = burgers_of(kind)
    amat = [[burgers[i] * dline[j] for j in range(3)] for i in range(3)]
    curl = [
        amat[1][2] - amat[2][1],
        amat[2][0] - amat[0][2],
        amat[0][1] - amat[1][0],
    ]
    turned = {
        (0, 0): (None, 2.0 * amat[2][0], -2.0 * amat[1][0]),
        (1, 1): (-2.0 * amat[2][1], None, 2.0 * amat[0][1]),
        (2, 2): (2.0 * amat[1][2], -2.0 * amat[0][2], None),
        (0, 1): (-amat[2][0], amat[2][1], amat[0][0] - amat[1][1]),
        (0, 2): (amat[1][0], amat[2][2] - amat[0][0], -amat[1][2]),
        (1, 2): (amat[1][1] - amat[2][2], -amat[0][1], amat[0][2]),
    }
    bulk3 = 3.0 * BULK_TERM
    curl_k = [BULK_TERM * item for item in curl]
    curl_3k = [bulk3 * item for item in curl]
    pairs = {(a, b): place[a] * place[b] for a in range(3) for b in range(a, 3)}
    single = [[curl_3k[i] * place[a] for a in range(3)] for i in range(3)]
    double = {}

    def doubled(i, a, b):
        key = (i, min(a, b), max(a, b))
        if key not in double:
            double[key] = curl_3k[i] * pairs[key[1:]]
        return double[key]

    columns = []
    for comp, (a, b) in enumerate(COMPONENTS):
        linear5 = [0.0, 0.0, 0.0]
        linear3 = [0.0, 0.0, 0.0]
        const5 = 0.0
        for sign, i, axes in CUBICS[comp]:
            for spot in range(3):
                rest = axes[:spot] + axes[spot + 1 :]
                linear5[axes[spot]] = linear5[axes[spot]] - sign * doubled(i, *rest)
            const5 = const5 + sign * (doubled(i, axes[0], axes[1]) * place[axes[2]])
        for axis in range(3):
            alpha3 = 0.0
            alpha5 = 0.0
            if turned[(a, b)][axis] is not None:
                alpha3 = (2.0 * SHEAR_TERM) * turned[(a, b)][axis]
                alpha5 = (3.0 * CORE_SQUARE * SHEAR_TERM) * turned[(a, b)][axis]
            if axis == b:
                alpha3 = alpha3 + curl_k[a]
            if axis == a:
                alpha3 = alpha3 + curl_k[b]
            if a == b:
                alpha3 = alpha3 - curl_k[axis]
                alpha5 = alpha5 - (3.0 * CORE_SQUARE) * curl_k[axis]
            if (a, b) == (2, 2):
                alpha3 = alpha3 - curl_3k[axis]
                alpha5 = alpha5 + CORE_SQUARE * curl_3k[axis]
            if b == 2 and a == axis and a < 2:
                alpha3 = alpha3 - curl_3k[2]
                alpha5 = alpha5 + CORE_SQUARE * curl_3k[2]
            linear3[axis] = alpha3
            linear5[axis] = linear5[axis] + alpha5
            const5 = const5 - alpha5 * place[axis]
        const3 = -(linear3[0] * place[0] + linear3[1] * place[1] + linear3[2] * place[2])
        columns.append((comp, const3, const5))
        for axis in range(3):
            columns.append((8 * (axis + 1) + comp, linear3[axis], linear5[axis]))
    spots = (32, 33, 34, 35, 36, 37, 38, 39, 6)
    for i in range(3):
        for a in range(3):
            columns.append((spots[3 * i + a], None, single[i][a]))
        columns.append((8 * (i + 1) + 6, None, curl_3k[i]))
    return columns


def parts_of(value):
    head = value.astype(bf16).astype(f32)
    rest = value - head
    middle = rest.astype(bf16).astype(f32)
    return head, middle, rest - middle


def near_kernel(
    blocks, ghosts, pairs_ref, gh_ref, base_ref, out_ref, xb, qt, acc
):
    zero = jnp.zeros((SEG, SEG), f32)
    blank = jnp.zeros((8, SEG), f32)

    def source_step(group, carry):
        first = pl.multiple_of(group * 64, 64)
        rows = [gh_ref[pl.ds(first + row, 8, stride=8), :] for row in range(7)]
        spots3 = [blank] * 40
        spots5 = [blank] * 40
        for spot, term3, term5 in source_columns(rows[0:3], rows[3:6], rows[6]):
            spots5[spot] = term5
            if term3 is not None:
                spots3[spot] = term3
        for half, spots, size in ((0, spots3, 32), (1, spots5, 40)):
            swapped = jnp.transpose(jnp.stack(spots[:size], axis=0), (1, 0, 2))
            for part in range(8):
                pieces = []
                for piece in parts_of(swapped[part]):
                    pieces.append(piece)
                    if size < 40:
                        pieces.append(blank)
                pieces.append(blank)
                qt[group * 8 + part, :, half * SEG : half * SEG + SEG] = jnp.concatenate(
                    pieces, axis=0
                ).astype(bf16)
        return carry

    row = lax.broadcasted_iota(jnp.int32, (16, 3 * SEG), 0)
    lane = lax.broadcasted_iota(jnp.int32, (16, 3 * SEG), 1)
    choose = jnp.where((row < 9) & (row % 3 == lane // SEG), 1.0, 0.0).astype(bf16)

    def target_step(block):
        tile = gh_ref[pl.ds(pl.multiple_of(block * 8, 8), 8), :]
        parts = jnp.concatenate(
            [piece[0:3] for piece in parts_of(tile)] + [jnp.zeros((7, SEG), f32)], axis=0
        ).astype(bf16)
        spread = lax.dot_general(
            parts, choose, (((0,), (0,)), ((), ())), preferred_element_type=f32
        )
        for axis in range(3):
            xb[3 * block + axis] = spread[:, axis * SEG : (axis + 1) * SEG]
        acc[block] = zero

    def both_step(group, carry):
        for part in range(8):
            target_step(group * 8 + part)
        return source_step(group, carry)

    lax.fori_loop(0, blocks // 8, both_step, 0)
    lax.fori_loop(blocks // 8, ghosts // 8, source_step, 0)

    def pair_step(turn, carry):
        for part in range(UNROLL):
            target = pairs_ref[0, turn * UNROLL + part]
            source = pairs_ref[1, turn * UNROLL + part]
            tile = gh_ref[pl.ds(pl.multiple_of(source * 8, 8), 8), :]
            heads = []
            tails = []
            for first in range(0, SEG, 32):
                dx = xb[3 * target, first : first + 32, :] - tile[0:1]
                dy = xb[3 * target + 1, first : first + 32, :] - tile[1:2]
                dz = xb[3 * target + 2, first : first + 32, :] - tile[2:3]
                inv_one = lax.rsqrt((dx * dx + CORE_SQUARE) + dy * dy + dz * dz)
                inv_two = inv_one * inv_one
                inv_three = inv_two * inv_one
                inv_five = inv_three * inv_two
                head3 = inv_three.astype(bf16)
                head5 = inv_five.astype(bf16)
                heads.append(jnp.concatenate([head3, head5], axis=1))
                tails.append(
                    jnp.concatenate(
                        [
                            (inv_three - head3.astype(f32)).astype(bf16),
                            (inv_five - head5.astype(f32)).astype(bf16),
                        ],
                        axis=1,
                    )
                )
            weight = qt[source]
            piece = lax.dot_general(
                jnp.concatenate(heads, axis=0), weight, TRANSPOSED, preferred_element_type=f32
            ) + lax.dot_general(
                jnp.concatenate(tails, axis=0), weight, TRANSPOSED, preferred_element_type=f32
            )
            acc[target] = acc[target] + piece
        return carry

    turns = jnp.int32(0)
    for first in range(0, pairs_ref.shape[1], PAIR_STEP):
        turns = turns + jnp.where(pairs_ref[0, first] < blocks, PAIR_STEP // UNROLL, 0)
    lax.fori_loop(0, turns, pair_step, 0)

    def force_step(block, carry):
        first = pl.multiple_of(block * 8, 8)
        tile = gh_ref[pl.ds(first, 8), :]
        sums = jnp.transpose(acc[block])
        sums = sums[0:40] + sums[40:80] + sums[80:120]
        place = [tile[axis : axis + 1] for axis in range(3)]
        dline = [tile[3 + axis : 4 + axis] for axis in range(3)]
        burgers = burgers_of(tile[6:7])
        linear = base_ref[:, pl.ds(pl.multiple_of(block * SEG, SEG), SEG)] + (
            sums[0:8] + place[0] * sums[8:16] + place[1] * sums[16:24] + place[2] * sums[24:32]
        )
        outer = [sums[32 + item : 33 + item] for item in range(8)] + [sums[6:7]]
        lone = [sums[14:15], sums[22:23], sums[30:31]]
        twice = {(a, b): place[a] * place[b] for a in range(3) for b in range(a, 3)}
        sigma = []
        for comp in range(6):
            total = linear[comp : comp + 1]
            if comp != 2:
                curved = 0.0
                for sign, i, axes in CUBICS[comp]:
                    value = lone[i] * place[axes[2]] - outer[3 * i + axes[2]]
                    value = value * twice[tuple(sorted(axes[:2]))]
                    value = value - place[axes[2]] * (
                        outer[3 * i + axes[0]] * place[axes[1]]
                        + outer[3 * i + axes[1]] * place[axes[0]]
                    )
                    curved = curved + sign * value
                sigma.append((total, curved))
            else:
                sigma.append((total, -(sigma[0][1] + sigma[1][1])))
        sigma = [total - curved for total, curved in sigma]
        full = [
            [sigma[0], sigma[3], sigma[4]],
            [sigma[3], sigma[1], sigma[5]],
            [sigma[4], sigma[5], sigma[2]],
        ]
        push = [
            full[row][0] * burgers[0] + full[row][1] * burgers[1] + full[row][2] * burgers[2]
            for row in range(3)
        ]
        force = [
            push[1] * dline[2] - push[2] * dline[1],
            push[2] * dline[0] - push[0] * dline[2],
            push[0] * dline[1] - push[1] * dline[0],
        ]
        length = jnp.sqrt(dline[0] * dline[0] + dline[1] * dline[1] + dline[2] * dline[2])
        out_ref[pl.ds(first, 8), :] = 0.5 * jnp.concatenate(
            force + [length] + sigma[0:4], axis=0
        )
        return carry

    lax.fori_loop(0, blocks, force_step, 0, unroll=8)


def near_call(pairs, ghosts, base):
    blocks = base.shape[1] // SEG
    number = ghosts.shape[0] // 8
    return pl.pallas_call(
        functools.partial(near_kernel, blocks, number),
        out_shape=jax.ShapeDtypeStruct((blocks * 8, SEG), f32),
        in_specs=[
            pl.BlockSpec(memory_space=pltpu.SMEM),
            pl.BlockSpec(memory_space=pltpu.VMEM),
            pl.BlockSpec(memory_space=pltpu.VMEM),
        ],
        out_specs=pl.BlockSpec(memory_space=pltpu.VMEM),
        scratch_shapes=[
            pltpu.VMEM((3 * blocks, SEG, SEG), f32),
            pltpu.VMEM((number, SEG, 2 * SEG), bf16),
            pltpu.VMEM((blocks, SEG, SEG), f32),
        ],
        compiler_params=pltpu.CompilerParams(vmem_limit_bytes=48 * 1024 * 1024),
    )(pairs, ghosts, base)


def wrapped(diff, extent):
    half = extent / 2.0
    return jnp.where(diff > half, diff - extent, jnp.where(diff < -half, diff + extent, diff))


def far_rows(plus, minus, step):
    both = [[plus[3 * i + j] + minus[3 * i + j] for j in range(3)] for i in range(3)]
    odd = [[plus[3 * i + j] - minus[3 * i + j] for j in range(3)] for i in range(3)]

    def curl_of(amat):
        return (amat[1][2] - amat[2][1], amat[2][0] - amat[0][2], amat[0][1] - amat[1][0])

    curl_both = curl_of(both)
    curl_odd = curl_of(odd)
    shear = SHEAR_TERM
    turned = [
        (None, 2.0 * both[2][0], -2.0 * both[1][0]),
        (step * (-2.0 * odd[2][1]), None, 2.0 * both[0][1]),
        (step * (2.0 * odd[1][2]), -2.0 * both[0][2], None),
        (step * -odd[2][0], both[2][1], both[0][0] - both[1][1]),
        (step * odd[1][0], both[2][2] - both[0][0], -both[1][2]),
        (step * (odd[1][1] - odd[2][2]), -both[0][1], both[0][2]),
    ]
    turned = [[None if item is None else shear * item for item in line] for line in turned]
    curls = {
        "ox": BULK_TERM * step * curl_odd[0],
        "oy": BULK_TERM * step * curl_odd[1],
        "oz": BULK_TERM * step * curl_odd[2],
        "bx": BULK_TERM * curl_both[0],
        "by": BULK_TERM * curl_both[1],
        "bz": BULK_TERM * curl_both[2],
        "sx": BULK_TERM * step * step * curl_both[0],
    }
    curls["ox2"] = 2.0 * curls["ox"]
    curls["by2"] = 2.0 * curls["by"]
    curls["bz2"] = 2.0 * curls["bz"]
    return turned, curls


def exchange_kernel(
    nx,
    ny,
    off_ref,
    line_ref,
    kind_ref,
    cell_ref,
    applied_ref,
    listx_ref,
    listy_ref,
    gh_ref,
    base_ref,
    products,
    hot,
    pack_x,
    land_x,
    pack_y,
    land_y,
    mine,
    row_land,
    row_block,
    all_land,
    far_acc,
    sem_x,
    sem_y,
    row_send,
    row_recv,
    all_send,
    all_recv,
):
    segs = cell_ref.shape[1]
    blocks = segs // SEG
    packet = listx_ref.shape[1]
    cells = hot.shape[0]
    me_x = lax.axis_index("gx")
    me_y = lax.axis_index("gy")
    mesh_ids = pl.DeviceIdType.MESH
    barrier = pltpu.get_barrier_semaphore()

    half_x = nx // 2
    high = me_x // half_x
    spot = me_x % half_x
    column = high * ny + me_y
    depth_count = 2 * ny

    def column_device(step):
        other = lax.rem(column + step, depth_count)
        return (other // ny * half_x + spot, other % ny)

    def plane_device(step):
        return (high * half_x + lax.rem(spot + step, half_x), me_y)

    def greet(device):
        pl.semaphore_signal(barrier, inc=1, device_id=device, device_id_type=mesh_ids)

    def greet_column(step, carry):
        greet(column_device(step))
        return carry

    def greet_plane(step, carry):
        greet(plane_device(step))
        return carry

    lax.fori_loop(1, depth_count, greet_column, 0)
    lax.fori_loop(1, half_x, greet_plane, 0)
    greet((lax.rem(me_x + nx - 1, nx), me_y))
    greet((lax.rem(me_x + 1, nx), me_y))

    cell_iota = lax.broadcasted_iota(jnp.int32, (cells, SEG), 0)
    origin = [0.5 - CENTER[axis] for axis in range(3)]

    def block_step(block, carry):
        lanes = pl.ds(pl.multiple_of(block * SEG, SEG), SEG)
        cell = cell_ref[:, lanes]
        kind = kind_ref[:, lanes]
        dline = line_ref[:, lanes]
        shift = off_ref[:, lanes]
        corner = (cell // (CCY * NCZ), cell // NCZ % CCY, cell % NCZ)
        place = [
            (corner[axis].astype(f32) + origin[axis]) + shift[axis : axis + 1] for axis in range(3)
        ]
        code = kind.astype(f32)
        gh_ref[block] = jnp.concatenate(
            place + [dline, code, jnp.zeros((1, SEG), f32)], axis=0
        )
        burgers = burgers_of(code)
        outer = jnp.concatenate(
            [burgers[0] * dline, burgers[1] * dline, burgers[2] * dline, jnp.zeros((7, SEG), f32)],
            axis=0,
        )
        for part, piece in enumerate(parts_of(outer)):
            products[part * 16 : part * 16 + 16, lanes] = piece.astype(bf16)
        hot[:, lanes] = (cell_iota == cell).astype(f32).astype(bf16)
        return carry

    lax.fori_loop(0, blocks, block_step, 0, unroll=4)

    def pick_x(item, carry):
        for side in range(2):
            source = listx_ref[side, item]
            pack_x[side, item] = gh_ref[source]
        return carry

    lax.fori_loop(0, packet, pick_x, 0, unroll=8)
    moments = lax.dot_general(products[...], hot[...], TRANSPOSED, preferred_element_type=f32)
    moments = moments[0:16] + moments[16:32] + moments[32:48]
    mine[...] = jnp.concatenate([moments, jnp.zeros((16, SEG - cells), f32)], axis=1)
    row_land[column] = mine[...]

    pl.semaphore_wait(barrier, depth_count - 1 + half_x - 1 + 2)

    copies_x = []
    for side in range(2):
        target = lax.rem(me_x + (nx - 1 if side == 0 else 1), nx)
        copies_x.append(
            pltpu.make_async_remote_copy(
                src_ref=pack_x.at[side],
                dst_ref=land_x.at[1 - side],
                send_sem=sem_x.at[side],
                recv_sem=sem_x.at[2 + side],
                device_id=(target, me_y),
                device_id_type=mesh_ids,
            )
        )
    def row_copy(step):
        return pltpu.make_async_remote_copy(
            src_ref=mine,
            dst_ref=row_land.at[column],
            send_sem=row_send.at[step],
            recv_sem=row_recv.at[step],
            device_id=column_device(step),
            device_id_type=mesh_ids,
        )

    def row_start(step, carry):
        row_copy(step).start()
        return carry

    def row_wait(step, carry):
        row_copy(step).wait()
        return carry

    lax.fori_loop(1, depth_count, row_start, 0)
    for copy in copies_x:
        copy.start()

    row_iota = lax.broadcasted_iota(jnp.int32, (8, SEG), 0)

    lax.fori_loop(1, depth_count, row_wait, 0)
    lane_iota = lax.broadcasted_iota(jnp.int32, (16, SEG), 1)
    for part in range(2):
        lasts = []
        for tile in range(4):
            first = row_land[part * ny + 2 * tile]
            second = row_land[part * ny + 2 * tile + 1]
            merged = jnp.where(lane_iota < cells, first, pltpu.roll(second, cells, 1))
            row_block[40 * part + 8 * tile : 40 * part + 8 * tile + 8, :] = merged[0:8]
            lasts.append(merged[8:9])
        row_block[40 * part + 32 : 40 * part + 40, :] = jnp.concatenate(
            lasts + [jnp.zeros((4, SEG), f32)], axis=0
        )
    all_land[spot] = row_block[...]

    def all_copy(step):
        return pltpu.make_async_remote_copy(
            src_ref=row_block,
            dst_ref=all_land.at[spot],
            send_sem=all_send.at[step],
            recv_sem=all_recv.at[step],
            device_id=plane_device(step),
            device_id_type=mesh_ids,
        )

    def all_start(step, carry):
        all_copy(step).start()
        all_copy(half_x - step).start()
        return carry

    def all_sent(step, carry):
        all_copy(step).wait_send()
        return carry

    lax.fori_loop(1, half_x // 2, all_start, 0)
    all_copy(half_x // 2).start()

    far_acc[...] = jnp.zeros_like(far_acc)

    lane = lax.broadcasted_iota(jnp.int32, (8, SEG), 1)
    source_z = (lane % NCZ).astype(f32)
    depth = [
        wrapped((row_iota + 8 * half).astype(f32) - source_z, float(NCZ)) for half in range(2)
    ]
    extent_y = float(CCY * ny)

    def far_step(apart, tile):
        step = apart.astype(f32)
        middle = apart == nx // 2
        upper = me_x >= nx // 2
        weight_plus = jnp.where(middle & jnp.logical_not(upper), 0.0, 1.0)
        weight_minus = jnp.where((apart == 0) | (middle & upper), 0.0, 1.0)
        place_plus = lax.rem(me_x - apart + nx, nx)
        place_minus = lax.rem(me_x + apart, nx)
        spot_plus = place_plus % half_x
        spot_minus = place_minus % half_x
        row_plus = place_plus // half_x * 40
        row_minus = place_minus // half_x * 40
        head_plus = (
            all_land[spot_plus, pl.ds(pl.multiple_of(row_plus + tile * 8, 8), 8), :] * weight_plus
        )
        head_minus = (
            all_land[spot_minus, pl.ds(pl.multiple_of(row_minus + tile * 8, 8), 8), :]
            * weight_minus
        )
        plus = [head_plus[item : item + 1] for item in range(8)]
        minus = [head_minus[item : item + 1] for item in range(8)]
        plus.append(all_land[spot_plus, pl.ds(row_plus + 32 + tile, 1), :] * weight_plus)
        minus.append(all_land[spot_minus, pl.ds(row_minus + 32 + tile, 1), :] * weight_minus)
        turned, curls = far_rows(plus, minus, step)
        source_y = (lane // NCZ + tile * 8).astype(f32)
        close = apart <= 1
        for quarter in range(CCY):
            ry = wrapped((me_y * CCY + quarter).astype(f32) - source_y, extent_y)
            plane = (ry * ry + CORE_SQUARE) + step * step
            beside = jnp.logical_and(jnp.abs(ry) <= 1.0, close)
            for half in range(2):
                rz = depth[half]
                inv_one = lax.rsqrt(plane + rz * rz)
                keep = jnp.logical_and(beside, jnp.abs(rz) <= 1.0)
                inv_two = inv_one * inv_one
                inv_three = jnp.where(keep, 0.0, inv_two * inv_one)
                inv_five = inv_three * inv_two
                fifth = (3.0 * CORE_SQUARE) * inv_five
                middle_gain = inv_three + fifth
                gain = inv_three + middle_gain
                dot_both = curls["ox"] + ry * curls["by"] + rz * curls["bz"]
                dot_odd = curls["sx"] + ry * curls["oy"] + rz * curls["oz"]
                trace = middle_gain * dot_both
                thrice = 3.0 * inv_five
                wave = thrice * dot_both
                wave_odd = thrice * dot_odd
                wave_y = wave * ry
                bends = (
                    curls["ox2"],
                    ry * curls["by2"],
                    rz * curls["bz2"],
                    ry * curls["bx"] + curls["oy"],
                    rz * curls["bx"] + curls["oz"],
                    rz * curls["by"] + ry * curls["bz"],
                )
                curved = (
                    wave * (step * step),
                    wave_y * ry,
                    (wave * rz) * rz,
                    wave_odd * ry,
                    wave_odd * rz,
                    wave_y * rz,
                )
                first = 8 * (2 * quarter + half)
                for comp in range(6):
                    swirl = None
                    for factor, item in zip((None, ry, rz), turned[comp]):
                        if item is not None:
                            item = item if factor is None else factor * item
                            swirl = item if swirl is None else swirl + item
                    value = gain * swirl + inv_three * bends[comp] - curved[comp]
                    if comp < 3:
                        value = value - trace
                    far_acc[comp, first : first + 8, :] = far_acc[comp, first : first + 8, :] + value

    def far_own(turn, carry):
        far_step(turn // 4 * half_x, turn % 4)
        return carry

    def far_columns(near_by, carry):
        all_copy(near_by).wait_recv()
        all_copy(half_x - near_by).wait_recv()

        def far_two(turn, inner):
            far_step(jnp.where(turn < 4, near_by, half_x - near_by), turn % 4)
            return inner

        return lax.fori_loop(0, 8, far_two, carry)

    def far_last(turn, carry):
        far_step(jnp.int32(half_x // 2), turn)
        return carry

    lax.fori_loop(0, 8, far_own, 0)

    for copy in copies_x:
        copy.wait()
    for slot in range(2):
        moved = jnp.where(row_iota == 0, -float(CCX) if slot == 0 else float(CCX), 0.0)

        def take_x(item, carry, slot=slot, moved=moved):
            gh_ref[blocks + slot * packet + item] = land_x[slot, item] + moved
            return carry

        lax.fori_loop(0, packet, take_x, 0, unroll=8)

    def pick_y(item, carry):
        for side in range(2):
            source = listy_ref[side, item]
            pack_y[side, item] = gh_ref[source]
        return carry

    lax.fori_loop(0, packet, pick_y, 0, unroll=8)
    copies_y = []
    for side in range(2):
        target = lax.rem(me_y + (ny - 1 if side == 0 else 1), ny)
        copies_y.append(
            pltpu.make_async_remote_copy(
                src_ref=pack_y.at[side],
                dst_ref=land_y.at[1 - side],
                send_sem=sem_y.at[side],
                recv_sem=sem_y.at[2 + side],
                device_id=(me_x, target),
                device_id_type=mesh_ids,
            )
        )
    for copy in copies_y:
        copy.start()


    lax.fori_loop(1, half_x // 2, far_columns, 0)
    all_copy(half_x // 2).wait_recv()
    lax.fori_loop(0, 4, far_last, 0)
    lax.fori_loop(1, half_x, all_sent, 0)

    pick = (
        lax.broadcasted_iota(jnp.int32, (8, 6 * SEG), 1) // SEG
        == lax.broadcasted_iota(jnp.int32, (8, 6 * SEG), 0)
    ).astype(f32)
    far = lax.dot_general(
        pick,
        jnp.concatenate([far_acc[comp] for comp in range(6)], axis=1),
        TRANSPOSED,
        precision=lax.Precision.HIGHEST,
        preferred_element_type=f32,
    )
    far = jnp.concatenate(list(parts_of(far)) + [jnp.zeros((8, cells), f32)], axis=0).astype(bf16)
    outside = jnp.zeros((8, 1), f32)
    comp_iota = lax.broadcasted_iota(jnp.int32, (8, 1), 0)
    for comp in range(6):
        outside = jnp.where(comp_iota == comp, applied_ref[comp], outside)
    width = 8 * SEG

    def base_step(part, carry):
        lanes = pl.ds(pl.multiple_of(part * width, width), width)
        value = jnp.dot(far, hot[:, lanes], preferred_element_type=f32)
        base_ref[:, lanes] = (value[0:8] + value[8:16] + value[16:24]) + outside
        return carry

    lax.fori_loop(0, segs // width, base_step, 0)

    for copy in copies_y:
        copy.wait()
    for slot in range(2):
        moved = jnp.where(row_iota == 1, -float(CCY) if slot == 0 else float(CCY), 0.0)

        def take_y(item, carry, slot=slot, moved=moved):
            gh_ref[blocks + (2 + slot) * packet + item] = land_y[slot, item] + moved
            return carry

        lax.fori_loop(0, packet, take_y, 0, unroll=8)


def exchange_call(nx, ny, offsets, dline, kind, cell, applied, list_x, list_y):
    segs = cell.shape[1]
    blocks = segs // SEG
    packet = list_x.shape[1]
    number = blocks + 4 * packet
    cells = CCX * CCY * NCZ
    vmem = pl.BlockSpec(memory_space=pltpu.VMEM)
    smem = pl.BlockSpec(memory_space=pltpu.SMEM)
    return pl.pallas_call(
        functools.partial(exchange_kernel, nx, ny),
        out_shape=(
            jax.ShapeDtypeStruct((number, 8, SEG), f32),
            jax.ShapeDtypeStruct((8, segs), f32),
        ),
        in_specs=[vmem] * 4 + [smem] * 3,
        out_specs=(vmem, vmem),
        scratch_shapes=[
            pltpu.VMEM((48, segs), bf16),
            pltpu.VMEM((cells, segs), bf16),
            pltpu.VMEM((2, packet, 8, SEG), f32),
            pltpu.VMEM((2, packet, 8, SEG), f32),
            pltpu.VMEM((2, packet, 8, SEG), f32),
            pltpu.VMEM((2, packet, 8, SEG), f32),
            pltpu.VMEM((16, SEG), f32),
            pltpu.VMEM((2 * ny, 16, SEG), f32),
            pltpu.VMEM((80, SEG), f32),
            pltpu.VMEM((nx // 2, 80, SEG), f32),
            pltpu.VMEM((6, cells, SEG), f32),
            pltpu.SemaphoreType.DMA((4,)),
            pltpu.SemaphoreType.DMA((4,)),
            pltpu.SemaphoreType.DMA((2 * ny,)),
            pltpu.SemaphoreType.DMA((2 * ny,)),
            pltpu.SemaphoreType.DMA((nx // 2,)),
            pltpu.SemaphoreType.DMA((nx // 2,)),
        ],
        compiler_params=pltpu.CompilerParams(
            collective_id=0, has_side_effects=True, vmem_limit_bytes=32 * 1024 * 1024
        ),
    )(offsets, dline, kind, cell, applied, list_x, list_y)


NODE_COLS = 256
CHUNK = 1024


def nodal_kernel(
    nx,
    ny,
    half_ref,
    node_ref,
    owner_ref,
    drag_ref,
    out_ref,
    column_hot,
    row_hot,
    totals,
    outgoing,
    landing,
    send_sem,
    recv_sem,
):
    segs = node_ref.shape[1]
    rows = drag_ref.shape[1] // NODE_COLS
    me_x = lax.axis_index("gx")
    me_y = lax.axis_index("gy")
    mesh_ids = pl.DeviceIdType.MESH
    beside = (
        (lax.rem(me_x + nx - 1, nx), me_y),
        (lax.rem(me_x + 1, nx), me_y),
        (me_x, lax.rem(me_y + ny - 1, ny)),
        (me_x, lax.rem(me_y + 1, ny)),
    )
    barrier = pltpu.get_barrier_semaphore()
    for device in beside:
        pl.semaphore_signal(barrier, inc=1, device_id=device, device_id_type=mesh_ids)

    column_iota = lax.broadcasted_iota(jnp.int32, (NODE_COLS, SEG), 0)

    def column_step(block, carry):
        lanes = pl.ds(pl.multiple_of(block * SEG, SEG), SEG)
        for end in range(2):
            column = node_ref[end : end + 1, lanes] % NODE_COLS
            where = pl.ds(pl.multiple_of(end * segs + block * SEG, SEG), SEG)
            column_hot[:, where] = (column_iota == column).astype(f32).astype(bf16)
        return carry

    lax.fori_loop(0, segs // SEG, column_step, 0, unroll=2)

    tiles = CHUNK // SEG
    chunks = 2 * segs // CHUNK

    def add_up(first_row, count):
        row_iota = lax.broadcasted_iota(jnp.int32, (count, SEG), 0) + first_row

        def build(buffer, chunk):
            end = chunk // (segs // CHUNK)
            for tile in range(tiles):
                block = chunk % (segs // CHUNK) * tiles + tile
                lanes = pl.ds(pl.multiple_of(block * SEG, SEG), SEG)
                both = owner_ref[:, lanes] * rows + node_ref[:, lanes] // NODE_COLS
                slot = jnp.where(end == 0, both[0:1], both[1:2])
                mask = (row_iota == slot).astype(f32).astype(bf16)
                values = half_ref[pl.ds(pl.multiple_of(block * 8, 8), 8), :]
                heads = values.astype(bf16).astype(f32)
                tails = values - heads
                for item in range(4):
                    for part, piece in enumerate((heads, tails)):
                        spot = (2 * item + part) * count
                        row = jnp.broadcast_to(piece[item : item + 1], (16, SEG)).astype(bf16)
                        row = jnp.concatenate([row] * (count // 16), axis=0)
                        row_hot[buffer, spot : spot + count, tile * SEG : (tile + 1) * SEG] = (
                            mask * row
                        )

        def add_chunk(buffer, chunk):
            where = pl.ds(pl.multiple_of(chunk * CHUNK, CHUNK), CHUNK)
            totals[0 : 8 * count, :] = totals[0 : 8 * count, :] + lax.dot_general(
                row_hot[buffer, 0 : 8 * count, :],
                column_hot[:, where],
                TRANSPOSED,
                preferred_element_type=f32,
            )

        def chunk_step(turn, carry):
            build(1, 2 * turn + 1)
            add_chunk(0, 2 * turn)
            build(0, jnp.minimum(2 * turn + 2, chunks - 1))
            add_chunk(1, 2 * turn + 1)
            return carry

        totals[0 : 8 * count, :] = jnp.zeros((8 * count, NODE_COLS), f32)
        build(0, jnp.int32(0))
        lax.fori_loop(0, chunks // 2, chunk_step, 0)

    add_up(rows, 4 * rows)
    for side in range(4):
        for item in range(4):
            spot = 2 * item * 4 * rows + side * rows
            outgoing[side, item * rows : (item + 1) * rows, :] = (
                totals[spot : spot + rows, :] + totals[spot + 4 * rows : spot + 5 * rows, :]
            )
    pl.semaphore_wait(barrier, 4)
    copies = []
    for side in range(4):
        copies.append(
            pltpu.make_async_remote_copy(
                src_ref=outgoing.at[side],
                dst_ref=landing.at[side],
                send_sem=send_sem.at[side],
                recv_sem=recv_sem.at[side],
                device_id=beside[side],
                device_id_type=mesh_ids,
            )
        )
    for copy in copies:
        copy.start()
    add_up(0, rows)
    for copy in copies:
        copy.wait()
    sums = []
    for item in range(4):
        spot = 2 * item * rows
        value = totals[spot : spot + rows, :] + totals[spot + rows : spot + 2 * rows, :]
        for side in range(4):
            value = value + landing[side, item * rows : (item + 1) * rows, :]
        sums.append(value)
    drag = jnp.concatenate(
        [drag_ref[:, row * NODE_COLS : (row + 1) * NODE_COLS] for row in range(rows)], axis=0
    )
    scale = 1.0 / (drag * (sums[3] + CORE_LENGTH))
    speed = [sums[item] * scale for item in range(3)]
    for item in range(3):
        for row in range(rows):
            first = (item * rows + row) * NODE_COLS
            out_ref[:, first : first + NODE_COLS] = speed[item][row : row + 1]


def nodal_call(nx, ny, half, node, owner, drag):
    segs = node.shape[1]
    rows = drag.shape[1] // NODE_COLS
    vmem = pl.BlockSpec(memory_space=pltpu.VMEM)
    return pl.pallas_call(
        functools.partial(nodal_kernel, nx, ny),
        out_shape=jax.ShapeDtypeStruct((1, 3 * drag.shape[1]), f32),
        in_specs=[vmem] * 4,
        out_specs=vmem,
        scratch_shapes=[
            pltpu.VMEM((NODE_COLS, 2 * segs), bf16),
            pltpu.VMEM((2, 32 * rows, CHUNK), bf16),
            pltpu.VMEM((32 * rows, NODE_COLS), f32),
            pltpu.VMEM((4, 4 * rows, NODE_COLS), f32),
            pltpu.VMEM((4, 4 * rows, NODE_COLS), f32),
            pltpu.SemaphoreType.DMA((4,)),
            pltpu.SemaphoreType.DMA((4,)),
        ],
        compiler_params=pltpu.CompilerParams(
            collective_id=1, has_side_effects=True, vmem_limit_bytes=48 * 1024 * 1024
        ),
    )(half, node, owner, drag)


def on_device(
    offsets,
    line,
    burgers_kind,
    seg_cell,
    end_node,
    end_owner,
    drag,
    applied,
    pair_list,
    ghost_x_list,
    ghost_y_list,
):
    nx = lax.axis_size("gx")
    ny = lax.axis_size("gy")
    pairs = pair_list[0, 0]
    ghosts, base = exchange_call(
        nx,
        ny,
        offsets[0, 0],
        line[0, 0],
        burgers_kind[0],
        seg_cell[0],
        applied,
        ghost_x_list[0, 0],
        ghost_y_list[0, 0],
    )
    half = near_call(pairs, ghosts.reshape(-1, SEG), base)
    velocity = nodal_call(nx, ny, half, end_node[0, 0], end_owner[0, 0], drag[0])
    return velocity.reshape(1, 1, 3, -1)


def solution(mesh):
    return jax.shard_map(
        on_device,
        mesh=mesh,
        in_specs=(
            P("gx", "gy", None, None),
            P("gx", "gy", None, None),
            P("gx", "gy", None),
            P("gx", "gy", None),
            P("gx", "gy", None, None),
            P("gx", "gy", None, None),
            P("gx", "gy", None),
            P(),
            P("gx", "gy", None, None),
            P("gx", "gy", None, None),
            P("gx", "gy", None, None),
        ),
        out_specs=P("gx", "gy", None, None),
        check_vma=False,
    )
```

```python
import functools
import math

import jax
import jax.numpy as jnp
from jax import lax
from jax.experimental import pallas as pl
from jax.experimental.pallas import tpu as pltpu
from jax.sharding import PartitionSpec as P

SEG = 128
CCX = 1
CCY = 4
NCZ = 16
CORE_SQUARE = 0.25
SHEAR_TERM = 1.0 / (8.0 * math.pi)
BULK_TERM = 1.0 / (4.0 * math.pi * 0.7)
CORE_LENGTH = 1.0
COMPONENTS = ((0, 0), (1, 1), (2, 2), (0, 1), (0, 2), (1, 2))
CUBICS = (
    ((1.0, 0, (0, 0, 0)), (1.0, 1, (1, 0, 0)), (1.0, 2, (2, 0, 0))),
    ((1.0, 0, (0, 1, 1)), (1.0, 1, (1, 1, 1)), (1.0, 2, (2, 1, 1))),
    (
        (-1.0, 0, (0, 0, 0)),
        (-1.0, 1, (1, 0, 0)),
        (-1.0, 2, (2, 0, 0)),
        (-1.0, 0, (0, 1, 1)),
        (-1.0, 1, (1, 1, 1)),
        (-1.0, 2, (2, 1, 1)),
    ),
    ((1.0, 0, (0, 0, 1)), (1.0, 1, (1, 0, 1)), (1.0, 2, (2, 0, 1))),
    ((1.0, 0, (0, 0, 2)), (1.0, 1, (0, 1, 2)), (-1.0, 2, (0, 0, 0)), (-1.0, 2, (0, 1, 1))),
    ((1.0, 0, (0, 1, 2)), (1.0, 1, (1, 1, 2)), (-1.0, 2, (0, 0, 1)), (-1.0, 2, (1, 1, 1))),
)
CENTER = (CCX / 2.0, CCY / 2.0, NCZ / 2.0)
UNROLL = 128
PAIR_STEP = 256
TRANSPOSED = (((1,), (1,)), ((), ()))
f32 = jnp.float32
bf16 = jnp.bfloat16


def burgers_of(kind):
    code = kind.astype(jnp.int32)
    return [1.0 - 2.0 * ((code >> bit) & 1).astype(f32) for bit in range(3)]


def source_columns(place, dline, kind):
    burgers = burgers_of(kind)
    amat = [[burgers[i] * dline[j] for j in range(3)] for i in range(3)]
    curl = [
        amat[1][2] - amat[2][1],
        amat[2][0] - amat[0][2],
        amat[0][1] - amat[1][0],
    ]
    turned = {
        (0, 0): (None, 2.0 * amat[2][0], -2.0 * amat[1][0]),
        (1, 1): (-2.0 * amat[2][1], None, 2.0 * amat[0][1]),
        (2, 2): (2.0 * amat[1][2], -2.0 * amat[0][2], None),
        (0, 1): (-amat[2][0], amat[2][1], amat[0][0] - amat[1][1]),
        (0, 2): (amat[1][0], amat[2][2] - amat[0][0], -amat[1][2]),
        (1, 2): (amat[1][1] - amat[2][2], -amat[0][1], amat[0][2]),
    }
    bulk3 = 3.0 * BULK_TERM
    curl_k = [BULK_TERM * item for item in curl]
    curl_3k = [bulk3 * item for item in curl]
    pairs = {(a, b): place[a] * place[b] for a in range(3) for b in range(a, 3)}
    single = [[curl_3k[i] * place[a] for a in range(3)] for i in range(3)]
    double = {}

    def doubled(i, a, b):
        key = (i, min(a, b), max(a, b))
        if key not in double:
            double[key] = curl_3k[i] * pairs[key[1:]]
        return double[key]

    columns = []
    for comp, (a, b) in enumerate(COMPONENTS):
        linear5 = [0.0, 0.0, 0.0]
        linear3 = [0.0, 0.0, 0.0]
        const5 = 0.0
        for sign, i, axes in CUBICS[comp]:
            for spot in range(3):
                rest = axes[:spot] + axes[spot + 1 :]
                linear5[axes[spot]] = linear5[axes[spot]] - sign * doubled(i, *rest)
            const5 = const5 + sign * (doubled(i, axes[0], axes[1]) * place[axes[2]])
        for axis in range(3):
            alpha3 = 0.0
            alpha5 = 0.0
            if turned[(a, b)][axis] is not None:
                alpha3 = (2.0 * SHEAR_TERM) * turned[(a, b)][axis]
                alpha5 = (3.0 * CORE_SQUARE * SHEAR_TERM) * turned[(a, b)][axis]
            if axis == b:
                alpha3 = alpha3 + curl_k[a]
            if axis == a:
                alpha3 = alpha3 + curl_k[b]
            if a == b:
                alpha3 = alpha3 - curl_k[axis]
                alpha5 = alpha5 - (3.0 * CORE_SQUARE) * curl_k[axis]
            if (a, b) == (2, 2):
                alpha3 = alpha3 - curl_3k[axis]
                alpha5 = alpha5 + CORE_SQUARE * curl_3k[axis]
            if b == 2 and a == axis and a < 2:
                alpha3 = alpha3 - curl_3k[2]
                alpha5 = alpha5 + CORE_SQUARE * curl_3k[2]
            linear3[axis] = alpha3
            linear5[axis] = linear5[axis] + alpha5
            const5 = const5 - alpha5 * place[axis]
        const3 = -(linear3[0] * place[0] + linear3[1] * place[1] + linear3[2] * place[2])
        columns.append((comp, const3, const5))
        for axis in range(3):
            columns.append((8 * (axis + 1) + comp, linear3[axis], linear5[axis]))
    spots = (32, 33, 34, 35, 36, 37, 38, 39, 6)
    for i in range(3):
        for a in range(3):
            columns.append((spots[3 * i + a], None, single[i][a]))
        columns.append((8 * (i + 1) + 6, None, curl_3k[i]))
    return columns


def parts_of(value):
    head = value.astype(bf16).astype(f32)
    rest = value - head
    middle = rest.astype(bf16).astype(f32)
    return head, middle, rest - middle


def near_kernel(
    blocks, ghosts, pairs_ref, gh_ref, base_ref, out_ref, xb, qt, acc
):
    zero = jnp.zeros((SEG, SEG), f32)
    blank = jnp.zeros((8, SEG), f32)

    def source_step(group, carry):
        first = pl.multiple_of(group * 64, 64)
        rows = [gh_ref[pl.ds(first + row, 8, stride=8), :] for row in range(7)]
        spots3 = [blank] * 40
        spots5 = [blank] * 40
        for spot, term3, term5 in source_columns(rows[0:3], rows[3:6], rows[6]):
            spots5[spot] = term5
            if term3 is not None:
                spots3[spot] = term3
        for half, spots, size in ((0, spots3, 32), (1, spots5, 40)):
            swapped = jnp.transpose(jnp.stack(spots[:size], axis=0), (1, 0, 2))
            for part in range(8):
                pieces = []
                for piece in parts_of(swapped[part]):
                    pieces.append(piece)
                    if size < 40:
                        pieces.append(blank)
                pieces.append(blank)
                qt[group * 8 + part, :, half * SEG : half * SEG + SEG] = jnp.concatenate(
                    pieces, axis=0
                ).astype(bf16)
        return carry

    row = lax.broadcasted_iota(jnp.int32, (16, 3 * SEG), 0)
    lane = lax.broadcasted_iota(jnp.int32, (16, 3 * SEG), 1)
    choose = jnp.where((row < 9) & (row % 3 == lane // SEG), 1.0, 0.0).astype(bf16)

    def target_step(block):
        tile = gh_ref[pl.ds(pl.multiple_of(block * 8, 8), 8), :]
        parts = jnp.concatenate(
            [piece[0:3] for piece in parts_of(tile)] + [jnp.zeros((7, SEG), f32)], axis=0
        ).astype(bf16)
        spread = lax.dot_general(
            parts, choose, (((0,), (0,)), ((), ())), preferred_element_type=f32
        )
        for axis in range(3):
            xb[3 * block + axis] = spread[:, axis * SEG : (axis + 1) * SEG]
        acc[block] = zero

    def both_step(group, carry):
        for part in range(8):
            target_step(group * 8 + part)
        return source_step(group, carry)

    lax.fori_loop(0, blocks // 8, both_step, 0)
    lax.fori_loop(blocks // 8, ghosts // 8, source_step, 0)

    def pair_step(turn, carry):
        for part in range(UNROLL):
            target = pairs_ref[0, turn * UNROLL + part]
            source = pairs_ref[1, turn * UNROLL + part]
            tile = gh_ref[pl.ds(pl.multiple_of(source * 8, 8), 8), :]
            heads = []
            tails = []
            for first in range(0, SEG, 32):
                dx = xb[3 * target, first : first + 32, :] - tile[0:1]
                dy = xb[3 * target + 1, first : first + 32, :] - tile[1:2]
                dz = xb[3 * target + 2, first : first + 32, :] - tile[2:3]
                inv_one = lax.rsqrt((dx * dx + CORE_SQUARE) + dy * dy + dz * dz)
                inv_two = inv_one * inv_one
                inv_three = inv_two * inv_one
                inv_five = inv_three * inv_two
                head3 = inv_three.astype(bf16)
                head5 = inv_five.astype(bf16)
                heads.append(jnp.concatenate([head3, head5], axis=1))
                tails.append(
                    jnp.concatenate(
                        [
                            (inv_three - head3.astype(f32)).astype(bf16),
                            (inv_five - head5.astype(f32)).astype(bf16),
                        ],
                        axis=1,
                    )
                )
            weight = qt[source]
            piece = lax.dot_general(
                jnp.concatenate(heads, axis=0), weight, TRANSPOSED, preferred_element_type=f32
            ) + lax.dot_general(
                jnp.concatenate(tails, axis=0), weight, TRANSPOSED, preferred_element_type=f32
            )
            acc[target] = acc[target] + piece
        return carry

    turns = jnp.int32(0)
    for first in range(0, pairs_ref.shape[1], PAIR_STEP):
        turns = turns + jnp.where(pairs_ref[0, first] < blocks, PAIR_STEP // UNROLL, 0)
    lax.fori_loop(0, turns, pair_step, 0)

    def force_step(block, carry):
        first = pl.multiple_of(block * 8, 8)
        tile = gh_ref[pl.ds(first, 8), :]
        sums = jnp.transpose(acc[block])
        sums = sums[0:40] + sums[40:80] + sums[80:120]
        place = [tile[axis : axis + 1] for axis in range(3)]
        dline = [tile[3 + axis : 4 + axis] for axis in range(3)]
        burgers = burgers_of(tile[6:7])
        linear = base_ref[:, pl.ds(pl.multiple_of(block * SEG, SEG), SEG)] + (
            sums[0:8] + place[0] * sums[8:16] + place[1] * sums[16:24] + place[2] * sums[24:32]
        )
        outer = [sums[32 + item : 33 + item] for item in range(8)] + [sums[6:7]]
        lone = [sums[14:15], sums[22:23], sums[30:31]]
        twice = {(a, b): place[a] * place[b] for a in range(3) for b in range(a, 3)}
        sigma = []
        for comp in range(6):
            total = linear[comp : comp + 1]
            if comp != 2:
                curved = 0.0
                for sign, i, axes in CUBICS[comp]:
                    value = lone[i] * place[axes[2]] - outer[3 * i + axes[2]]
                    value = value * twice[tuple(sorted(axes[:2]))]
                    value = value - place[axes[2]] * (
                        outer[3 * i + axes[0]] * place[axes[1]]
                        + outer[3 * i + axes[1]] * place[axes[0]]
                    )
                    curved = curved + sign * value
                sigma.append((total, curved))
            else:
                sigma.append((total, -(sigma[0][1] + sigma[1][1])))
        sigma = [total - curved for total, curved in sigma]
        full = [
            [sigma[0], sigma[3], sigma[4]],
            [sigma[3], sigma[1], sigma[5]],
            [sigma[4], sigma[5], sigma[2]],
        ]
        push = [
            full[row][0] * burgers[0] + full[row][1] * burgers[1] + full[row][2] * burgers[2]
            for row in range(3)
        ]
        force = [
            push[1] * dline[2] - push[2] * dline[1],
            push[2] * dline[0] - push[0] * dline[2],
            push[0] * dline[1] - push[1] * dline[0],
        ]
        length = jnp.sqrt(dline[0] * dline[0] + dline[1] * dline[1] + dline[2] * dline[2])
        out_ref[pl.ds(first, 8), :] = 0.5 * jnp.concatenate(
            force + [length] + sigma[0:4], axis=0
        )
        return carry

    lax.fori_loop(0, blocks, force_step, 0, unroll=8)


def near_call(pairs, ghosts, base):
    blocks = base.shape[1] // SEG
    number = ghosts.shape[0] // 8
    return pl.pallas_call(
        functools.partial(near_kernel, blocks, number),
        out_shape=jax.ShapeDtypeStruct((blocks * 8, SEG), f32),
        in_specs=[
            pl.BlockSpec(memory_space=pltpu.SMEM),
            pl.BlockSpec(memory_space=pltpu.VMEM),
            pl.BlockSpec(memory_space=pltpu.VMEM),
        ],
        out_specs=pl.BlockSpec(memory_space=pltpu.VMEM),
        scratch_shapes=[
            pltpu.VMEM((3 * blocks, SEG, SEG), f32),
            pltpu.VMEM((number, SEG, 2 * SEG), bf16),
            pltpu.VMEM((blocks, SEG, SEG), f32),
        ],
        compiler_params=pltpu.CompilerParams(vmem_limit_bytes=48 * 1024 * 1024),
    )(pairs, ghosts, base)


def wrapped(diff, extent):
    half = extent / 2.0
    return jnp.where(diff > half, diff - extent, jnp.where(diff < -half, diff + extent, diff))


def far_rows(plus, minus, step):
    both = [[plus[3 * i + j] + minus[3 * i + j] for j in range(3)] for i in range(3)]
    odd = [[plus[3 * i + j] - minus[3 * i + j] for j in range(3)] for i in range(3)]

    def curl_of(amat):
        return (amat[1][2] - amat[2][1], amat[2][0] - amat[0][2], amat[0][1] - amat[1][0])

    curl_both = curl_of(both)
    curl_odd = curl_of(odd)
    shear = SHEAR_TERM
    turned = [
        (None, 2.0 * both[2][0], -2.0 * both[1][0]),
        (step * (-2.0 * odd[2][1]), None, 2.0 * both[0][1]),
        (step * (2.0 * odd[1][2]), -2.0 * both[0][2], None),
        (step * -odd[2][0], both[2][1], both[0][0] - both[1][1]),
        (step * odd[1][0], both[2][2] - both[0][0], -both[1][2]),
        (step * (odd[1][1] - odd[2][2]), -both[0][1], both[0][2]),
    ]
    turned = [[None if item is None else shear * item for item in line] for line in turned]
    curls = {
        "ox": BULK_TERM * step * curl_odd[0],
        "oy": BULK_TERM * step * curl_odd[1],
        "oz": BULK_TERM * step * curl_odd[2],
        "bx": BULK_TERM * curl_both[0],
        "by": BULK_TERM * curl_both[1],
        "bz": BULK_TERM * curl_both[2],
        "sx": BULK_TERM * step * step * curl_both[0],
    }
    curls["ox2"] = 2.0 * curls["ox"]
    curls["by2"] = 2.0 * curls["by"]
    curls["bz2"] = 2.0 * curls["bz"]
    return turned, curls


def exchange_kernel(
    nx,
    ny,
    off_ref,
    line_ref,
    kind_ref,
    cell_ref,
    applied_ref,
    listx_ref,
    listy_ref,
    gh_ref,
    base_ref,
    products,
    hot,
    pack_x,
    land_x,
    pack_y,
    land_y,
    mine,
    row_land,
    row_block,
    all_land,
    far_acc,
    sem_x,
    sem_y,
    row_send,
    row_recv,
    all_send,
    all_recv,
):
    segs = cell_ref.shape[1]
    blocks = segs // SEG
    packet = listx_ref.shape[1]
    cells = hot.shape[0]
    me_x = lax.axis_index("gx")
    me_y = lax.axis_index("gy")
    mesh_ids = pl.DeviceIdType.MESH
    barrier = pltpu.get_barrier_semaphore()

    half_x = nx // 2
    high = me_x // half_x
    spot = me_x % half_x
    column = high * ny + me_y
    depth_count = 2 * ny

    def column_device(step):
        other = lax.rem(column + step, depth_count)
        return (other // ny * half_x + spot, other % ny)

    def plane_device(step):
        return (high * half_x + lax.rem(spot + step, half_x), me_y)

    def greet(device):
        pl.semaphore_signal(barrier, inc=1, device_id=device, device_id_type=mesh_ids)

    def greet_column(step, carry):
        greet(column_device(step))
        return carry

    def greet_plane(step, carry):
        greet(plane_device(step))
        return carry

    lax.fori_loop(1, depth_count, greet_column, 0)
    lax.fori_loop(1, half_x, greet_plane, 0)
    greet((lax.rem(me_x + nx - 1, nx), me_y))
    greet((lax.rem(me_x + 1, nx), me_y))

    cell_iota = lax.broadcasted_iota(jnp.int32, (cells, SEG), 0)
    origin = [0.5 - CENTER[axis] for axis in range(3)]

    def block_step(block, carry):
        lanes = pl.ds(pl.multiple_of(block * SEG, SEG), SEG)
        cell = cell_ref[:, lanes]
        kind = kind_ref[:, lanes]
        dline = line_ref[:, lanes]
        shift = off_ref[:, lanes]
        corner = (cell // (CCY * NCZ), cell // NCZ % CCY, cell % NCZ)
        place = [
            (corner[axis].astype(f32) + origin[axis]) + shift[axis : axis + 1] for axis in range(3)
        ]
        code = kind.astype(f32)
        gh_ref[block] = jnp.concatenate(
            place + [dline, code, jnp.zeros((1, SEG), f32)], axis=0
        )
        burgers = burgers_of(code)
        outer = jnp.concatenate(
            [burgers[0] * dline, burgers[1] * dline, burgers[2] * dline, jnp.zeros((7, SEG), f32)],
            axis=0,
        )
        for part, piece in enumerate(parts_of(outer)):
            products[part * 16 : part * 16 + 16, lanes] = piece.astype(bf16)
        hot[:, lanes] = (cell_iota == cell).astype(f32).astype(bf16)
        return carry

    lax.fori_loop(0, blocks, block_step, 0, unroll=4)

    def pick_x(item, carry):
        for side in range(2):
            source = listx_ref[side, item]
            pack_x[side, item] = gh_ref[source]
        return carry

    lax.fori_loop(0, packet, pick_x, 0, unroll=8)
    moments = lax.dot_general(products[...], hot[...], TRANSPOSED, preferred_element_type=f32)
    moments = moments[0:16] + moments[16:32] + moments[32:48]
    mine[...] = jnp.concatenate([moments, jnp.zeros((16, SEG - cells), f32)], axis=1)
    row_land[column] = mine[...]

    pl.semaphore_wait(barrier, depth_count - 1 + half_x - 1 + 2)

    copies_x = []
    for side in range(2):
        target = lax.rem(me_x + (nx - 1 if side == 0 else 1), nx)
        copies_x.append(
            pltpu.make_async_remote_copy(
                src_ref=pack_x.at[side],
                dst_ref=land_x.at[1 - side],
                send_sem=sem_x.at[side],
                recv_sem=sem_x.at[2 + side],
                device_id=(target, me_y),
                device_id_type=mesh_ids,
            )
        )
    def row_copy(step):
        return pltpu.make_async_remote_copy(
            src_ref=mine,
            dst_ref=row_land.at[column],
            send_sem=row_send.at[step],
            recv_sem=row_recv.at[step],
            device_id=column_device(step),
            device_id_type=mesh_ids,
        )

    def row_start(step, carry):
        row_copy(step).start()
        return carry

    def row_wait(step, carry):
        row_copy(step).wait()
        return carry

    lax.fori_loop(1, depth_count, row_start, 0)
    for copy in copies_x:
        copy.start()

    row_iota = lax.broadcasted_iota(jnp.int32, (8, SEG), 0)

    lax.fori_loop(1, depth_count, row_wait, 0)
    lane_iota = lax.broadcasted_iota(jnp.int32, (16, SEG), 1)
    for part in range(2):
        lasts = []
        for tile in range(4):
            first = row_land[part * ny + 2 * tile]
            second = row_land[part * ny + 2 * tile + 1]
            merged = jnp.where(lane_iota < cells, first, pltpu.roll(second, cells, 1))
            row_block[40 * part + 8 * tile : 40 * part + 8 * tile + 8, :] = merged[0:8]
            lasts.append(merged[8:9])
        row_block[40 * part + 32 : 40 * part + 40, :] = jnp.concatenate(
            lasts + [jnp.zeros((4, SEG), f32)], axis=0
        )
    all_land[spot] = row_block[...]

    def all_copy(step):
        return pltpu.make_async_remote_copy(
            src_ref=row_block,
            dst_ref=all_land.at[spot],
            send_sem=all_send.at[step],
            recv_sem=all_recv.at[step],
            device_id=plane_device(step),
            device_id_type=mesh_ids,
        )

    def all_start(step, carry):
        all_copy(step).start()
        all_copy(half_x - step).start()
        return carry

    def all_sent(step, carry):
        all_copy(step).wait_send()
        return carry

    lax.fori_loop(1, half_x // 2, all_start, 0)
    all_copy(half_x // 2).start()

    far_acc[...] = jnp.zeros_like(far_acc)

    lane = lax.broadcasted_iota(jnp.int32, (8, SEG), 1)
    source_z = (lane % NCZ).astype(f32)
    depth = [
        wrapped((row_iota + 8 * half).astype(f32) - source_z, float(NCZ)) for half in range(2)
    ]
    extent_y = float(CCY * ny)

    def far_step(apart, tile):
        step = apart.astype(f32)
        middle = apart == nx // 2
        upper = me_x >= nx // 2
        weight_plus = jnp.where(middle & jnp.logical_not(upper), 0.0, 1.0)
        weight_minus = jnp.where((apart == 0) | (middle & upper), 0.0, 1.0)
        place_plus = lax.rem(me_x - apart + nx, nx)
        place_minus = lax.rem(me_x + apart, nx)
        spot_plus = place_plus % half_x
        spot_minus = place_minus % half_x
        row_plus = place_plus // half_x * 40
        row_minus = place_minus // half_x * 40
        head_plus = (
            all_land[spot_plus, pl.ds(pl.multiple_of(row_plus + tile * 8, 8), 8), :] * weight_plus
        )
        head_minus = (
            all_land[spot_minus, pl.ds(pl.multiple_of(row_minus + tile * 8, 8), 8), :]
            * weight_minus
        )
        plus = [head_plus[item : item + 1] for item in range(8)]
        minus = [head_minus[item : item + 1] for item in range(8)]
        plus.append(all_land[spot_plus, pl.ds(row_plus + 32 + tile, 1), :] * weight_plus)
        minus.append(all_land[spot_minus, pl.ds(row_minus + 32 + tile, 1), :] * weight_minus)
        turned, curls = far_rows(plus, minus, step)
        source_y = (lane // NCZ + tile * 8).astype(f32)
        close = apart <= 1
        for quarter in range(CCY):
            ry = wrapped((me_y * CCY + quarter).astype(f32) - source_y, extent_y)
            plane = (ry * ry + CORE_SQUARE) + step * step
            beside = jnp.logical_and(jnp.abs(ry) <= 1.0, close)
            for half in range(2):
                rz = depth[half]
                inv_one = lax.rsqrt(plane + rz * rz)
                keep = jnp.logical_and(beside, jnp.abs(rz) <= 1.0)
                inv_two = inv_one * inv_one
                inv_three = jnp.where(keep, 0.0, inv_two * inv_one)
                inv_five = inv_three * inv_two
                fifth = (3.0 * CORE_SQUARE) * inv_five
                middle_gain = inv_three + fifth
                gain = inv_three + middle_gain
                dot_both = curls["ox"] + ry * curls["by"] + rz * curls["bz"]
                dot_odd = curls["sx"] + ry * curls["oy"] + rz * curls["oz"]
                trace = middle_gain * dot_both
                thrice = 3.0 * inv_five
                wave = thrice * dot_both
                wave_odd = thrice * dot_odd
                wave_y = wave * ry
                bends = (
                    curls["ox2"],
                    ry * curls["by2"],
                    rz * curls["bz2"],
                    ry * curls["bx"] + curls["oy"],
                    rz * curls["bx"] + curls["oz"],
                    rz * curls["by"] + ry * curls["bz"],
                )
                curved = (
                    wave * (step * step),
                    wave_y * ry,
                    (wave * rz) * rz,
                    wave_odd * ry,
                    wave_odd * rz,
                    wave_y * rz,
                )
                first = 8 * (2 * quarter + half)
                for comp in range(6):
                    swirl = None
                    for factor, item in zip((None, ry, rz), turned[comp]):
                        if item is not None:
                            item = item if factor is None else factor * item
                            swirl = item if swirl is None else swirl + item
                    value = gain * swirl + inv_three * bends[comp] - curved[comp]
                    if comp < 3:
                        value = value - trace
                    far_acc[comp, first : first + 8, :] = far_acc[comp, first : first + 8, :] + value

    def far_own(turn, carry):
        far_step(turn // 4 * half_x, turn % 4)
        return carry

    def far_columns(near_by, carry):
        all_copy(near_by).wait_recv()
        all_copy(half_x - near_by).wait_recv()

        def far_two(turn, inner):
            far_step(jnp.where(turn < 4, near_by, half_x - near_by), turn % 4)
            return inner

        return lax.fori_loop(0, 8, far_two, carry)

    def far_last(turn, carry):
        far_step(jnp.int32(half_x // 2), turn)
        return carry

    lax.fori_loop(0, 8, far_own, 0)

    for copy in copies_x:
        copy.wait()
    for slot in range(2):
        moved = jnp.where(row_iota == 0, -float(CCX) if slot == 0 else float(CCX), 0.0)

        def take_x(item, carry, slot=slot, moved=moved):
            gh_ref[blocks + slot * packet + item] = land_x[slot, item] + moved
            return carry

        lax.fori_loop(0, packet, take_x, 0, unroll=8)

    def pick_y(item, carry):
        for side in range(2):
            source = listy_ref[side, item]
            pack_y[side, item] = gh_ref[source]
        return carry

    lax.fori_loop(0, packet, pick_y, 0, unroll=8)
    copies_y = []
    for side in range(2):
        target = lax.rem(me_y + (ny - 1 if side == 0 else 1), ny)
        copies_y.append(
            pltpu.make_async_remote_copy(
                src_ref=pack_y.at[side],
                dst_ref=land_y.at[1 - side],
                send_sem=sem_y.at[side],
                recv_sem=sem_y.at[2 + side],
                device_id=(me_x, target),
                device_id_type=mesh_ids,
            )
        )
    for copy in copies_y:
        copy.start()


    lax.fori_loop(1, half_x // 2, far_columns, 0)
    all_copy(half_x // 2).wait_recv()
    lax.fori_loop(0, 4, far_last, 0)
    lax.fori_loop(1, half_x, all_sent, 0)

    pick = (
        lax.broadcasted_iota(jnp.int32, (8, 6 * SEG), 1) // SEG
        == lax.broadcasted_iota(jnp.int32, (8, 6 * SEG), 0)
    ).astype(f32)
    far = lax.dot_general(
        pick,
        jnp.concatenate([far_acc[comp] for comp in range(6)], axis=1),
        TRANSPOSED,
        precision=lax.Precision.HIGHEST,
        preferred_element_type=f32,
    )
    far = jnp.concatenate(list(parts_of(far)) + [jnp.zeros((8, cells), f32)], axis=0).astype(bf16)
    outside = jnp.zeros((8, 1), f32)
    comp_iota = lax.broadcasted_iota(jnp.int32, (8, 1), 0)
    for comp in range(6):
        outside = jnp.where(comp_iota == comp, applied_ref[comp], outside)
    width = 8 * SEG

    def base_step(part, carry):
        lanes = pl.ds(pl.multiple_of(part * width, width), width)
        value = jnp.dot(far, hot[:, lanes], preferred_element_type=f32)
        base_ref[:, lanes] = (value[0:8] + value[8:16] + value[16:24]) + outside
        return carry

    lax.fori_loop(0, segs // width, base_step, 0)

    for copy in copies_y:
        copy.wait()
    for slot in range(2):
        moved = jnp.where(row_iota == 1, -float(CCY) if slot == 0 else float(CCY), 0.0)

        def take_y(item, carry, slot=slot, moved=moved):
            gh_ref[blocks + (2 + slot) * packet + item] = land_y[slot, item] + moved
            return carry

        lax.fori_loop(0, packet, take_y, 0, unroll=8)


def exchange_call(nx, ny, offsets, dline, kind, cell, applied, list_x, list_y):
    segs = cell.shape[1]
    blocks = segs // SEG
    packet = list_x.shape[1]
    number = blocks + 4 * packet
    cells = CCX * CCY * NCZ
    vmem = pl.BlockSpec(memory_space=pltpu.VMEM)
    smem = pl.BlockSpec(memory_space=pltpu.SMEM)
    return pl.pallas_call(
        functools.partial(exchange_kernel, nx, ny),
        out_shape=(
            jax.ShapeDtypeStruct((number, 8, SEG), f32),
            jax.ShapeDtypeStruct((8, segs), f32),
        ),
        in_specs=[vmem] * 4 + [smem] * 3,
        out_specs=(vmem, vmem),
        scratch_shapes=[
            pltpu.VMEM((48, segs), bf16),
            pltpu.VMEM((cells, segs), bf16),
            pltpu.VMEM((2, packet, 8, SEG), f32),
            pltpu.VMEM((2, packet, 8, SEG), f32),
            pltpu.VMEM((2, packet, 8, SEG), f32),
            pltpu.VMEM((2, packet, 8, SEG), f32),
            pltpu.VMEM((16, SEG), f32),
            pltpu.VMEM((2 * ny, 16, SEG), f32),
            pltpu.VMEM((80, SEG), f32),
            pltpu.VMEM((nx // 2, 80, SEG), f32),
            pltpu.VMEM((6, cells, SEG), f32),
            pltpu.SemaphoreType.DMA((4,)),
            pltpu.SemaphoreType.DMA((4,)),
            pltpu.SemaphoreType.DMA((2 * ny,)),
            pltpu.SemaphoreType.DMA((2 * ny,)),
            pltpu.SemaphoreType.DMA((nx // 2,)),
            pltpu.SemaphoreType.DMA((nx // 2,)),
        ],
        compiler_params=pltpu.CompilerParams(
            collective_id=0, has_side_effects=True, vmem_limit_bytes=32 * 1024 * 1024
        ),
    )(offsets, dline, kind, cell, applied, list_x, list_y)


NODE_COLS = 256
CHUNK = 1024


def nodal_kernel(
    nx,
    ny,
    half_ref,
    node_ref,
    owner_ref,
    drag_ref,
    out_ref,
    column_hot,
    row_hot,
    totals,
    outgoing,
    landing,
    send_sem,
    recv_sem,
):
    segs = node_ref.shape[1]
    rows = drag_ref.shape[1] // NODE_COLS
    me_x = lax.axis_index("gx")
    me_y = lax.axis_index("gy")
    mesh_ids = pl.DeviceIdType.MESH
    beside = (
        (lax.rem(me_x + nx - 1, nx), me_y),
        (lax.rem(me_x + 1, nx), me_y),
        (me_x, lax.rem(me_y + ny - 1, ny)),
        (me_x, lax.rem(me_y + 1, ny)),
    )
    barrier = pltpu.get_barrier_semaphore()
    for device in beside:
        pl.semaphore_signal(barrier, inc=1, device_id=device, device_id_type=mesh_ids)

    column_iota = lax.broadcasted_iota(jnp.int32, (NODE_COLS, SEG), 0)

    def column_step(block, carry):
        lanes = pl.ds(pl.multiple_of(block * SEG, SEG), SEG)
        for end in range(2):
            column = node_ref[end : end + 1, lanes] % NODE_COLS
            where = pl.ds(pl.multiple_of(end * segs + block * SEG, SEG), SEG)
            column_hot[:, where] = (column_iota == column).astype(f32).astype(bf16)
        return carry

    lax.fori_loop(0, segs // SEG, column_step, 0, unroll=4)

    tiles = CHUNK // SEG
    chunks = 2 * segs // CHUNK

    def add_up(first_row, count):
        row_iota = lax.broadcasted_iota(jnp.int32, (count, SEG), 0) + first_row

        def build(buffer, chunk):
            end = chunk // (segs // CHUNK)
            for tile in range(tiles):
                block = chunk % (segs // CHUNK) * tiles + tile
                lanes = pl.ds(pl.multiple_of(block * SEG, SEG), SEG)
                both = owner_ref[:, lanes] * rows + node_ref[:, lanes] // NODE_COLS
                slot = jnp.where(end == 0, both[0:1], both[1:2])
                mask = (row_iota == slot).astype(f32).astype(bf16)
                values = half_ref[pl.ds(pl.multiple_of(block * 8, 8), 8), :]
                heads = values.astype(bf16).astype(f32)
                tails = values - heads
                for item in range(4):
                    for part, piece in enumerate((heads, tails)):
                        spot = (2 * item + part) * count
                        row = jnp.broadcast_to(piece[item : item + 1], (16, SEG)).astype(bf16)
                        row = jnp.concatenate([row] * (count // 16), axis=0)
                        row_hot[buffer, spot : spot + count, tile * SEG : (tile + 1) * SEG] = (
                            mask * row
                        )

        def add_chunk(buffer, chunk):
            where = pl.ds(pl.multiple_of(chunk * CHUNK, CHUNK), CHUNK)
            totals[0 : 8 * count, :] = totals[0 : 8 * count, :] + lax.dot_general(
                row_hot[buffer, 0 : 8 * count, :],
                column_hot[:, where],
                TRANSPOSED,
                preferred_element_type=f32,
            )

        def chunk_step(turn, carry):
            build(1, 2 * turn + 1)
            add_chunk(0, 2 * turn)
            build(0, jnp.minimum(2 * turn + 2, chunks - 1))
            add_chunk(1, 2 * turn + 1)
            return carry

        totals[0 : 8 * count, :] = jnp.zeros((8 * count, NODE_COLS), f32)
        build(0, jnp.int32(0))
        lax.fori_loop(0, chunks // 2, chunk_step, 0)

    add_up(rows, 4 * rows)
    for side in range(4):
        for item in range(4):
            spot = 2 * item * 4 * rows + side * rows
            outgoing[side, item * rows : (item + 1) * rows, :] = (
                totals[spot : spot + rows, :] + totals[spot + 4 * rows : spot + 5 * rows, :]
            )
    pl.semaphore_wait(barrier, 4)
    copies = []
    for side in range(4):
        copies.append(
            pltpu.make_async_remote_copy(
                src_ref=outgoing.at[side],
                dst_ref=landing.at[side],
                send_sem=send_sem.at[side],
                recv_sem=recv_sem.at[side],
                device_id=beside[side],
                device_id_type=mesh_ids,
            )
        )
    for copy in copies:
        copy.start()
    add_up(0, rows)
    for copy in copies:
        copy.wait()
    sums = []
    for item in range(4):
        spot = 2 * item * rows
        value = totals[spot : spot + rows, :] + totals[spot + rows : spot + 2 * rows, :]
        for side in range(4):
            value = value + landing[side, item * rows : (item + 1) * rows, :]
        sums.append(value)
    drag = jnp.concatenate(
        [drag_ref[:, row * NODE_COLS : (row + 1) * NODE_COLS] for row in range(rows)], axis=0
    )
    scale = 1.0 / (drag * (sums[3] + CORE_LENGTH))
    speed = [sums[item] * scale for item in range(3)]
    for item in range(3):
        for row in range(rows):
            first = (item * rows + row) * NODE_COLS
            out_ref[:, first : first + NODE_COLS] = speed[item][row : row + 1]


def nodal_call(nx, ny, half, node, owner, drag):
    segs = node.shape[1]
    rows = drag.shape[1] // NODE_COLS
    vmem = pl.BlockSpec(memory_space=pltpu.VMEM)
    return pl.pallas_call(
        functools.partial(nodal_kernel, nx, ny),
        out_shape=jax.ShapeDtypeStruct((1, 3 * drag.shape[1]), f32),
        in_specs=[vmem] * 4,
        out_specs=vmem,
        scratch_shapes=[
            pltpu.VMEM((NODE_COLS, 2 * segs), bf16),
            pltpu.VMEM((2, 32 * rows, CHUNK), bf16),
            pltpu.VMEM((32 * rows, NODE_COLS), f32),
            pltpu.VMEM((4, 4 * rows, NODE_COLS), f32),
            pltpu.VMEM((4, 4 * rows, NODE_COLS), f32),
            pltpu.SemaphoreType.DMA((4,)),
            pltpu.SemaphoreType.DMA((4,)),
        ],
        compiler_params=pltpu.CompilerParams(
            collective_id=1, has_side_effects=True, vmem_limit_bytes=48 * 1024 * 1024
        ),
    )(half, node, owner, drag)


def on_device(
    offsets,
    line,
    burgers_kind,
    seg_cell,
    end_node,
    end_owner,
    drag,
    applied,
    pair_list,
    ghost_x_list,
    ghost_y_list,
):
    nx = lax.axis_size("gx")
    ny = lax.axis_size("gy")
    pairs = pair_list[0, 0]
    ghosts, base = exchange_call(
        nx,
        ny,
        offsets[0, 0],
        line[0, 0],
        burgers_kind[0],
        seg_cell[0],
        applied,
        ghost_x_list[0, 0],
        ghost_y_list[0, 0],
    )
    half = near_call(pairs, ghosts.reshape(-1, SEG), base)
    velocity = nodal_call(nx, ny, half, end_node[0, 0], end_owner[0, 0], drag[0])
    return velocity.reshape(1, 1, 3, -1)


def solution(mesh):
    return jax.shard_map(
        on_device,
        mesh=mesh,
        in_specs=(
            P("gx", "gy", None, None),
            P("gx", "gy", None, None),
            P("gx", "gy", None),
            P("gx", "gy", None),
            P("gx", "gy", None, None),
            P("gx", "gy", None, None),
            P("gx", "gy", None),
            P(),
            P("gx", "gy", None, None),
            P("gx", "gy", None, None),
            P("gx", "gy", None, None),
        ),
        out_specs=P("gx", "gy", None, None),
        check_vma=False,
    )
```
